32 devices in a mesh: batch: 4 (over z), seq: 2 (over x), mp: 4 (over y, core).
Axes of the slice: x: 2, y: 2, z: 4, core: 2. Of those that a mesh axis runs over, the one named last changes fastest.
Arguments:
- text_rows: float32 [4, 2, 492, 768], P('batch', None, 'seq'), may hold values from -6 to 6
- memory_in: float32 [4, 10, 768], P('batch', 'seq'), may hold values from -6 to 6
- text_length: int32 [4], P('batch'), may hold values from 246 to 492, as said below
- mlm_mask: int32 [4, 2, 492], P('batch', None, 'seq'), may hold values 0 or 1
- out_grad: float32 [4, 2, 492, 768], P('batch', None, 'seq'), may hold values from -6 to 6
- attn_in: float32 [3, 768, 768], P(None, None, 'mp'), may hold values from -0.3125 to 0.3125
- attn_out: float32 [768, 768], P('mp'), may hold values from -0.875 to 0.875
- ffn_in: float32 [768, 3072], P(None, 'mp'), may hold values from -0.21875 to 0.21875
- ffn_out: float32 [3072, 768], P('mp'), may hold values from -0.109375 to 0.109375
- norm_gains: float32 [2, 768], replicated, may hold values from 0.5 to 1.5
- norm_biases: float32 [2, 768], replicated, may hold values from -3 to 3
Outputs:
- text_out: float32 [4, 2, 492, 768], P('batch', None, 'seq')
- memory_out: float32 [4, 10, 768], P('batch', 'seq')
- text_grad: float32 [4, 2, 492, 768], P('batch', None, 'seq')
- memory_grad: float32 [4, 10, 768], P('batch', 'seq')
- attn_in_grad: float32 [3, 768, 768], P(None, ('batch', 'seq'), 'mp')
- attn_out_grad: float32 [768, 768], P('mp', ('batch', 'seq'))
- ffn_in_grad: float32 [768, 3072], P(('batch', 'seq'), 'mp')
- ffn_out_grad: float32 [3072, 768], P('mp', ('batch', 'seq'))
- gains_grad: float32 [2, 768], P(None, ('batch', 'seq'))
- biases_grad: float32 [2, 768], P(None, ('batch', 'seq'))
The draws below stay inside these ranges and needn't reach their ends.
Inputs may be any that keep to these rules, and one draw needn't show every extreme that they name: `text_length`: in each aligned block of 4 items, one item's last segment holds all 492 text tokens.
All inputs are finite; a program needn't handle non-finite values. No bound on the sum of `mlm_mask` on one device may be relied on, other than what follows from the above.
Results may differ from the reference program's by a relative error of at most 0.0003.
Values sent between devices are 32-bit elements; how exact they have to be, the bound alone decides.
No kernel may reach another device: no remote copies, remote signals or barrier semaphores. Data moves between devices by JAX's collectives and lax.ppermute only.
A program may use at most 128 MiB of HBM per device.

```python
import math
import jax
import jax.numpy as jnp
from jax import lax

D = 768
H = 12
HD = 64
FF = 3072
MEM = 10
TEXT = 492
SEG = 2
ITEMS_ALL = 4


def draw_text_length(key, part):
    key = jax.random.fold_in(key, 11)
    first_key, second_key = jax.random.split(key)
    lengths = jax.random.randint(first_key, (ITEMS_ALL,), TEXT // 2, TEXT + 1)
    chosen = jax.random.randint(second_key, (ITEMS_ALL // 4,), 0, 4)
    place = jnp.arange(ITEMS_ALL) % 4
    full_item = place == jnp.repeat(chosen, 4)
    return jnp.where(full_item, TEXT, lengths).astype(jnp.int32)


def plant(values, key, smallest, largest):
    longest = values.shape.index(max(values.shape))
    spots = []
    for shift in (0, 1):
        where = [jax.random.randint(jax.random.fold_in(key, axis), (), 0, length) for axis, length in enumerate(values.shape)]
        where[longest] = (where[longest] + shift) % values.shape[longest]
        spots.append(tuple(where))
    return values.at[spots[0]].set(smallest).at[spots[1]].set(largest)


def with_spikes(entries, stream_key, source, target, parts, factor):
    def block_of(position):
        return (jnp.arange(entries.shape[position]) // (entries.shape[position] // parts)).reshape((-1,) + (1,) * (entries.ndim - 1 - position))

    first = jax.random.permutation(stream_key, parts)[block_of(target)]
    second = (block_of(target) + parts // 2) % parts
    return jnp.where((block_of(source) == first) | (block_of(source) == second), factor * entries, entries)


def block_scale(rng, shape, shards, low, largest):
    factor_of = 1.0
    for dim, blocks in shards:
        steps = jax.random.uniform(jax.random.fold_in(jax.random.fold_in(rng, 6), dim), (blocks,), jnp.float32, low / len(shards), largest / len(shards))
        factor_of = factor_of * jnp.repeat(jnp.exp(steps), shape[dim] // blocks).reshape((-1,) + (1,) * (len(shape) - 1 - dim))
    return factor_of


def scatter_about(rng, extent, spread, reach, cuts=(), held_as=jnp.bfloat16):
    array = jax.random.normal(rng, extent, jnp.float32) * spread
    if len(cuts) > 0:
        array = block_scale(rng, extent, cuts, -0.22, 0.18) * array
    return jnp.clip(array, min=-reach, max=reach).astype(held_as)


def heavy_noise(rng, dims, deviation, most, shards, heavy, kind=jnp.bfloat16):
    values = deviation * jax.random.normal(rng, dims, jnp.float32)
    if shards:
        values = values * block_scale(rng, dims, shards, -0.22, 0.18)
    return jnp.clip(with_spikes(values, jax.random.fold_in(rng, 3), *heavy), -most, most).astype(kind)


def setup_inputs(seed: int = 0) -> dict:
    arg_keys = jax.random.split(jax.random.key(seed), 12)
    text_rows = heavy_noise(arg_keys[0], (ITEMS_ALL, SEG, TEXT, D), 1.0, 6.0, ((0, 4), (2, 2)), (0, 3, 4, 2.0), jnp.float32)
    memory_in = scatter_about(arg_keys[1], (ITEMS_ALL, MEM, D), 1.0, 6.0, ((0, 4), (1, 2)), jnp.float32)
    text_length = draw_text_length(jax.random.fold_in(arg_keys[11], 71), 0)
    mlm_mask = plant((jax.random.randint(arg_keys[3], (ITEMS_ALL, SEG, TEXT), 0, 20) < 3).astype(jnp.int32), jax.random.fold_in(arg_keys[3], 1), 0, 1)
    out_grad = heavy_noise(arg_keys[4], (ITEMS_ALL, SEG, TEXT, D), 1.0, 6.0, ((0, 4), (2, 2)), (0, 3, 4, 2.0), jnp.float32)
    attn_in = scatter_about(arg_keys[5], (3, D, D), (D // 2) ** -0.5, 0.3125, ((2, 4),), jnp.float32)
    attn_out = scatter_about(arg_keys[6], (D, D), (D // 16) ** -0.5, 0.875, ((0, 4),), jnp.float32)
    ffn_in = scatter_about(arg_keys[7], (D, FF), D ** -0.5, 0.21875, ((1, 4),), jnp.float32)
    ffn_out = scatter_about(arg_keys[8], (FF, D), FF ** -0.5, 0.109375, ((0, 4),), jnp.float32)
    norm_gains = jnp.clip(1.0 + 0.1 * jax.random.normal(arg_keys[9], (2, D), jnp.float32), 0.5, 1.5)
    norm_biases = scatter_about(arg_keys[10], (2, D), 0.5, 3.0, (), jnp.float32)
    return dict(text_rows=text_rows, memory_in=memory_in, text_length=text_length, mlm_mask=mlm_mask, out_grad=out_grad, attn_in=attn_in, attn_out=attn_out, ffn_in=ffn_in, ffn_out=ffn_out, norm_gains=norm_gains, norm_biases=norm_biases)


EPS = 1e-12
NEG = -1e+30
HIGH = lax.Precision.HIGHEST

def layer_norm(inputs, gain_row, bias_row):
    centre = inputs - lax.optimization_barrier(jnp.mean(inputs, axis=-1, keepdims=True))
    return centre * lax.rsqrt(lax.optimization_barrier(jnp.mean(centre * centre, axis=-1, keepdims=True)) + EPS) * gain_row + bias_row

def layer_forward(rows_in, key_mask, attn_in, attn_out, ffn_in, ffn_out, norm_gains, norm_biases):
    row_count = rows_in.shape[0]
    project = jnp.einsum('sd,tde->tse', rows_in, attn_in, precision=HIGH)
    queries = project[0].reshape(row_count, H, HD)
    key_rows = project[1].reshape(row_count, H, HD)
    values = project[2].reshape(row_count, H, HD)
    scores = jnp.einsum('qhd,khd->hqk', queries, key_rows, precision=HIGH) * (1.0 / math.sqrt(HD))
    scores = jnp.where(key_mask[None, None, :], scores, NEG)
    probs = jax.nn.softmax(scores, axis=-1)
    context = jnp.einsum('hqk,khd->qhd', probs, values, precision=HIGH).reshape(row_count, D)
    hidden = layer_norm(rows_in + jnp.dot(context, attn_out, precision=HIGH), norm_gains[0], norm_biases[0])
    ffn_act = jax.nn.gelu(jnp.dot(hidden, ffn_in, precision=HIGH), approximate=False)
    return layer_norm(hidden + jnp.dot(ffn_act, ffn_out, precision=HIGH), norm_gains[1], norm_biases[1])

def item_forward(params, text_item, memory_item, length):
    memory_rows = memory_item
    outputs = []
    for segment in range(SEG):
        text_limit = length if segment == SEG - 1 else TEXT
        text_mask = jnp.arange(TEXT, dtype=jnp.int32) < text_limit
        key_mask = jnp.concatenate([jnp.ones((MEM,), jnp.bool_), text_mask, jnp.ones((MEM,), jnp.bool_)])
        rows_in = jnp.concatenate([memory_rows, text_item[segment], memory_rows], axis=0)
        result = layer_forward(rows_in, key_mask, *params)
        outputs.append(result[MEM:MEM + TEXT])
        memory_rows = result[MEM + TEXT:]
    return (jnp.stack(outputs), memory_rows)

def reference(text_rows, memory_in, text_length, mlm_mask, out_grad, attn_in, attn_out, ffn_in, ffn_out, norm_gains, norm_biases):

    def forward(text_all, memory_all, *params):

        def one_item(packed):
            return item_forward(params, packed[0], packed[1], packed[2])
        return lax.map(jax.checkpoint(one_item), (text_all, memory_all, text_length))
    primal, pullback = jax.vjp(forward, text_rows, memory_in, attn_in, attn_out, ffn_in, ffn_out, norm_gains, norm_biases)
    text_out, memory_out = primal
    limits = jnp.where(jnp.arange(SEG, dtype=jnp.int32)[None, :] == SEG - 1, text_length[:, None], TEXT)
    live_mask = (jnp.arange(TEXT, dtype=jnp.int32)[None, None, :] < limits[:, :, None]).astype(jnp.float32)
    grad_weight = mlm_mask.astype(jnp.float32) * live_mask
    gradients = pullback((out_grad * grad_weight[..., None], jnp.zeros_like(memory_out)))
    return (text_out, memory_out, gradients[0], gradients[1], gradients[2], gradients[3], gradients[4], gradients[5], gradients[6], gradients[7])
```

```python
import functools
import math

import jax
import jax.numpy as jnp
from jax import lax
from jax.experimental import pallas as pl
from jax.experimental.pallas import tpu as pltpu
from jax.sharding import PartitionSpec as P

HD = 64
EPS = 1e-12
NEG = -1e30
SMALL = 16
SCALE = 1.0 / math.sqrt(HD)
F32 = jnp.float32
BF16 = jnp.bfloat16
NN = ((1,), (0,))
NT = ((1,), (1,))
TN = ((0,), (0,))
CORE_SWAP = [(0, 1), (1, 0), (2, 3), (3, 2)]
CHIP_SWAP = [(0, 2), (2, 0), (1, 3), (3, 1)]
CROSS_SWAP = [(0, 3), (3, 0), (1, 2), (2, 1)]
SEQ_SWAP = [(0, 1), (1, 0)]
VMEM_SPEC = pl.BlockSpec(memory_space=pltpu.VMEM)
SMEM_SPEC = pl.BlockSpec(memory_space=pltpu.SMEM)
KERNEL_VMEM = 16 << 20


def pair(values):
    high = values.astype(BF16)
    return high, (values - high.astype(F32)).astype(BF16)


def dot(a, b, dims):
    return lax.dot_general(a, b, (dims, ((), ())), preferred_element_type=F32)


def mm3(a, b, dims=NN):
    return dot(a[0], b[0], dims) + (dot(a[0], b[1], dims) + dot(a[1], b[0], dims))


def read(refs):
    return refs[0][...], refs[1][...]


def mean_of(values):
    return jnp.sum(values, axis=-1, keepdims=True) * (1.0 / values.shape[-1])


def norm_forward(inputs, gain_row, bias_row):
    centre = inputs - mean_of(inputs)
    inverse = lax.rsqrt(mean_of(centre * centre) + EPS)
    normed = centre * inverse
    return normed * gain_row + bias_row, normed, inverse


def norm_backward(upstream, normed, inverse, gain_row):
    scaled = upstream * gain_row
    return inverse * (scaled - mean_of(scaled) - normed * mean_of(scaled * normed))


def gelu_both(inputs):
    cdf = 0.5 * (1.0 + lax.erf(inputs * (1.0 / math.sqrt(2.0))))
    density = jnp.exp(-0.5 * inputs * inputs) * (1.0 / math.sqrt(2.0 * math.pi))
    return inputs * cdf, cdf + inputs * density


def put_halves(core, values, keep, give):
    half = values.shape[0] // 2
    first, second = values[:half], values[half:]
    keep[...] = jnp.where(core == 0, first, second)
    give[...] = jnp.where(core == 0, second, first)


def whole_of(core, own, other):
    return jnp.concatenate(
        [jnp.where(core == 0, own, other), jnp.where(core == 0, other, own)], axis=0
    )


def sum_refs(refs):
    total = refs[0][...]
    for ref in refs[1:]:
        total = total + ref[...]
    return total


def head(values, index):
    return values[:, index * HD : (index + 1) * HD]


def split_kernel(*refs):
    count = len(refs) // 3
    for index in range(count):
        high, low = pair(refs[index][...])
        refs[count + 2 * index][...] = high
        refs[count + 2 * index + 1][...] = low


def start_kernel(scal, text, memory, attn_in, rows0, rows1, high, low, q0, q1, kv0, kv1):
    text_dev = text.shape[0]
    mem_dev = memory.shape[0]
    cols = attn_in.shape[1]
    rows0[0:text_dev] = text[:, 0, :]
    for index in range(2 * mem_dev):
        rows0[text_dev + index : text_dev + index + 1] = memory[index % mem_dev]
    rows1[-SMALL:] = jnp.zeros((SMALL, rows1.shape[1]), F32)
    rows1[0:text_dev] = text[:, 1, :]
    left = pair(jnp.concatenate([rows0[...], rows1[...]], axis=0))
    rows_dev = rows0.shape[0]
    for part in range(3):
        right = pair(attn_in[part])
        high[part], low[part] = right
        product = mm3(left, right, NT)
        if part == 0:
            q0[...] = product[:rows_dev]
            q1[...] = product[rows_dev:]
        else:
            place = slice((part - 1) * cols, part * cols)
            kv0[:, place] = product[:rows_dev]
            kv1[:, place] = product[rows_dev:]


def upstream_kernel(scal, out_grad, mlm, up0, up1):
    text_dev = out_grad.shape[0]
    row = lax.broadcasted_iota(jnp.int32, (text_dev, text_dev), 0)
    column = lax.broadcasted_iota(jnp.int32, (text_dev, text_dev), 1)
    position = lax.broadcasted_iota(jnp.int32, (text_dev, 1), 0)
    for segment, up in enumerate((up0, up1)):
        flags = mlm[segment : segment + 1].astype(F32)
        weight = jnp.sum(jnp.where(row == column, flags, 0.0), axis=1, keepdims=True)
        if segment == 1:
            weight = jnp.where(scal[1] * text_dev + position < scal[2], weight, 0.0)
        up[-SMALL:] = jnp.zeros((SMALL, up.shape[1]), F32)
        up[0:text_dev] = out_grad[:, segment, :] * weight


def attend_core(scal, query, kv_own, kv_oth, masked, text_dev, cols, probs, context):
    rows_dev = query.shape[0]
    keys = 2 * rows_dev
    if masked:
        place = lax.broadcasted_iota(jnp.int32, (1, keys), 1)
        shard = jnp.where(place < rows_dev, scal[1], 1 - scal[1])
        inside = jnp.where(place < rows_dev, place, place - rows_dev)
        valid = (inside >= text_dev) | (shard * text_dev + inside < scal[2])
    kv_all = jnp.concatenate([kv_own, kv_oth], axis=0)
    for index in range(cols // HD):
        key = pair(head(kv_all, index))
        value = pair(head(kv_all, cols // HD + index))
        scores = mm3(pair(head(query, index)), key, NT) * SCALE
        if masked:
            scores = jnp.where(valid, scores, NEG)
        expo = jnp.exp(scores - jnp.max(scores, axis=-1, keepdims=True))
        prob = expo * (1.0 / jnp.sum(expo, axis=-1, keepdims=True))
        probs[index] = prob
        context[:, index * HD : (index + 1) * HD] = mm3(pair(prob), value)


def attend_first_kernel(text_dev, scal, q, kv_own, kv_oth, wh, wl, context, probs, keep, give, tail):
    attend_core(scal, q[...], kv_own[...], kv_oth[...], False, text_dev, q.shape[1], probs, context)
    partial = mm3(pair(context[...]), (wh[...], wl[...]))
    put_halves(scal[0], partial, keep, give)
    tail[...] = partial[-SMALL:]


def attend_last_kernel(
    text_dev, scal, q, q_tail, kv_own, kv_oth, own_tail, oth_tail, wh, wl,
    context, probs, keep, give, q_full, own_full, oth_full,
):
    head_rows = q.shape[0] - SMALL
    for full, body, tail in (
        (q_full, q, q_tail),
        (own_full, kv_own, own_tail),
        (oth_full, kv_oth, oth_tail),
    ):
        full[0:head_rows] = body[0:head_rows]
        full[head_rows:] = tail[...]
    attend_core(
        scal, q_full[...], own_full[...], oth_full[...], True, text_dev, q.shape[1], probs, context
    )
    partial = mm3(pair(context[...]), (wh[...], wl[...]))
    put_halves(scal[0], partial, keep, give)


def feed_tail_kernel(rows, p0, p1, p2, p3, gains, biases, ih, il, oh, ol, hidden, partial):
    attended = sum_refs((p0, p1, p2, p3))
    value, _, _ = norm_forward(rows[-SMALL:] + attended, gains[0:1], biases[0:1])
    hidden[...] = value
    act, _ = gelu_both(mm3(pair(value), (ih[...], il[...])))
    partial[...] = mm3(pair(act), (oh[...], ol[...]))


def link_tail_kernel(
    text_dev, hidden, p0, p1, p2, p3, gains, biases, rows, high, low, rows_full, q_tail, kv_tail
):
    mixed = sum_refs((p0, p1, p2, p3))
    result, _, _ = norm_forward(hidden[...] + mixed, gains[1:2], biases[1:2])
    head_rows = rows.shape[0] - SMALL
    place = lax.broadcasted_iota(jnp.int32, (SMALL, 1), 0)
    tail = jnp.where(place < text_dev - head_rows, rows[-SMALL:], result)
    rows_full[0:head_rows] = rows[0:head_rows]
    rows_full[head_rows:] = tail
    left = pair(tail)
    cols = q_tail.shape[1]
    q_tail[...] = mm3(left, (high[0], low[0]), NT)
    kv_tail[:, 0:cols] = mm3(left, (high[1], low[1]), NT)
    kv_tail[:, cols:] = mm3(left, (high[2], low[2]), NT)


def feed_kernel(
    scal, rows, own, oth, gains, biases, ih, il, oh, ol,
    hidden, normed, inverse, act_high, act_low, slope, keep, give,
):
    attended = whole_of(scal[0], own[...], oth[...])
    value, unit, scale = norm_forward(rows[...] + attended, gains[0:1], biases[0:1])
    hidden[...] = value
    normed[...] = unit
    inverse[...] = scale
    act, grad = gelu_both(mm3(pair(value), (ih[...], il[...])))
    slope[...] = grad
    act = pair(act)
    act_high[...], act_low[...] = act
    put_halves(scal[0], mm3(act, (oh[...], ol[...])), keep, give)


def feed_back_kernel(
    scal, hidden, own, oth, gains, biases, upstream, slope, ih, il, oh, ol,
    outcome, normed_tail, inverse_tail, pre_two, pre_back, sums, keep, give,
):
    mixed = whole_of(scal[0], own[...], oth[...])
    result, unit, scale = norm_forward(hidden[...] + mixed, gains[1:2], biases[1:2])
    outcome[...] = result
    normed_tail[...] = unit[-SMALL:]
    inverse_tail[...] = scale[-SMALL:]
    back = upstream[...]
    sums[0:1] = jnp.sum(back * unit, axis=0, keepdims=True)
    sums[1:2] = jnp.sum(back, axis=0, keepdims=True)
    grad_two = norm_backward(back, unit, scale, gains[1:2])
    pre_two[...] = grad_two
    grad = mm3(pair(grad_two), (oh[...], ol[...]), NT) * slope[...]
    pre_back[...] = grad
    put_halves(scal[0], mm3(pair(grad), (ih[...], il[...]), NT), keep, give)


def heads_back(context_back, context, prob_of, query, kv_all, cols, query_back, kv_back):
    product = context_back * context
    count = cols // HD
    for index in range(count):
        key = pair(head(kv_all, index))
        value = pair(head(kv_all, count + index))
        back = pair(head(context_back, index))
        delta = jnp.sum(head(product, index), axis=-1, keepdims=True)
        prob = prob_of(index)
        score_back = prob * (mm3(back, value, NT) - delta) * SCALE
        score_back = pair(score_back)
        query_back[:, index * HD : (index + 1) * HD] = mm3(score_back, key)
        kv_back[index * HD : (index + 1) * HD] = mm3(pair(head(query, index)), score_back, TN)
        kv_back[cols + index * HD : cols + (index + 1) * HD] = mm3(back, pair(prob), TN)


def attend_back_kernel(
    scal, pre_two, own, oth, normed, inverse, gains, context, probs, q, kv_own, kv_oth, wh, wl,
    pre_one, sums, q_back, own_back, give_back, own_tail, give_tail, kv_back,
):
    hidden_back = pre_two[...] + whole_of(scal[0], own[...], oth[...])
    unit = normed[...]
    sums[0:1] = jnp.sum(hidden_back * unit, axis=0, keepdims=True)
    sums[1:2] = jnp.sum(hidden_back, axis=0, keepdims=True)
    grad_one = norm_backward(hidden_back, unit, inverse[...], gains[0:1])
    pre_one[...] = grad_one
    context_back = mm3(pair(grad_one), (wh[...], wl[...]), NT)
    kv_all = jnp.concatenate([kv_own[...], kv_oth[...]], axis=0)
    cols = q.shape[1]
    heads_back(
        context_back, context[...], lambda index: probs[index], q[...], kv_all, cols, q_back, kv_back
    )
    rows_dev = q.shape[0]
    own_back[...] = kv_back[:, 0:rows_dev]
    give_back[...] = kv_back[:, rows_dev:]
    own_tail[...] = kv_back[:, rows_dev - 128 : rows_dev].T[-SMALL:]
    give_tail[...] = kv_back[:, 2 * rows_dev - 128 : 2 * rows_dev].T[-SMALL:]


def project_back(query_back, kv_back, high, low):
    cols = query_back.shape[1]
    total = mm3(pair(query_back), (high[0], low[0]))
    total = total + mm3(pair(kv_back[:, 0:cols]), (high[1], low[1]))
    return total + mm3(pair(kv_back[:, cols:]), (high[2], low[2]))


def rows_tail_kernel(q_back, own_tail, got_tail, high, low, give_back, partial, give_next):
    partial[...] = project_back(q_back[-SMALL:], own_tail[...] + got_tail[...], high, low)
    give_next[...] = give_back[...]


def rows_kernel(scal, q_back, own_back, got_back, high, low, kv_back, keep, give):
    total = (own_back[...] + got_back[...]).T
    kv_back[...] = total
    put_halves(scal[0], project_back(q_back[...], total, high, low), keep, give)


def rows_norms_kernel(
    scal, q_back, own_back, got_back, high, low, own_sums, kv_back, keep, give, sums
):
    rows, width = own_back.shape
    rows_kernel(scal, q_back, own_back, got_back.at[0:rows], high, low, kv_back, keep, give)
    count = sums.shape[1] // width
    for part in range(count):
        place = slice(part * width, (part + 1) * width)
        sums[:, place] = own_sums[:, place] + got_back[rows + 8 * part : rows + 8 * part + 8]


def feed_back_tail_kernel(
    mem_dev, pre_one, p0, p1, p2, p3, normed, inverse, gains, slope, ih, il, oh, ol,
    pre_two, pre_back, partial, sums, back,
):
    rows_back = pre_one[-SMALL:] + sum_refs((p0, p1, p2, p3))
    first = SMALL - mem_dev
    back[0:first] = jnp.zeros((first, back.shape[1]), F32)
    back[first:] = rows_back[first - mem_dev : first] + rows_back[first:]
    upstream = back[...]
    unit = normed[...]
    sums[0:1] = jnp.sum(upstream * unit, axis=0, keepdims=True)
    sums[1:2] = jnp.sum(upstream, axis=0, keepdims=True)
    grad_two = norm_backward(upstream, unit, inverse[...], gains[1:2])
    pre_two[...] = grad_two
    grad = mm3(pair(grad_two), (oh[...], ol[...]), NT) * slope[-SMALL:]
    pre_back[...] = grad
    partial[...] = mm3(pair(grad), (ih[...], il[...]), NT)


def attend_back_tail_kernel(
    pre_two, p0, p1, p2, p3, normed, inverse, gains, context, probs, q, kv_own, kv_oth, wh, wl,
    pre_one, q_back, own_back, give_back, sums_one0, sums_one1, sums_two0, sums_two1, sums_two_tail,
    pre_one_all, sums, q_back_all, own_back_all, give_back_all, q_tail, kv_back,
):
    hidden_back = pre_two[...] + sum_refs((p0, p1, p2, p3))
    unit = normed[-SMALL:]
    one = sums_one0[...] + sums_one1[...]
    two = sums_two0[...] + sums_two1[...] + sums_two_tail[...]
    sums[0:1] = one[0:1] + jnp.sum(hidden_back * unit, axis=0, keepdims=True)
    sums[1:2] = two[0:1]
    sums[2:3] = one[1:2] + jnp.sum(hidden_back, axis=0, keepdims=True)
    sums[3:4] = two[1:2]
    sums[4:] = jnp.zeros((4, sums.shape[1]), F32)
    grad_one = norm_backward(hidden_back, unit, inverse[-SMALL:], gains[0:1])
    head_rows = pre_one.shape[0] - SMALL
    pre_one_all[0:head_rows] = pre_one[0:head_rows]
    pre_one_all[head_rows:] = pre_one[head_rows:] + grad_one
    context_back = mm3(pair(grad_one), (wh[...], wl[...]), NT)
    kv_all = jnp.concatenate([kv_own[...], kv_oth[...]], axis=0)
    heads_back(
        context_back, context[-SMALL:], lambda index: probs[index, -SMALL:], q[-SMALL:], kv_all,
        q.shape[1], q_tail, kv_back,
    )
    q_back_all[0:head_rows] = q_back[0:head_rows]
    q_back_all[head_rows:] = q_back[head_rows:] + q_tail[...]
    rows_dev = q.shape[0]
    own_back_all[...] = own_back[...] + kv_back[:, 0:rows_dev]
    keys = kv_back.shape[0]
    give_back_all[0:keys] = give_back[...] + kv_back[:, rows_dev:]
    for part in range(sums.shape[1] // rows_dev):
        place = slice(part * rows_dev, (part + 1) * rows_dev)
        give_back_all[keys + 8 * part : keys + 8 * part + 8] = sums[:, place]


def put_parts(seq, values, keeps, gives):
    batch_count, chunk, width = keeps[0].shape
    for part, (keep, give) in enumerate(zip(keeps, gives)):
        place = slice(part * width, (part + 1) * width)
        for block in range(batch_count):
            even = values[2 * block * chunk : (2 * block + 1) * chunk, place]
            odd = values[(2 * block + 1) * chunk : (2 * block + 2) * chunk, place]
            keep[block] = jnp.where(seq == 0, even, odd)
            give[block] = jnp.where(seq == 0, odd, even)


def feed_in_kernel(scal, hidden0, hidden1, back0, back1, back_tail, *outs):
    head_rows = hidden0.shape[0] - SMALL
    hidden = pair(jnp.concatenate([hidden0[...], hidden1[...]], axis=0))
    back = pair(
        jnp.concatenate(
            [back0[0:head_rows], back0[head_rows:] + back_tail[...], back1[...]], axis=0
        )
    )
    count = len(outs) // 2
    put_parts(scal[1], mm3(hidden, back, TN), outs[:count], outs[count:])


def feed_out_kernel(scal, ah0, al0, ah1, al1, two0, two1, two_tail, *outs):
    head_rows = two0.shape[0] - SMALL
    two = pair(
        jnp.concatenate([two0[0:head_rows], two0[head_rows:] + two_tail[...], two1[...]], axis=0)
    )
    act = (
        jnp.concatenate([ah0[...], ah1[...]], axis=0),
        jnp.concatenate([al0[...], al1[...]], axis=0),
    )
    count = len(outs) // 2
    put_parts(scal[1], mm3(two, act, TN), outs[:count], outs[count:])


def attend_weights_kernel(
    scal, rows0, rows1, q0, q1, kv0, kv1, one0, one1, c0, c1, keep0, keep1, give0, give1
):
    def stacked(first, second):
        return pair(jnp.concatenate([first[...], second[...]], axis=0))

    rows = stacked(rows0, rows1)
    cols = q0.shape[1]
    kv = stacked(kv0, kv1)
    seq = scal[1]
    by_query = mm3(rows, stacked(q0, q1), TN)
    by_key = mm3(rows, (kv[0][:, :cols], kv[1][:, :cols]), TN)
    put_parts(seq, jnp.concatenate([by_query, by_key], axis=1), [keep0], [give0])
    by_value = mm3(rows, (kv[0][:, cols:], kv[1][:, cols:]), TN)
    by_out = mm3(stacked(one0, one1), stacked(c0, c1), TN)
    put_parts(seq, jnp.concatenate([by_value, by_out], axis=1), [keep1], [give1])


def join_kernel(first, second, out):
    out[...] = first[...] + second[...]


def join_both_kernel(first, second, third, fourth, out, other):
    out[...] = first[...] + second[...]
    other[...] = third[...] + fourth[...]


def turn_kernel(batch_count, scal, keep, got, *pieces):
    for shift in range(batch_count):
        block = lax.rem(scal[3] + shift, batch_count)
        pieces[shift][...] = keep[block] + got[block]


def turn_norms_kernel(batch_count, scal, keep, got, sums, *pieces):
    chunk, width = keep.shape[1:]
    for shift in range(batch_count):
        block = lax.rem(scal[3] + shift, batch_count)
        pieces[shift][0:chunk] = keep[block] + got[block]
        pieces[shift][chunk : chunk + 8] = sums[:, 0:width]
        pieces[shift][chunk + 8 :] = sums[:, width:]


def end_parts_kernel(*refs):
    *pieces, out = refs
    chunk = out.shape[0]
    width = pieces[0].shape[1]
    for part in range(len(pieces) // 4):
        some = [ref.at[0:chunk] for ref in pieces[4 * part : 4 * part + 4]]
        out[:, part * width : (part + 1) * width] = sum_refs(some)


def end_attend_kernel(p0, p1, p2, p3, p4, p5, p6, p7, grad_in, grad_out):
    first, second = sum_refs((p0, p1, p2, p3)), sum_refs((p4, p5, p6, p7))
    cols = grad_in.shape[2]
    grad_in[0] = first[:, 0:cols]
    grad_in[1] = first[:, cols:]
    grad_in[2] = second[:, 0:cols]
    grad_out[...] = second[:, cols:].T


def end_norms_kernel(blocks, scal, p0, p1, p2, p3, gains, biases):
    chunk = gains.shape[1]
    total = sum_refs([ref.at[chunk:] for ref in (p0, p1, p2, p3)])
    total = jnp.concatenate([total[0:8], total[8:16]], axis=1)
    mine = scal[3] * 2 + scal[1]
    picked = jnp.zeros((total.shape[0], chunk), F32)
    for block in range(blocks):
        picked = jnp.where(mine == block, total[:, block * chunk : (block + 1) * chunk], picked)
    gains[...] = picked[0:2]
    biases[...] = picked[2:4]


def end_text_kernel(first_row, first, second, memory, text, last):
    text_dev = text.shape[0]
    text[:, 0, :] = first[0:text_dev]
    text[:, 1, :] = second[0:text_dev]
    mem_dev = last.shape[0]
    for index in range(mem_dev):
        last[index] = memory[first_row + index : first_row + index + 1]


def end_rows_kernel(mem_dev, scal, pre_one, own, oth, rows_back, memory_grad):
    total = pre_one[...] + whole_of(scal[0], own[...], oth[...])
    rows_back[...] = total
    text_dev = total.shape[0] - 2 * mem_dev
    memory_grad[0:mem_dev] = total[text_dev : text_dev + mem_dev] + total[text_dev + mem_dev :]
    memory_grad[mem_dev:] = jnp.zeros((SMALL - mem_dev, total.shape[1]), F32)


def shape(*dims, dtype=F32):
    return jax.ShapeDtypeStruct(dims, dtype)


class Order:
    def __init__(self):
        self.last = None
        self.extra = []

    def wait(self, *values):
        self.extra += values

    def call(self, kernel, outs, *args, scal=None, scratch=(), name=None):
        after = [] if self.last is None else [self.last]
        after += self.extra
        self.extra = []
        count = len(args) + (scal is not None)
        skip = len(after)

        def body(*refs):
            kernel(*refs[:count], *refs[count + skip :])

        ins = [SMEM_SPEC] * (scal is not None) + [VMEM_SPEC] * len(args)
        ins += [pl.BlockSpec(memory_space=pl.ANY)] * skip
        operands = ([scal] if scal is not None else []) + list(args) + after
        result = pl.pallas_call(
            body,
            out_shape=outs,
            in_specs=ins,
            out_specs=jax.tree.map(lambda _: VMEM_SPEC, outs),
            scratch_shapes=list(scratch),
            compiler_params=pltpu.CompilerParams(vmem_limit_bytes=KERNEL_VMEM),
            cost_estimate=pl.CostEstimate(flops=0, bytes_accessed=0, transcendentals=0),
            name=name,
        )(*operands)
        self.last = min(jax.tree.leaves(result), key=lambda value: value.size)
        return result


def swap_seq(values):
    return lax.ppermute(values, "seq", SEQ_SWAP)


def spread_mp(values):
    return (values,) + tuple(
        lax.ppermute(values, "mp", way) for way in (CORE_SWAP, CHIP_SWAP, CROSS_SWAP)
    )


def turn(call, scal, keep, got, name, sums=None):
    batch_count, chunk, width = keep.shape
    rows = chunk if sums is None else chunk + 16
    if batch_count != 4:
        total = lax.psum_scatter(keep + got, "batch", scatter_dimension=0, tiled=True)[0]
        if sums is not None:
            sums = lax.psum(sums, "batch")
            total = jnp.concatenate([total, sums[:, 0:width], sums[:, width:]], axis=0)
        return (total,) + (jnp.zeros_like(total),) * 3
    pieces = call(
        functools.partial(turn_kernel if sums is None else turn_norms_kernel, batch_count),
        [shape(rows, width)] * batch_count,
        keep,
        got,
        *([] if sums is None else [sums]),
        scal=scal,
        name=name,
    )
    return (pieces[0],) + tuple(
        lax.ppermute(
            pieces[shift], "batch", [(i, (i + shift) % batch_count) for i in range(batch_count)]
        )
        for shift in range(1, batch_count)
    )


def local(
    text_rows,
    memory_in,
    text_length,
    mlm_mask,
    out_grad,
    attn_in,
    attn_out,
    ffn_in,
    ffn_out,
    norm_gains,
    norm_biases,
):
    seg_count, text_dev, width = text_rows.shape[1:]
    mem_dev = memory_in.shape[1]
    cols = attn_in.shape[2]
    units = ffn_in.shape[1]
    heads = cols // HD
    batch_count = lax.axis_size("batch")
    seq_count = lax.axis_size("seq")
    rows_dev = text_dev + 2 * mem_dev
    half = rows_dev // 2
    chunk = width // (batch_count * seq_count)
    text_rows = text_rows.reshape(seg_count, text_dev, width).transpose(1, 0, 2)
    out_grad = out_grad.reshape(seg_count, text_dev, width).transpose(1, 0, 2)
    memory_in = memory_in.transpose(1, 0, 2)
    mlm_mask = mlm_mask.reshape(seg_count, text_dev)
    attn_in = attn_in.transpose(0, 2, 1)
    scal = jnp.stack(
        [lax.axis_index("mp") % 2, lax.axis_index("seq"), text_length[0], lax.axis_index("batch")]
    ).astype(jnp.int32)

    whole = shape(rows_dev, width)
    halves = [shape(half, width)] * 2
    tail_shape = shape(SMALL, width)
    column = shape(rows_dev, 1)

    order = Order()
    call = order.call

    def join(keep, got, name):
        return call(join_kernel, shape(*keep.shape), keep, got, name=name)

    def join_both(first, second, third, fourth, name):
        return call(
            join_both_kernel,
            [shape(*first.shape), shape(*third.shape)],
            first,
            second,
            third,
            fourth,
            name=name,
        )

    def to_core(values):
        return lax.ppermute(values, "mp", CORE_SWAP)

    def to_chip(values):
        return lax.ppermute(values, "mp", CHIP_SWAP)

    def feed(segment, rows, total):
        return call(
            feed_kernel,
            [whole, whole, column]
            + [shape(rows_dev, units, dtype=BF16)] * 2
            + [shape(rows_dev, units)]
            + halves,
            rows,
            *total,
            norm_gains,
            norm_biases,
            *feed_w,
            scal=scal,
            name="feed%d" % segment,
        )

    def feed_back(segment, hidden, total, slope):
        return call(
            feed_back_kernel,
            [whole, tail_shape, shape(SMALL, 1), whole]
            + [shape(rows_dev, units), shape(2, width)]
            + halves,
            hidden,
            *total,
            norm_gains,
            norm_biases,
            upstream[segment],
            slope,
            *feed_w,
            scal=scal,
            name="feed_back%d" % segment,
        )

    def attend_back(segment, pre_two, total, normed, inverse, context, probs, query, kv):
        return call(
            attend_back_kernel,
            [whole, shape(2, width), shape(rows_dev, cols)]
            + [shape(2 * cols, rows_dev)] * 2
            + [shape(SMALL, 2 * cols)] * 2,
            pre_two,
            *total,
            normed,
            inverse,
            norm_gains,
            context,
            probs,
            query,
            *kv,
            *out_w,
            scal=scal,
            scratch=[pltpu.VMEM((2 * cols, seq_count * rows_dev), F32)],
            name="attend_back%d" % segment,
        )

    def rows(segment, qb, own, got):
        return call(
            rows_kernel,
            [shape(rows_dev, 2 * cols)] + halves,
            qb,
            own,
            got,
            *in_w,
            scal=scal,
            name="rows%d" % segment,
        )

    def end_rows(segment, one, total):
        return call(
            functools.partial(end_rows_kernel, mem_dev),
            [whole, tail_shape],
            one,
            *total,
            scal=scal,
            name="end_rows%d" % segment,
        )

    rows0, rows1, in_h, in_l, q0, q1, kv0, kv1 = call(
        start_kernel,
        [whole, whole, shape(3, cols, width, dtype=BF16), shape(3, cols, width, dtype=BF16)]
        + [shape(rows_dev, cols)] * 2
        + [shape(rows_dev, 2 * cols)] * 2,
        text_rows,
        memory_in,
        attn_in,
        scal=scal,
        name="start",
    )
    kv0_oth = swap_seq(kv0)
    kv1_oth = swap_seq(kv1)
    out_w = call(split_kernel, [shape(cols, width, dtype=BF16)] * 2, attn_out, name="split_attn")
    upstream = call(upstream_kernel, [whole] * 2, out_grad, mlm_mask, scal=scal, name="upstream")
    feed_w = call(
        split_kernel,
        [shape(width, units, dtype=BF16)] * 2 + [shape(units, width, dtype=BF16)] * 2,
        ffn_in,
        ffn_out,
        name="split_ffn",
    )
    in_w = (in_h, in_l)

    attended = [shape(rows_dev, cols), shape(heads, rows_dev, seq_count * rows_dev)] + halves
    c0, probs0, keep, give, tail = call(
        functools.partial(attend_first_kernel, text_dev),
        attended + [tail_shape],
        q0,
        kv0,
        kv0_oth,
        *out_w,
        scal=scal,
        name="attend0",
    )
    tails = spread_mp(tail)
    got = to_core(give)
    hidden_tail, tail = call(
        feed_tail_kernel,
        [tail_shape, tail_shape],
        rows0,
        *tails,
        norm_gains,
        norm_biases,
        *feed_w,
        name="feed_tail",
    )
    tails = spread_mp(tail)
    order.wait(*tails[1:])
    chip0 = join(keep, got, "chip_one0")
    y0 = to_chip(chip0)
    rows1, q_tail, kv_tail = call(
        functools.partial(link_tail_kernel, text_dev),
        [whole, shape(SMALL, cols), shape(SMALL, 2 * cols)],
        hidden_tail,
        *tails,
        norm_gains,
        norm_biases,
        rows1,
        *in_w,
        name="link_tail",
    )
    kv_tail_oth = swap_seq(kv_tail)
    c1, probs1, keep, give, q1, kv1, kv1_oth = call(
        functools.partial(attend_last_kernel, text_dev),
        attended + [shape(rows_dev, cols)] + [shape(rows_dev, 2 * cols)] * 2,
        q1,
        q_tail,
        kv1,
        kv1_oth,
        kv_tail,
        kv_tail_oth,
        *out_w,
        scal=scal,
        name="attend1",
    )
    both0, chip1 = join_both(chip0, y0, keep, to_core(give), "both_one0")
    y1 = to_chip(chip1)
    hidden0, normed0, inverse0, ah0, al0, slope0, keep, give = feed(
        0, rows0, (both0, to_core(both0))
    )
    both1, chip0 = join_both(chip1, y1, keep, to_core(give), "both_one1")
    y0 = to_chip(chip0)
    hidden1, normed1, inverse1, ah1, al1, slope1, keep, give = feed(
        1, rows1, (both1, to_core(both1))
    )
    both0, chip1 = join_both(chip0, y0, keep, to_core(give), "both_two0")
    y1 = to_chip(chip1)
    text0, unit_tail, scale_tail, two0, back0, sums_two0, keep, give = feed_back(
        0, hidden0, (both0, to_core(both0)), slope0
    )
    both1, chip0 = join_both(chip1, y1, keep, to_core(give), "both_two1")
    y0 = to_chip(chip0)
    text1, _, _, two1, back1, sums_two1, keep, give = feed_back(
        1, hidden1, (both1, to_core(both1)), slope1
    )
    both0, chip1 = join_both(chip0, y0, keep, to_core(give), "both_three0")
    y1 = to_chip(chip1)
    pre_one0, sums_one0, qb0, own0, give0, _, _ = attend_back(
        0, two0, (both0, to_core(both0)), normed0, inverse0, c0, probs0, q0, (kv0, kv0_oth)
    )
    both1 = join(chip1, y1, "both_three1")
    pre_one1, sums_one1, qb1, own1, give1, own_tail, give_tail = attend_back(
        1, two1, (both1, to_core(both1)), normed1, inverse1, c1, probs1, q1, (kv1, kv1_oth)
    )
    tail, give1 = call(
        rows_tail_kernel,
        [tail_shape, shape(2 * cols, rows_dev)],
        qb1,
        own_tail,
        swap_seq(give_tail),
        *in_w,
        give1,
        name="rows_tail",
    )
    got1 = swap_seq(give1)
    two_tail, back_tail, tail, sums_two_tail = call(
        functools.partial(feed_back_tail_kernel, mem_dev),
        [tail_shape, shape(SMALL, units), tail_shape, shape(2, width)],
        pre_one1,
        *spread_mp(tail),
        unit_tail,
        scale_tail,
        norm_gains,
        slope0,
        *feed_w,
        scratch=[pltpu.VMEM((SMALL, width), F32)],
        name="feed_back_tail",
    )
    tails = spread_mp(tail)
    pre_one0, sums, qb0, own0, give0 = call(
        attend_back_tail_kernel,
        [whole, shape(8, width), shape(rows_dev, cols), shape(2 * cols, rows_dev)]
        + [shape(2 * cols + 8 * (width // rows_dev), rows_dev)],
        two_tail,
        *tails,
        normed0,
        inverse0,
        norm_gains,
        c0,
        probs0,
        q0,
        kv0,
        kv0_oth,
        *out_w,
        pre_one0,
        qb0,
        own0,
        give0,
        sums_one0,
        sums_one1,
        sums_two0,
        sums_two1,
        sums_two_tail,
        scratch=[
            pltpu.VMEM((SMALL, cols), F32),
            pltpu.VMEM((2 * cols, seq_count * rows_dev), F32),
        ],
        name="attend_back_tail",
    )
    got0 = swap_seq(give0)
    kv_back1, keep, give = rows(1, qb1, own1, got1)
    chip1 = join(keep, to_core(give), "chip_four1")
    y1 = to_chip(chip1)
    fo_keep0, fo_keep1, fo_give0, fo_give1 = call(
        feed_out_kernel,
        [shape(batch_count, chunk, units // 2)] * 4,
        ah0,
        al0,
        ah1,
        al1,
        two0,
        two1,
        two_tail,
        scal=scal,
        name="feed_out",
    )
    kv_back0, keep, give, sums = call(
        rows_norms_kernel,
        [shape(rows_dev, 2 * cols)] + halves + [shape(8, width)],
        qb0,
        own0,
        got0,
        *in_w,
        sums,
        scal=scal,
        name="rows0",
    )
    got_fo = swap_seq(fo_give0), swap_seq(fo_give1)
    both1, chip0 = join_both(chip1, y1, keep, to_core(give), "both_four1")
    y0 = to_chip(chip0)
    in_keep0, in_keep1, in_give0, in_give1 = call(
        feed_in_kernel,
        [shape(batch_count, chunk, units // 2)] * 4,
        hidden0,
        hidden1,
        back0,
        back1,
        back_tail,
        scal=scal,
        name="feed_in",
    )
    got_in = swap_seq(in_give0), swap_seq(in_give1)
    at_keep0, at_keep1, at_give0, at_give1 = call(
        attend_weights_kernel,
        [shape(batch_count, chunk, 2 * cols)] * 4,
        rows0,
        rows1,
        qb0,
        qb1,
        kv_back0,
        kv_back1,
        pre_one0,
        pre_one1,
        c0,
        c1,
        scal=scal,
        name="attend_weights",
    )
    got_at = swap_seq(at_give0), swap_seq(at_give1)
    parts = [turn(call, scal, fo_keep0, got_fo[0], "turn_out0", sums)]
    rows_back1, _ = end_rows(1, pre_one1, (both1, to_core(both1)))
    both0 = join(chip0, y0, "both_four0")
    text_shape = [shape(text_dev, seg_count, width), shape(mem_dev, 1, width)]
    text_out, memory_out = call(
        functools.partial(end_text_kernel, rows_dev - mem_dev),
        text_shape,
        text0,
        text1,
        text1,
        name="end_out",
    )
    parts.append(turn(call, scal, fo_keep1, got_fo[1], "turn_out1"))
    rows_back0, memory_grad = end_rows(0, pre_one0, (both0, to_core(both0)))
    text_grad, memory_grad = call(
        functools.partial(end_text_kernel, 0),
        text_shape,
        rows_back0,
        rows_back1,
        memory_grad,
        name="end_grad",
    )
    parts.append(turn(call, scal, in_keep0, got_in[0], "turn_in0"))
    gains_grad, biases_grad = call(
        functools.partial(end_norms_kernel, batch_count * seq_count),
        [shape(2, chunk)] * 2,
        *parts[0],
        scal=scal,
        name="end_norms",
    )
    parts.append(turn(call, scal, in_keep1, got_in[1], "turn_in1"))
    ffn_out_grad = call(
        end_parts_kernel, shape(chunk, units), *parts[0], *parts[1], name="end_feed_out"
    ).T
    parts.append(turn(call, scal, at_keep0, got_at[0], "turn_attend0"))
    ffn_in_grad = call(
        end_parts_kernel, shape(chunk, units), *parts[2], *parts[3], name="end_feed_in"
    )
    parts.append(turn(call, scal, at_keep1, got_at[1], "turn_attend1"))
    attn_in_grad, attn_out_grad = call(
        end_attend_kernel,
        [shape(3, chunk, cols), shape(cols, chunk)],
        *parts[4],
        *parts[5],
        name="end_attend",
    )
    return (
        text_out.transpose(1, 0, 2)[None],
        memory_out.transpose(1, 0, 2),
        text_grad.transpose(1, 0, 2)[None],
        memory_grad.transpose(1, 0, 2),
        attn_in_grad,
        attn_out_grad,
        ffn_in_grad,
        ffn_out_grad,
        gains_grad,
        biases_grad,
    )


def solution(mesh):
    placed = (
        P("batch", None, "seq", None),
        P("batch", "seq", None),
        P("batch"),
        P("batch", None, "seq"),
        P("batch", None, "seq", None),
        P(None, None, "mp"),
        P("mp", None),
        P(None, "mp"),
        P("mp", None),
        P(),
        P(),
    )
    return jax.shard_map(
        local,
        mesh=mesh,
        in_specs=placed,
        out_specs=(
            P("batch", None, "seq", None),
            P("batch", "seq", None),
            P("batch", None, "seq", None),
            P("batch", "seq", None),
            P(None, ("batch", "seq"), "mp"),
            P("mp", ("batch", "seq")),
            P(("batch", "seq"), "mp"),
            P("mp", ("batch", "seq")),
            P(None, ("batch", "seq")),
            P(None, ("batch", "seq")),
        ),
        check_vma=False,
    )
```

```python
import functools
import math

import jax
import jax.numpy as jnp
from jax import lax
from jax.experimental import pallas as pl
from jax.experimental.pallas import tpu as pltpu
from jax.sharding import PartitionSpec as P

HD = 64
EPS = 1e-12
NEG = -1e30
SMALL = 16
SCALE = 1.0 / math.sqrt(HD)
F32 = jnp.float32
BF16 = jnp.bfloat16
NN = ((1,), (0,))
NT = ((1,), (1,))
TN = ((0,), (0,))
CORE_SWAP = [(0, 1), (1, 0), (2, 3), (3, 2)]
CHIP_SWAP = [(0, 2), (2, 0), (1, 3), (3, 1)]
CROSS_SWAP = [(0, 3), (3, 0), (1, 2), (2, 1)]
SEQ_SWAP = [(0, 1), (1, 0)]
VMEM_SPEC = pl.BlockSpec(memory_space=pltpu.VMEM)
SMEM_SPEC = pl.BlockSpec(memory_space=pltpu.SMEM)
KERNEL_VMEM = 16 << 20
CORE, SEQ, LENGTH, BATCH, MP = range(5)


def pair(values):
    high = values.astype(BF16)
    return high, (values - high.astype(F32)).astype(BF16)


def dot(a, b, dims):
    return lax.dot_general(a, b, (dims, ((), ())), preferred_element_type=F32)


def mm3(a, b, dims=NN):
    rows = a[0].shape[0]
    if dims != TN and rows <= 128:
        both = dot(jnp.concatenate(a, axis=0), b[0], dims)
        return both[:rows] + (both[rows:] + dot(a[0], b[1], dims))
    return dot(a[0], b[0], dims) + (dot(a[0], b[1], dims) + dot(a[1], b[0], dims))


def load(refs):
    return refs[0][...], refs[1][...]


def mean_of(values):
    return jnp.sum(values, axis=-1, keepdims=True) * (1.0 / values.shape[-1])


def sum_rows(values):
    return jnp.sum(values, axis=0, keepdims=True)


def norm_forward(inputs, gain_row, bias_row):
    centre = inputs - mean_of(inputs)
    inverse = lax.rsqrt(mean_of(centre * centre) + EPS)
    normed = centre * inverse
    return normed * gain_row + bias_row, normed, inverse


def norm_backward(upstream, normed, inverse, gain_row):
    scaled = upstream * gain_row
    return inverse * (scaled - mean_of(scaled) - normed * mean_of(scaled * normed))


def gelu_both(inputs):
    cdf = 0.5 * (1.0 + lax.erf(inputs * (1.0 / math.sqrt(2.0))))
    density = jnp.exp(-0.5 * inputs * inputs) * (1.0 / math.sqrt(2.0 * math.pi))
    return inputs * cdf, cdf + inputs * density


def in_order(core, own, other):
    return jnp.concatenate(
        [jnp.where(core == 0, own, other), jnp.where(core == 0, other, own)], axis=0
    )


def sum_refs(refs):
    total = refs[0][...]
    for ref in refs[1:]:
        total = total + ref[...]
    return total


def head(values, index):
    return values[:, index * HD : (index + 1) * HD]


def half_of(ref, core):
    half = ref.shape[0] // 2
    return ref[pl.ds(pl.multiple_of(core * half, half), half), :]


def split_kernel(*refs):
    count = len(refs) // 3
    for index in range(count):
        high, low = pair(refs[index][...])
        refs[count + 2 * index][...] = high
        refs[count + 2 * index + 1][...] = low


def turn_weights_kernel(*refs):
    count = len(refs) // 2
    for source, target in zip(refs[:count], refs[count:]):
        target[...] = source[...].T


def start_kernel(scal, text, memory, attn_in, rows0, rows1, high, low, kv0):
    text_dev = text.shape[0]
    mem_dev = memory.shape[0]
    cols = attn_in.shape[1]
    rows0[0:text_dev] = text[:, 0, :]
    for index in range(2 * mem_dev):
        rows0[text_dev + index : text_dev + index + 1] = memory[index % mem_dev]
    rows1[-SMALL:] = jnp.zeros((SMALL, rows1.shape[1]), F32)
    rows1[0:text_dev] = text[:, 1, :]
    left = pair(rows0[...])
    for part in range(3):
        right = pair(attn_in[part])
        high[part], low[part] = right
        if part > 0:
            kv0[:, (part - 1) * cols : part * cols] = mm3(left, right, NT)


def project_kernel(rows0, rows1, high, low, q0, q1, kv1):
    cols = q0.shape[1]
    left = pair(rows1[...])
    for part in range(3):
        right = (high[part], low[part])
        if part == 0:
            q0[...] = mm3(pair(rows0[...]), right, NT)
            q1[...] = mm3(left, right, NT)
        else:
            kv1[:, (part - 1) * cols : part * cols] = mm3(left, right, NT)


def upstream_kernel(scal, out_grad, mlm, up0, up1):
    text_dev = out_grad.shape[0]
    row = lax.broadcasted_iota(jnp.int32, (text_dev, text_dev), 0)
    column = lax.broadcasted_iota(jnp.int32, (text_dev, text_dev), 1)
    position = lax.broadcasted_iota(jnp.int32, (text_dev, 1), 0)
    for segment, up in enumerate((up0, up1)):
        flags = mlm[segment : segment + 1].astype(F32)
        weight = jnp.sum(jnp.where(row == column, flags, 0.0), axis=1, keepdims=True)
        if segment == 1:
            weight = jnp.where(scal[SEQ] * text_dev + position < scal[LENGTH], weight, 0.0)
        up[-SMALL:] = jnp.zeros((SMALL, up.shape[1]), F32)
        up[0:text_dev] = out_grad[:, segment, :] * weight


def attend(scal, query, kv_own, kv_oth, masked, text_dev, cols, probs, context):
    rows_dev = query.shape[0]
    keys = 2 * rows_dev
    if masked:
        place = lax.broadcasted_iota(jnp.int32, (1, keys), 1)
        shard = jnp.where(place < rows_dev, scal[SEQ], 1 - scal[SEQ])
        inside = jnp.where(place < rows_dev, place, place - rows_dev)
        valid = (inside >= text_dev) | (shard * text_dev + inside < scal[LENGTH])
    kv_all = jnp.concatenate([kv_own, kv_oth], axis=0)
    for index in range(cols // HD):
        key = pair(head(kv_all, index))
        value = pair(head(kv_all, cols // HD + index))
        scores = mm3(pair(head(query, index)), key, NT) * SCALE
        if masked:
            scores = jnp.where(valid, scores, NEG)
        expo = jnp.exp(scores - jnp.max(scores, axis=-1, keepdims=True))
        prob = expo * (1.0 / jnp.sum(expo, axis=-1, keepdims=True))
        probs[index] = prob
        context[:, index * HD : (index + 1) * HD] = mm3(pair(prob), value)


def attend_first_kernel(text_dev, scal, q, kv_own, kv_oth, wh, wl, context, probs, give, tail):
    attend(scal, q[...], kv_own[...], kv_oth[...], False, text_dev, q.shape[1], probs, context)
    give[...] = half_of(context, 1 - scal[CORE])
    tail[...] = mm3(pair(context[-SMALL:]), (wh[...], wl[...]))


def attend_last_kernel(
    text_dev, scal, q, q_tail, kv_own, kv_oth, own_tail, oth_tail,
    context, probs, give, q_full, own_full, oth_full,
):
    head_rows = q.shape[0] - SMALL
    for full, body, tail in (
        (q_full, q, q_tail),
        (own_full, kv_own, own_tail),
        (oth_full, kv_oth, oth_tail),
    ):
        full[0:head_rows] = body[0:head_rows]
        full[head_rows:] = tail[...]
    attend(
        scal, q_full[...], own_full[...], oth_full[...], True, text_dev, q.shape[1], probs, context
    )
    give[...] = half_of(context, 1 - scal[CORE])


def attend_out_kernel(scal, context, got, wh, wl, sh, sl, partial):
    own = mm3(pair(half_of(context, scal[CORE])), (wh[...], wl[...]))
    partial[...] = own + mm3(pair(got[...]), (sh[...], sl[...]))


def feed_rows(hidden, weights, act_own, act_sib, slope_own, slope_sib):
    left = pair(hidden)
    total = None
    for (ih, il, oh, ol), act, slope in (
        (weights[:4], act_own, slope_own),
        (weights[4:], act_sib, slope_sib),
    ):
        value, grad = gelu_both(mm3(left, load((ih, il))))
        act[...] = value
        slope[...] = grad
        term = mm3(pair(value), load((oh, ol)))
        total = term if total is None else total + term
    return total


def feed_tail_kernel(rows, p0, p1, p2, p3, gains, biases, *refs):
    weights, (hidden, normed, inverse, *others, partial) = refs[:8], refs[8:]
    attended = sum_refs((p0, p1, p2, p3))
    value, unit, scale = norm_forward(rows[-SMALL:] + attended, gains[0:1], biases[0:1])
    hidden[...] = value
    normed[...] = unit
    inverse[...] = scale
    partial[...] = feed_rows(value, weights, *others)


def link_tail_kernel(
    text_dev, hidden, own, oth, gains, biases, rows, high, low, first,
    rows_full, q_tail, kv_tail, normed, inverse, first_next,
):
    first_next[...] = first[...]
    mixed = own[...] + oth[...]
    result, unit, scale = norm_forward(hidden[...] + mixed, gains[1:2], biases[1:2])
    normed[...] = unit
    inverse[...] = scale
    head_rows = rows.shape[0] - SMALL
    place = lax.broadcasted_iota(jnp.int32, (SMALL, 1), 0)
    tail = jnp.where(place < text_dev - head_rows, rows[-SMALL:], result)
    rows_full[0:head_rows] = rows[0:head_rows]
    rows_full[head_rows:] = tail
    left = pair(tail)
    cols = q_tail.shape[1]
    q_tail[...] = mm3(left, (high[0], low[0]), NT)
    kv_tail[:, 0:cols] = mm3(left, (high[1], low[1]), NT)
    kv_tail[:, cols:] = mm3(left, (high[2], low[2]), NT)


def feed_kernel(scal, rows, own, oth, gains, biases, *refs):
    weights, (hidden, normed, inverse, *others, partial) = refs[:8], refs[8:]
    inputs = half_of(rows, scal[CORE]) + (own[...] + oth[...])
    value, unit, scale = norm_forward(inputs, gains[0:1], biases[0:1])
    hidden[...] = value
    normed[...] = unit
    inverse[...] = scale
    partial[...] = feed_rows(value, weights, *others)


def feed_rows_back(grad_two, weights, slope_own, slope_sib, back_own, back_sib):
    left = pair(grad_two)
    total = None
    for (ih, il, oh, ol), slope, back in (
        (weights[:4], slope_own, back_own),
        (weights[4:], slope_sib, back_sib),
    ):
        grad = mm3(left, load((oh, ol))) * slope[...]
        back[...] = grad
        term = mm3(pair(grad), load((ih, il)))
        total = term if total is None else total + term
    return total


def feed_back_kernel(scal, hidden, own, oth, gains, biases, upstream, slope_own, slope_sib, *refs):
    weights, (outcome, pre_two, back_own, *sib, sums, partial, back_sib) = refs[:8], refs[8:]
    mixed = own[...] + oth[...]
    result, unit, scale = norm_forward(hidden[...] + mixed, gains[1:2], biases[1:2])
    outcome[...] = result
    back = half_of(upstream, scal[CORE])
    sums[0:1] = sum_rows(back * unit)
    sums[1:2] = sum_rows(back)
    grad_two = norm_backward(back, unit, scale, gains[1:2])
    pre_two[...] = grad_two
    partial[...] = feed_rows_back(grad_two, weights, slope_own, slope_sib, back_own, back_sib)
    width = sib[0].shape[1]
    for place, some in enumerate(sib):
        some[...] = back_sib[:, place * width : (place + 1) * width]


def context_back_kernel(
    pre_two, own, oth, normed, inverse, gains, wh, wl, sh, sl, pre_one, sums, back_own, back_sib
):
    hidden_back = pre_two[...] + (own[...] + oth[...])
    unit = normed[...]
    sums[0:1] = sum_rows(hidden_back * unit)
    sums[1:2] = sum_rows(hidden_back)
    grad_one = norm_backward(hidden_back, unit, inverse[...], gains[0:1])
    pre_one[...] = grad_one
    left = pair(grad_one)
    back_own[...] = mm3(left, (wh[...], wl[...]), NT)
    back_sib[...] = mm3(left, (sh[...], sl[...]), NT)


def heads_back(context_back, context, prob_of, query, kv_all, cols, query_back, kv_back):
    product = context_back * context
    count = cols // HD
    for index in range(count):
        key = pair(head(kv_all, index))
        value = pair(head(kv_all, count + index))
        back = pair(head(context_back, index))
        delta = jnp.sum(head(product, index), axis=-1, keepdims=True)
        prob = prob_of(index)
        score_back = prob * (mm3(back, value, NT) - delta) * SCALE
        score_back = pair(score_back)
        query_back[:, index * HD : (index + 1) * HD] = mm3(score_back, key)
        kv_back[index * HD : (index + 1) * HD] = mm3(pair(head(query, index)), score_back, TN)
        kv_back[cols + index * HD : cols + (index + 1) * HD] = mm3(back, pair(prob), TN)


def attend_back_kernel(
    scal, back_own, back_got, context, probs, q, kv_own, kv_oth,
    q_back, own_back, give_back, own_tail, give_tail, kv_back,
):
    context_back = in_order(scal[CORE], back_own[...], back_got[...])
    kv_all = jnp.concatenate([kv_own[...], kv_oth[...]], axis=0)
    heads_back(
        context_back,
        context[...],
        lambda index: probs[index],
        q[...],
        kv_all,
        q.shape[1],
        q_back,
        kv_back,
    )
    rows_dev = q.shape[0]
    own_back[...] = kv_back[:, 0:rows_dev]
    give_back[...] = kv_back[:, rows_dev:]
    own_tail[...] = kv_back[:, rows_dev - 128 : rows_dev].T[-SMALL:]
    give_tail[...] = kv_back[:, 2 * rows_dev - 128 : 2 * rows_dev].T[-SMALL:]


def project_back(query_back, kv_back, high, low):
    cols = query_back.shape[1]
    total = mm3(pair(query_back), (high[0], low[0]))
    total = total + mm3(pair(kv_back[:, 0:cols]), (high[1], low[1]))
    return total + mm3(pair(kv_back[:, cols:]), (high[2], low[2]))


def rows_tail_kernel(
    scal, q_back, own_tail, got_tail, high, low, pre_one, give_back, partial, give_next
):
    total = project_back(q_back[-SMALL:], own_tail[...] + got_tail[...], high, low)
    partial[...] = total + jnp.where(scal[MP] == 1, pre_one[-SMALL:], 0.0)
    give_next[...] = give_back[...]


def feed_back_tail_kernel(
    mem_dev, p0, p1, p2, p3, normed, inverse, gains, slope_own, slope_sib, hidden, act, *refs
):
    weights, (pre_two, back_own, partial, sums, bundle, back_sib, back) = refs[:8], refs[8:]
    rows_back = sum_refs((p0, p1, p2, p3))
    first = SMALL - mem_dev
    back[0:first] = jnp.zeros((first, back.shape[1]), F32)
    back[first:] = rows_back[first - mem_dev : first] + rows_back[first:]
    upstream = back[...]
    unit = normed[...]
    sums[0:1] = sum_rows(upstream * unit)
    sums[1:2] = sum_rows(upstream)
    grad_two = norm_backward(upstream, unit, inverse[...], gains[1:2])
    pre_two[...] = grad_two
    partial[...] = feed_rows_back(grad_two, weights, slope_own, slope_sib, back_own, back_sib)
    bundle[0:8] = hidden[8:]
    bundle[8:16] = back_own[8:]
    bundle[16:24] = pre_two[8:]
    bundle[24:32] = act[8:]


def attend_back_tail_kernel(
    scal, pre_two, own, oth, normed, inverse, gains, context, probs, q, kv_own, kv_oth, wh, wl,
    q_back, own_back, give_back, sums_one0, sums_one1, sums_two0, sums_two1, sums_two_tail,
    pre_one, sums, q_back_all, own_back_all, give_back_all, q_tail, kv_back,
):
    hidden_back = pre_two[...] + (own[...] + oth[...])
    unit = normed[...]
    one = sums_one0[...] + sums_one1[...]
    two = sums_two0[...] + sums_two1[...]
    once = jnp.where(scal[CORE] == 0, 1.0, 0.0)
    two = two + once * sums_two_tail[...]
    sums[0:1] = one[0:1] + once * sum_rows(hidden_back * unit)
    sums[1:2] = two[0:1]
    sums[2:3] = one[1:2] + once * sum_rows(hidden_back)
    sums[3:4] = two[1:2]
    sums[4:] = jnp.zeros((4, sums.shape[1]), F32)
    grad_one = norm_backward(hidden_back, unit, inverse[...], gains[0:1])
    pre_one[...] = grad_one
    context_back = mm3(pair(grad_one), (wh[...], wl[...]), NT)
    kv_all = jnp.concatenate([kv_own[...], kv_oth[...]], axis=0)
    heads_back(
        context_back, context[-SMALL:], lambda index: probs[index, -SMALL:], q[-SMALL:], kv_all,
        q.shape[1], q_tail, kv_back,
    )
    head_rows = q.shape[0] - SMALL
    q_back_all[0:head_rows] = q_back[0:head_rows]
    q_back_all[head_rows:] = q_back[head_rows:] + q_tail[...]
    rows_dev = q.shape[0]
    own_back_all[...] = own_back[...] + kv_back[:, 0:rows_dev]
    keys = kv_back.shape[0]
    give_back_all[0:keys] = give_back[...] + kv_back[:, rows_dev:]
    for part in range(sums.shape[1] // rows_dev):
        place = slice(part * rows_dev, (part + 1) * rows_dev)
        give_back_all[keys + 8 * part : keys + 8 * part + 8] = sums[:, place]


def turn_back(scal, q_back, own_back, got_back, kv_back, give):
    cols = q_back.shape[1]
    rows = own_back.shape[0]
    half = q_back.shape[0] // 2
    kv_back[...] = (own_back[...] + got_back[0:rows]).T
    give[0:half, 0:cols] = half_of(q_back, 1 - scal[CORE])
    give[0:half, cols : 3 * cols] = half_of(kv_back, 1 - scal[CORE])


def turn_back_last_kernel(scal, q_back, own_back, got_back, kv_back, give):
    turn_back(scal, q_back, own_back, got_back, kv_back, give)


def turn_back_first_kernel(scal, q_back, own_back, got_back, own_sums, kv_back, give, sums):
    turn_back(scal, q_back, own_back, got_back, kv_back, give)
    rows, width = own_back.shape
    for part in range(sums.shape[1] // width):
        place = slice(part * width, (part + 1) * width)
        sums[:, place] = own_sums[:, place] + got_back[rows + 8 * part : rows + 8 * part + 8]
    give[q_back.shape[0] // 2 :] = sums[...]


def rows_kernel(scal, q_back, kv_back, got, high, low, sib_high, sib_low, partial):
    cols = q_back.shape[1]
    core = scal[CORE]
    half = q_back.shape[0] // 2
    own = project_back(half_of(q_back, core), half_of(kv_back, core), high, low)
    got_q, got_kv = got[0:half, 0:cols], got[0:half, cols : 3 * cols]
    partial[...] = own + project_back(got_q, got_kv, sib_high, sib_low)


def end_rows_kernel(scal, pre_one, own, oth, *refs):
    *tail, out = refs
    total = pre_one[...] + (own[...] + oth[...])
    out[...] = total
    if tail:
        out[-SMALL:] = total[-SMALL:] + jnp.where(scal[CORE] == 1, tail[0][...], 0.0)


def end_text(core, own0, oth0, own1, oth1, memory, text, last):
    text_dev = text.shape[0]
    text[:, 0, :] = in_order(core, own0, oth0)[0:text_dev]
    text[:, 1, :] = in_order(core, own1, oth1)[0:text_dev]
    for index in range(last.shape[0]):
        last[index] = memory[index : index + 1]


def end_text_kernel(scal, own0, oth0, own1, oth1, text, last):
    core = scal[CORE]
    memory = jnp.where(core == 1, own1[-SMALL:], oth1[-SMALL:])[SMALL - last.shape[0] :]
    end_text(core, own0[...], oth0[...], own1[...], oth1[...], memory, text, last)


def end_grad_kernel(scal, own0, oth0, own1, oth1, text, last):
    core = scal[CORE]
    mem_dev = last.shape[0]
    memory = jnp.where(core == 1, own0[-SMALL:], oth0[-SMALL:])[SMALL - 2 * mem_dev :]
    memory = memory[0:mem_dev] + memory[mem_dev:]
    end_text(core, own0[...], oth0[...], own1[...], oth1[...], memory, text, last)


def block_at(scal, slot):
    return jnp.bitwise_xor(scal[BATCH], slot)


def stacked(*refs):
    return jnp.concatenate([ref[...] for ref in refs], axis=0)


def put_chunks(product, scal, batch_count, chunk, outs):
    for part in range(len(outs) // 2):
        keep, give = outs[2 * part], outs[2 * part + 1]
        width = keep.shape[2]
        columns = slice(part * width, (part + 1) * width)
        for slot in range(batch_count):
            block = 2 * block_at(scal, slot)
            mine = pl.multiple_of((block + scal[SEQ]) * chunk, chunk)
            others = pl.multiple_of((block + 1 - scal[SEQ]) * chunk, chunk)
            keep[slot] = product[pl.ds(mine, chunk), columns]
            give[slot * chunk : (slot + 1) * chunk] = product[pl.ds(others, chunk), columns]


def feed_in_kernel(columns, batch_count, chunk, scal, *refs):
    lefts, rights, *outs, product = refs[0:4], refs[4:8], *refs[8:]
    rights = [rights[0].at[:, columns], rights[1], rights[2].at[:, columns], rights[3]]
    product[...] = mm3(pair(stacked(*lefts)), pair(stacked(*rights)), TN)
    if batch_count != 4:
        outs[0][...] = product[...]
        return
    put_chunks(product, scal, batch_count, chunk, outs)


def feed_out_kernel(batch_count, chunk, scal, *refs):
    lefts, rights, outs, product = refs[0:4], refs[4:8], refs[8:-1], refs[-1]
    product[...] = mm3(pair(stacked(*lefts)), pair(stacked(*rights)), TN)
    if batch_count != 4:
        outs[0][...] = product[...]
        return
    for slot in range(batch_count):
        block = 2 * block_at(scal, slot)
        mine = pl.multiple_of((block + scal[SEQ]) * chunk, chunk)
        others = pl.multiple_of((block + 1 - scal[SEQ]) * chunk, chunk)
        outs[slot % 2][slot // 2, 0:chunk] = product[pl.ds(mine, chunk), :]
        outs[slot % 2][slot // 2, chunk:] = product[pl.ds(others, chunk), :]


def attend_weights_kernel(
    batch_count, chunk, scal, rows0, rows1, q0, q1, kv0, kv1,
    one0, oth0, tail, one1, oth1, c0, c1, bundle, *refs,
):
    *outs, product = refs
    core = scal[CORE]
    rows = pair(stacked(rows0, rows1))
    cols = q0.shape[1]
    product[:, 0:cols] = mm3(rows, pair(stacked(q0, q1)), TN)
    product[:, cols : 3 * cols] = mm3(rows, pair(stacked(kv0, kv1)), TN)
    ones = in_order(core, one0[...], oth0[...])
    head_rows = ones.shape[0] - SMALL
    ones = jnp.concatenate(
        [ones[0:head_rows], ones[head_rows:] + tail[...], in_order(core, one1[...], oth1[...])],
        axis=0,
    )
    product[:, 3 * cols :] = mm3(pair(ones), pair(stacked(c0, c1)), TN)
    if batch_count != 4:
        outs[0][...] = product[...]
        return
    put_chunks(product, scal, batch_count, chunk, outs)
    put_folded(outs[1], batch_count * chunk, bundle[...])


def turn_seq_kernel(*refs):
    *terms, keep_next, give_next = refs
    chunk = terms[0].shape[1]
    first = 0
    for keep, got in zip(terms[0::2], terms[1::2]):
        place = slice(first, first + keep.shape[2])
        first += keep.shape[2]
        for slot in range(keep.shape[0]):
            target = give_next if slot % 2 else keep_next
            total = keep[slot] + got[slot * chunk : (slot + 1) * chunk]
            target[slot // 2, :, place] = total


def turn_batch_kernel(keep, got, keep_next, give_next):
    keep_next[...] = keep[0] + got[0]
    give_next[...] = keep[1] + got[1]


def turn_place_kernel(keep, got, keep_next, give_next):
    total = keep[...] + got[...]
    chunk = keep_next.shape[0]
    keep_next[...] = total[0:chunk]
    give_next[...] = total[chunk:]


def pick(values, blocks, chunk, index):
    picked = values[:, 0:chunk]
    for block in range(1, blocks):
        picked = jnp.where(index == block, values[:, block * chunk : (block + 1) * chunk], picked)
    return picked


def put_bundle(piece, sources, batch_count, chunk, mem_dev, index):
    first = 8 - mem_dev
    piece[...] = jnp.zeros(piece.shape, F32)
    for source in range(2):
        for kind in range(2):
            slot = 2 * source + kind
            left = sources[source][16 * kind : 16 * kind + 8]
            right = sources[source][16 * kind + 8 : 16 * kind + 16]
            left = pick(left, 2 * batch_count, chunk, index)
            piece[slot * mem_dev : (slot + 1) * mem_dev] = right[first:]
            row = 4 * mem_dev + slot
            for place in range(mem_dev):
                piece[row : row + 1, 128 * place : 128 * place + chunk] = left[
                    first + place : first + place + 1
                ]


def put_folded(target, first, values):
    rows, width = values.shape
    target[first : first + rows] = values[:, 0 : width // 2]
    target[first + rows : first + 2 * rows] = values[:, width // 2 :]
    return first + 2 * rows


def get_folded(source, first, rows):
    return jnp.concatenate(
        [source[first : first + rows], source[first + rows : first + 2 * rows]], axis=1
    )


def turn_first_kernel(
    batch_count, chunk, mem_dev, scal, keep, got, bundle, sums, got_give,
    keep_next, give_next, own, norms, *others,
):
    for slot in range(keep.shape[0]):
        total = keep[slot] + got[slot * chunk : (slot + 1) * chunk]
        if slot % 2:
            give_next[slot // 2 * chunk : (slot // 2 + 1) * chunk] = total
        else:
            keep_next[slot // 2] = total
    sources = (bundle[...], get_folded(got, batch_count * chunk, bundle.shape[0]))
    pieces = (own, *others)
    for slot in range(batch_count):
        index = 2 * block_at(scal, slot) + scal[SEQ]
        put_bundle(pieces[slot], sources, batch_count, chunk, mem_dev, index)
    norms[...] = sums[...] + got_give[-8:]
    row = 2 * chunk
    for values in (others[0], others[2], norms):
        row = put_folded(give_next, row, values[...])


def next_first_kernel(chunk, keep, got, norms, other, keep_next, give_next, bundle, norms_next):
    rows = bundle.shape[0]
    keep_next[...] = keep[0] + got[0:chunk]
    give_next[0:chunk] = keep[1] + got[chunk : 2 * chunk]
    row = 2 * chunk
    bundle[...] = get_folded(got, row, rows)
    norms_next[...] = norms[...] + get_folded(got, row + 4 * rows, 8)
    place = chunk
    for values in (other[...], get_folded(got, row + 2 * rows, rows), norms_next[...]):
        place = put_folded(give_next, place, values)


def end_bundle_kernel(blocks, scal, got, norms, bundle2, bundle3, gains, biases):
    rows = bundle2.shape[0]
    chunk = gains.shape[1]
    bundle2[...] = get_folded(got, chunk, rows)
    bundle3[...] = get_folded(got, chunk + 2 * rows, rows)
    total = norms[...] + get_folded(got, chunk + 4 * rows, 8)
    picked = pick(total, blocks, chunk, scal[BATCH] * 2 + scal[SEQ])
    gains[...] = picked[0:2]
    biases[...] = picked[2:4]


def bundle_product(kind, mem_dev, bundles, left, right):
    chunk = left.shape[1]
    left[...] = jnp.zeros(left.shape, F32)
    right[...] = jnp.zeros(right.shape, F32)
    for number, bundle in enumerate(bundles):
        for source in range(2):
            slot = 2 * source + kind
            base = 8 * (2 * number + source)
            right[base : base + mem_dev] = bundle[slot * mem_dev : (slot + 1) * mem_dev]
            row = 4 * mem_dev + slot
            for place in range(mem_dev):
                left[base + place : base + place + 1] = bundle[
                    row : row + 1, 128 * place : 128 * place + chunk
                ]
    return mm3(pair(left[...]), pair(right[...]), TN)


def end_out_kernel(mem_dev, keep, got, b0, b1, b2, b3, out, left, right):
    extra = bundle_product(1, mem_dev, (b0, b1, b2, b3), left, right)
    out[...] = keep[...] + got[...] + extra


def end_in_kernel(mem_dev, *refs):
    *terms, b0, b1, b2, b3, out, left, right = refs
    extra = bundle_product(0, mem_dev, (b0, b1, b2, b3), left, right)
    first = 0
    for keep, got in zip(terms[0::2], terms[1::2]):
        last = first + keep.shape[1]
        out[:, first:last] = keep[...] + got[...] + extra[:, first:last]
        first = last


def end_attend_kernel(*refs):
    *terms, grad_in, grad_out = refs
    chunk = grad_in.shape[1]
    parts = [keep[...] + got[0:chunk] for keep, got in zip(terms[0::2], terms[1::2])]
    total = jnp.concatenate(parts, axis=1)
    cols = grad_in.shape[2]
    for part in range(3):
        grad_in[part] = total[:, part * cols : (part + 1) * cols]
    grad_out[...] = total[:, 3 * cols :].T


def shape(*dims, dtype=F32):
    return jax.ShapeDtypeStruct(dims, dtype)


COSTS = {
    "attend": 3.2,
    "feed": 3.3,
    "feed_back": 3.2,
    "context_back": 0.9,
    "attend_back": 3.8,
    "feed_in": 1.8,
    "feed_out": 2.8,
    "rows_tail": 6.0,
    "feed_tail": 2.0,
    "feed_back_tail": 10.0,
    "attend_back_tail": 8.0,
    "attend_weights": 3.5,
    "attend_out": 1.0,
    "rows": 1.6,
    "end_text": 15.0,
    "end_grad": 2.0,
    "turn_attend": 1.0,
    "turn_back": 0.8,
    "turn_weights": 2.5,
    "split_in_sib": 1.8,
    "upstream": 1.0,
    "project": 1.5,
    "start": 2.0,
    "split_feed": 0.7,
    "split_feed_sib": 0.7,
    "end_rows": 0.6,
}
COST_SCALE = 0.4


class Order:
    def __init__(self, scal):
        self.scal = scal
        self.last = None
        self.extra = []

    def wait(self, *values):
        self.extra += values

    def call(self, kernel, outs, *args, scal=False, scratch=(), name=None):
        cost = COST_SCALE * COSTS.get(name.rstrip("0123456789"), 0.2)
        after = [] if self.last is None else [self.last]
        after += self.extra
        self.extra = []
        count = len(args) + scal
        skip = len(after)

        def body(*refs):
            kernel(*refs[:count], *refs[count + skip :])

        ins = [SMEM_SPEC] * scal + [VMEM_SPEC] * len(args)
        ins += [pl.BlockSpec(memory_space=pl.ANY)] * skip
        result = pl.pallas_call(
            body,
            out_shape=outs,
            in_specs=ins,
            out_specs=jax.tree.map(lambda _: VMEM_SPEC, outs),
            scratch_shapes=list(scratch),
            compiler_params=pltpu.CompilerParams(vmem_limit_bytes=KERNEL_VMEM),
            cost_estimate=pl.CostEstimate(
                flops=int(cost * 10**9), bytes_accessed=0, transcendentals=0
            ),
            name=name,
        )(*([self.scal] if scal else []), *args, *after)
        self.last = min(jax.tree.leaves(result), key=lambda value: value.size)
        return result


def swap_seq(values):
    return lax.ppermute(values, "seq", SEQ_SWAP)


def to_core(values):
    return lax.ppermute(values, "mp", CORE_SWAP)


def to_chip(values):
    return lax.ppermute(values, "mp", CHIP_SWAP)


def spread_mp(values):
    return values, to_core(values), to_chip(values), lax.ppermute(values, "mp", CROSS_SWAP)


def swap_batch(values, bit):
    count = lax.axis_size("batch")
    return lax.ppermute(values, "batch", [(place, place ^ bit) for place in range(count)])


def local(
    text_rows,
    memory_in,
    text_length,
    mlm_mask,
    out_grad,
    attn_in,
    attn_out,
    ffn_in,
    ffn_out,
    norm_gains,
    norm_biases,
):
    seg_count, text_dev, width = text_rows.shape[1:]
    mem_dev = memory_in.shape[1]
    cols = attn_in.shape[2]
    units = ffn_in.shape[1]
    heads = cols // HD
    batch_count = lax.axis_size("batch")
    seq_count = lax.axis_size("seq")
    rows_dev = text_dev + 2 * mem_dev
    half = rows_dev // 2
    third = units // 3
    chunk = width // (batch_count * seq_count)
    text_rows = text_rows.reshape(seg_count, text_dev, width).transpose(1, 0, 2)
    out_grad = out_grad.reshape(seg_count, text_dev, width).transpose(1, 0, 2)
    memory_in = memory_in.transpose(1, 0, 2)
    mlm_mask = mlm_mask.reshape(seg_count, text_dev)
    attn_in = attn_in.transpose(0, 2, 1)
    scal = jnp.stack(
        [
            lax.axis_index("mp") % 2,
            lax.axis_index("seq"),
            text_length[0],
            lax.axis_index("batch"),
            lax.axis_index("mp"),
        ]
    ).astype(jnp.int32)

    whole = shape(rows_dev, width)
    part = shape(half, width)
    tail_shape = shape(SMALL, width)
    row_sums = shape(2, width)
    order = Order(scal)
    call = order.call

    def feed(segment, rows, own, oth):
        return call(
            feed_kernel,
            [part, part, shape(half, 1)] + [shape(half, units)] * 4 + [part],
            rows,
            own,
            oth,
            norm_gains,
            norm_biases,
            *feed_w,
            scal=True,
            name="feed%d" % segment,
        )

    def feed_back(segment, hidden, own, oth, slopes):
        return call(
            feed_back_kernel,
            [part, part, shape(half, units)] + [shape(half, third)] * 3 + [row_sums, part],
            hidden,
            own,
            oth,
            norm_gains,
            norm_biases,
            upstream[segment],
            *slopes,
            *feed_turned,
            scal=True,
            scratch=[pltpu.VMEM((half, units), F32)],
            name="feed_back%d" % segment,
        )

    def context_back(segment, pre_two, own, oth, normed, inverse):
        return call(
            context_back_kernel,
            [part, row_sums] + [shape(half, cols)] * 2,
            pre_two,
            own,
            oth,
            normed,
            inverse,
            norm_gains,
            *out_w,
            *out_sib,
            name="context_back%d" % segment,
        )

    def attend_back(segment, own, got, context, probs, query, kv):
        return call(
            attend_back_kernel,
            [shape(rows_dev, cols)]
            + [shape(2 * cols, rows_dev)] * 2
            + [shape(SMALL, 2 * cols)] * 2,
            own,
            got,
            context,
            probs,
            query,
            *kv,
            scal=True,
            scratch=[pltpu.VMEM((2 * cols, seq_count * rows_dev), F32)],
            name="attend_back%d" % segment,
        )

    def turn_seq(*terms, name):
        columns = sum(keep.shape[2] for keep in terms[0::2])
        keep, give = call(turn_seq_kernel, [shape(2, chunk, columns)] * 2, *terms, name=name)
        return keep, swap_batch(give, 1)

    def turn_batch(keep, got, name):
        keep, give = call(turn_batch_kernel, [shape(*keep.shape[1:])] * 2, keep, got, name=name)
        return keep, swap_batch(give, 2)

    def rows_partial(segment, qb, kv_back, got):
        return call(
            rows_kernel, part, qb, kv_back, got, *in_w, *in_sib, scal=True, name="rows%d" % segment
        )

    rows0, rows1, in_h, in_l, kv0 = call(
        start_kernel,
        [whole, whole]
        + [shape(3, cols, width, dtype=BF16)] * 2
        + [shape(rows_dev, 2 * cols)],
        text_rows,
        memory_in,
        attn_in,
        scal=True,
        name="start",
    )
    kv0_oth = swap_seq(kv0)
    in_w = (in_h, in_l)
    q0, q1, kv1 = call(
        project_kernel,
        [shape(rows_dev, cols)] * 2 + [shape(rows_dev, 2 * cols)],
        rows0,
        rows1,
        *in_w,
        name="project",
    )
    kv1_oth = swap_seq(kv1)
    out_w = call(split_kernel, [shape(cols, width, dtype=BF16)] * 2, attn_out, name="split_out")
    feed_shapes = [shape(width, units, dtype=BF16)] * 2 + [shape(units, width, dtype=BF16)] * 2
    feed_own = call(split_kernel, feed_shapes, ffn_in, ffn_out, name="split_feed")
    feed_sib = call(
        split_kernel, feed_shapes, to_core(ffn_in), to_core(ffn_out), name="split_feed_sib"
    )
    feed_w = (*feed_own, *feed_sib)
    out_sib = call(
        split_kernel, [shape(cols, width, dtype=BF16)] * 2, to_core(attn_out), name="split_out_sib"
    )

    attended = [shape(rows_dev, cols), shape(heads, rows_dev, seq_count * rows_dev)]
    attended += [shape(half, cols)]
    c0, probs0, give, tail = call(
        functools.partial(attend_first_kernel, text_dev),
        attended + [tail_shape],
        q0,
        kv0,
        kv0_oth,
        *out_w,
        scal=True,
        name="attend0",
    )
    tails = spread_mp(tail)
    got_c0 = to_core(give)
    hidden_tail, unit_one, scale_one, act_tail, _, slope_tail, slope_tail_sib, tail = call(
        feed_tail_kernel,
        [tail_shape, tail_shape, shape(SMALL, 1)] + [shape(SMALL, units)] * 4 + [tail_shape],
        rows0,
        *tails,
        norm_gains,
        norm_biases,
        *feed_w,
        name="feed_tail",
    )
    tail_oth = to_chip(tail)
    own0 = call(
        attend_out_kernel,
        part,
        c0,
        got_c0,
        *out_w,
        *out_sib,
        scal=True,
        name="attend_out0",
    )
    order.wait(kv1_oth)
    rows1, q_tail, kv_tail, unit_two, scale_two, own0 = call(
        functools.partial(link_tail_kernel, text_dev),
        [whole, shape(SMALL, cols), shape(SMALL, 2 * cols), tail_shape, shape(SMALL, 1), part],
        hidden_tail,
        tail,
        tail_oth,
        norm_gains,
        norm_biases,
        rows1,
        *in_w,
        own0,
        name="link_tail",
    )
    kv_tail_oth = swap_seq(kv_tail)
    oth0 = to_chip(own0)
    c1, probs1, give, q1, kv1, kv1_oth = call(
        functools.partial(attend_last_kernel, text_dev),
        attended + [shape(rows_dev, cols)] + [shape(rows_dev, 2 * cols)] * 2,
        q1,
        q_tail,
        kv1,
        kv1_oth,
        kv_tail,
        kv_tail_oth,
        scal=True,
        name="attend1",
    )
    order.wait(oth0)
    own1 = call(
        attend_out_kernel, part, c1, to_core(give), *out_w, *out_sib, scal=True, name="attend_out1"
    )
    oth1 = to_chip(own1)
    hidden0, normed0, inverse0, act0, give, slope0, slope0_sib, own0 = feed(0, rows0, own0, oth0)
    oth0 = to_chip(own0)
    got_feed0 = to_core(hidden0), to_core(give)
    feed_turned = call(
        turn_weights_kernel,
        [shape(units, width, dtype=BF16)] * 2
        + [shape(width, units, dtype=BF16)] * 2
        + [shape(units, width, dtype=BF16)] * 2
        + [shape(width, units, dtype=BF16)] * 2,
        *feed_w,
        name="turn_weights",
    )
    in_sib = call(
        split_kernel, [shape(3, cols, width, dtype=BF16)] * 2, to_core(attn_in), name="split_in_sib"
    )
    upstream = call(upstream_kernel, [whole] * 2, out_grad, mlm_mask, scal=True, name="upstream")
    hidden1, normed1, inverse1, act1, give, slope1, slope1_sib, own1 = feed(1, rows1, own1, oth1)
    oth1 = to_chip(own1)
    got_feed1 = to_core(hidden1), to_core(give)
    order.wait(*got_feed0)
    text0, two0, back0, *gives, sums_two0, own0 = feed_back(
        0, hidden0, own0, oth0, (slope0, slope0_sib)
    )
    oth0 = to_chip(own0)
    got_two0, got_back0 = to_core(two0), [to_core(give) for give in gives]
    got_text0 = to_core(text0)
    order.wait(*got_feed1)
    text1, two1, back1, *gives, sums_two1, own1 = feed_back(
        1, hidden1, own1, oth1, (slope1, slope1_sib)
    )
    oth1 = to_chip(own1)
    got_two1, got_back1 = to_core(two1), [to_core(give) for give in gives]
    got_text1 = to_core(text1)

    def weights(kernel, outs, arrays, columns, name):
        if batch_count != 4:
            outs = [shape(width, columns)]
        return call(
            functools.partial(kernel, batch_count, chunk),
            outs,
            *arrays,
            scal=True,
            scratch=[pltpu.VMEM((width, columns), F32)],
            name=name,
        )

    def feed_in(number, first, last, name):
        return weights(
            functools.partial(feed_in_kernel, slice(first, last)),
            [shape(batch_count, chunk, last - first), shape(batch_count * chunk, last - first)],
            (hidden0, got_feed0[0], hidden1, got_feed1[0])
            + (back0, got_back0[number], back1, got_back1[number]),
            last - first,
            name,
        )

    in_first = feed_in(0, 0, third, "feed_in0")
    in_terms = ()
    if batch_count == 4:
        in_terms = in_first[0], swap_seq(in_first[1])
    one0, sums_one0, back_own, back_give = context_back(0, two0, own0, oth0, normed0, inverse0)
    got_one0, back_got = to_core(one0), to_core(back_give)
    qb0, kvo0, kvg0, _, _ = attend_back(0, back_own, back_got, c0, probs0, q0, (kv0, kv0_oth))
    one1, sums_one1, back_own, back_give = context_back(1, two1, own1, oth1, normed1, inverse1)
    got_one1, back_got = to_core(one1), to_core(back_give)
    out_terms = weights(
        feed_out_kernel,
        [shape(2, 2 * chunk, units)] * 2,
        (two0, got_two0, two1, got_two1, act0, got_feed0[1], act1, got_feed1[1]),
        units,
        "feed_out",
    )
    if batch_count == 4:
        out_got = swap_batch(out_terms[1], 1)
    order.wait(*in_terms[1:])
    qb1, kvo1, kvg1, own_tail, give_tail = attend_back(
        1, back_own, back_got, c1, probs1, q1, (kv1, kv1_oth)
    )
    tail, kvg1 = call(
        rows_tail_kernel,
        [tail_shape, shape(2 * cols, rows_dev)],
        qb1,
        own_tail,
        swap_seq(give_tail),
        *in_w,
        one1,
        kvg1,
        scal=True,
        name="rows_tail",
    )
    got1 = swap_seq(kvg1)
    two_tail, back_tail, tail, sums_two_tail, bundle = call(
        functools.partial(feed_back_tail_kernel, mem_dev),
        [tail_shape, shape(SMALL, units), tail_shape, row_sums, shape(32, width)],
        *spread_mp(tail),
        unit_two,
        scale_two,
        norm_gains,
        slope_tail,
        slope_tail_sib,
        hidden_tail,
        act_tail,
        *feed_turned,
        scratch=[pltpu.VMEM((SMALL, units), F32), pltpu.VMEM((SMALL, width), F32)],
        name="feed_back_tail",
    )
    tail_oth = to_chip(tail)
    text_shape = [shape(text_dev, seg_count, width), shape(mem_dev, 1, width)]

    in_second = feed_in(1, third, 2 * third, "feed_in1")
    if batch_count == 4:
        in_terms += in_second[0], swap_seq(in_second[1])
    one_tail, sums, qb0, kvo0, kvg0 = call(
        attend_back_tail_kernel,
        [tail_shape, shape(8, width), shape(rows_dev, cols), shape(2 * cols, rows_dev)]
        + [shape(2 * cols + 8 * (width // rows_dev), rows_dev)],
        two_tail,
        tail,
        tail_oth,
        unit_one,
        scale_one,
        norm_gains,
        c0,
        probs0,
        q0,
        kv0,
        kv0_oth,
        *out_w,
        qb0,
        kvo0,
        kvg0,
        sums_one0,
        sums_one1,
        sums_two0,
        sums_two1,
        sums_two_tail,
        scal=True,
        scratch=[
            pltpu.VMEM((SMALL, cols), F32),
            pltpu.VMEM((2 * cols, seq_count * rows_dev), F32),
        ],
        name="attend_back_tail",
    )
    got0 = swap_seq(kvg0)
    if batch_count == 4:
        out_keep, give = call(
            turn_batch_kernel,
            [shape(2 * chunk, units)] * 2,
            out_terms[0],
            out_got,
            name="turn_out",
        )
        out_got = swap_batch(give, 2)
    kvb1, give = call(
        turn_back_last_kernel,
        [shape(rows_dev, 2 * cols), shape(half, 3 * cols)],
        qb1,
        kvo1,
        got1,
        scal=True,
        name="turn_back1",
    )
    got_give1 = to_core(give)
    def end_rows(segment, one, own, oth, *tail):
        return call(
            end_rows_kernel, part, one, own, oth, *tail, scal=True, name="end_rows%d" % segment
        )

    in_third = feed_in(2, 2 * third, units, "feed_in2")
    if batch_count == 4:
        in_terms += in_third[0], swap_seq(in_third[1])
    kvb0, give, sums = call(
        turn_back_first_kernel,
        [shape(rows_dev, 2 * cols), shape(half + 8, width), shape(8, width)],
        qb0,
        kvo0,
        got0,
        sums,
        scal=True,
        name="turn_back0",
    )
    got_give0 = to_core(give)
    if batch_count != 4:
        outs = [shape(width, 4 * cols)]
    else:
        outs = [shape(batch_count, chunk, 2 * cols), shape(batch_count * chunk + 64, 2 * cols)]
        outs += [shape(batch_count, chunk, 2 * cols), shape(batch_count * chunk, 2 * cols)]
    attend_terms = call(
        functools.partial(attend_weights_kernel, batch_count, chunk),
        outs,
        rows0,
        rows1,
        qb0,
        qb1,
        kvb0,
        kvb1,
        one0,
        got_one0,
        one_tail,
        one1,
        got_one1,
        c0,
        c1,
        bundle,
        scal=True,
        scratch=[pltpu.VMEM((width, 4 * cols), F32)],
        name="attend_weights",
    )
    if batch_count == 4:
        in_turned = turn_seq(*in_terms, name="turn_in")
        attend_got = swap_seq(attend_terms[1]), swap_seq(attend_terms[3])
    own1 = rows_partial(1, qb1, kvb1, got_give1)
    oth1 = to_chip(own1)
    own0 = rows_partial(0, qb0, kvb0, got_give0)
    oth0 = to_chip(own0)
    if batch_count == 4:
        out_keep, give = call(
            turn_place_kernel,
            [shape(chunk, units)] * 2,
            out_keep,
            out_got,
            name="next_out",
        )
        out_got = swap_seq(give)
    text_out, memory_out = call(
        end_text_kernel,
        text_shape,
        text0,
        got_text0,
        text1,
        got_text1,
        scal=True,
        name="end_text",
    )
    if batch_count == 4:
        in_pieces = turn_batch(*in_turned, "next_in")
        folded = [shape(2 * chunk + 112, 2 * cols)] + [shape(24, width), shape(8, width)]
        attend_keep, give, bundle0, norms, _, other, _ = call(
            functools.partial(turn_first_kernel, batch_count, chunk, mem_dev),
            [shape(2, chunk, 2 * cols)] + folded + [shape(24, width)] * 3,
            attend_terms[0],
            attend_got[0],
            bundle,
            sums,
            got_give0,
            scal=True,
            name="turn_attend0",
        )
        got = swap_batch(give, 1)
    rows_back1 = end_rows(1, one1, own1, oth1)
    got_rows1 = to_core(rows_back1)
    rows_back0 = end_rows(0, one0, own0, oth0, one_tail)
    got_rows0 = to_core(rows_back0)
    if batch_count == 4:
        attend_second = turn_seq(attend_terms[2], attend_got[1], name="turn_attend1")
        order.wait(in_pieces[1])
        attend_keep, give, bundle1, norms = call(
            functools.partial(next_first_kernel, chunk),
            [shape(chunk, 2 * cols), shape(chunk + 112, 2 * cols)] + folded[1:],
            attend_keep,
            got,
            norms,
            other,
            name="next_attend0",
        )
        attend_pieces = attend_keep, swap_batch(give, 2)
    text_grad, memory_grad = call(
        end_grad_kernel,
        text_shape,
        rows_back0,
        got_rows0,
        rows_back1,
        got_rows1,
        scal=True,
        name="end_grad",
    )
    if batch_count == 4:
        attend_pieces += turn_batch(*attend_second, "next_attend1")
        bundle2, bundle3, gains_grad, biases_grad = call(
            functools.partial(end_bundle_kernel, batch_count * seq_count),
            [shape(24, width)] * 2 + [shape(2, chunk)] * 2,
            attend_pieces[1],
            norms,
            scal=True,
            name="end_bundle",
        )
        bundles = bundle0, bundle1, bundle2, bundle3
        factors = [pltpu.VMEM((64, chunk), F32), pltpu.VMEM((64, units), F32)]
        ffn_out_grad = call(
            functools.partial(end_out_kernel, mem_dev),
            shape(chunk, units),
            out_keep,
            out_got,
            *bundles,
            scratch=factors,
            name="end_out",
        )
        ffn_in_grad = call(
            functools.partial(end_in_kernel, mem_dev),
            shape(chunk, units),
            *in_pieces,
            *bundles,
            scratch=factors,
            name="end_in",
        )
        attn_in_grad, attn_out_grad = call(
            end_attend_kernel,
            [shape(3, chunk, cols), shape(cols, chunk)],
            *attend_pieces,
            name="end_attend",
        )
    else:

        def scatter(values, axis):
            return lax.psum_scatter(values, ("batch", "seq"), scatter_dimension=axis, tiled=True)

        def outer(left, right):
            return jnp.einsum("rd,rf->df", left, right, precision=lax.Precision.HIGHEST)

        ffn_out_grad = scatter(out_terms[0] + outer(bundle[16:24], bundle[24:32]), 0)
        in_terms = jnp.concatenate([in_first[0], in_second[0], in_third[0]], axis=1)
        ffn_in_grad = scatter(in_terms + outer(bundle[0:8], bundle[8:16]), 0)
        total = scatter(attend_terms[0], 0)
        attn_in_grad = jnp.stack([total[:, t * cols : (t + 1) * cols] for t in range(3)])
        attn_out_grad = total[:, 3 * cols :].T
        norms = lax.psum(sums + got_give0[half:], "batch")
        place = (lax.axis_index("batch") * seq_count + lax.axis_index("seq")) * chunk
        norms = lax.dynamic_slice_in_dim(norms, place, chunk, 1)
        gains_grad, biases_grad = norms[0:2], norms[2:4]
    return (
        text_out.transpose(1, 0, 2)[None],
        memory_out.transpose(1, 0, 2),
        text_grad.transpose(1, 0, 2)[None],
        memory_grad.transpose(1, 0, 2),
        attn_in_grad,
        attn_out_grad,
        ffn_in_grad,
        ffn_out_grad.T,
        gains_grad,
        biases_grad,
    )


def solution(mesh):
    placed = (
        P("batch", None, "seq", None),
        P("batch", "seq", None),
        P("batch"),
        P("batch", None, "seq"),
        P("batch", None, "seq", None),
        P(None, None, "mp"),
        P("mp", None),
        P(None, "mp"),
        P("mp", None),
        P(),
        P(),
    )
    return jax.shard_map(
        local,
        mesh=mesh,
        in_specs=placed,
        out_specs=(
            P("batch", None, "seq", None),
            P("batch", "seq", None),
            P("batch", None, "seq", None),
            P("batch", "seq", None),
            P(None, ("batch", "seq"), "mp"),
            P("mp", ("batch", "seq")),
            P(("batch", "seq"), "mp"),
            P("mp", ("batch", "seq")),
            P(None, ("batch", "seq")),
            P(None, ("batch", "seq")),
        ),
        check_vma=False,
    )
```

```python
import functools
import math
import types

import jax
import jax.numpy as jnp
from jax import lax
from jax.experimental import pallas as pl
from jax.experimental.pallas import tpu as pltpu
from jax.sharding import PartitionSpec as P

HD = 64
EPS = 1e-12
NEG = -1e30
SMALL = 16
SCALE = 1.0 / math.sqrt(HD)
F32 = jnp.float32
BF16 = jnp.bfloat16
NN = ((1,), (0,))
NT = ((1,), (1,))
TN = ((0,), (0,))
CORE_SWAP = [(0, 1), (1, 0), (2, 3), (3, 2)]
CHIP_SWAP = [(0, 2), (2, 0), (1, 3), (3, 1)]
CROSS_SWAP = [(0, 3), (3, 0), (1, 2), (2, 1)]
SEQ_SWAP = [(0, 1), (1, 0)]
VMEM_SPEC = pl.BlockSpec(memory_space=pltpu.VMEM)
SMEM_SPEC = pl.BlockSpec(memory_space=pltpu.SMEM)
KERNEL_VMEM = 16 << 20
CORE, SEQ, LENGTH, BATCH, MP = range(5)


def pair(values):
    high = values.astype(BF16)
    return high, (values - high.astype(F32)).astype(BF16)


def dot(a, b, dims):
    return lax.dot_general(a, b, (dims, ((), ())), preferred_element_type=F32)


def mm3(a, b, dims=NN):
    rows = a[0].shape[0]
    if dims != TN and rows <= 128:
        both = dot(jnp.concatenate(a, axis=0), b[0], dims)
        return both[:rows] + (both[rows:] + dot(a[0], b[1], dims))
    return dot(a[0], b[0], dims) + (dot(a[0], b[1], dims) + dot(a[1], b[0], dims))


def load(refs):
    return refs[0][...], refs[1][...]


def mean_of(values):
    return jnp.sum(values, axis=-1, keepdims=True) * (1.0 / values.shape[-1])


def sum_rows(values):
    return jnp.sum(values, axis=0, keepdims=True)


def norm_forward(inputs, gain_row, bias_row):
    centre = inputs - mean_of(inputs)
    inverse = lax.rsqrt(mean_of(centre * centre) + EPS)
    normed = centre * inverse
    return normed * gain_row + bias_row, normed, inverse


def norm_backward(upstream, normed, inverse, gain_row):
    scaled = upstream * gain_row
    return inverse * (scaled - mean_of(scaled) - normed * mean_of(scaled * normed))


def gelu_both(inputs):
    cdf = 0.5 * (1.0 + lax.erf(inputs * (1.0 / math.sqrt(2.0))))
    density = jnp.exp(-0.5 * inputs * inputs) * (1.0 / math.sqrt(2.0 * math.pi))
    return inputs * cdf, cdf + inputs * density


def in_order(core, own, other):
    return jnp.concatenate(
        [jnp.where(core == 0, own, other), jnp.where(core == 0, other, own)], axis=0
    )


def sum_refs(refs):
    total = refs[0][...]
    for ref in refs[1:]:
        total = total + ref[...]
    return total


def head(values, index):
    return values[:, index * HD : (index + 1) * HD]


def half_of(ref, core):
    half = ref.shape[0] // 2
    return ref[pl.ds(pl.multiple_of(core * half, half), half), :]


def split_kernel(*refs):
    count = len(refs) // 3
    for index in range(count):
        high, low = pair(refs[index][...])
        refs[count + 2 * index][...] = high
        refs[count + 2 * index + 1][...] = low


def turn_weights_kernel(*refs):
    count = len(refs) // 2
    for source, target in zip(refs[:count], refs[count:]):
        target[...] = source[...].T


def start_kernel(scal, text, memory, attn_in, rows0, rows1, high, low, k0, v0):
    text_dev = text.shape[0]
    mem_dev = memory.shape[0]
    rows0[0:text_dev] = text[:, 0, :]
    for index in range(2 * mem_dev):
        rows0[text_dev + index : text_dev + index + 1] = memory[index % mem_dev]
    rows1[-SMALL:] = jnp.zeros((SMALL, rows1.shape[1]), F32)
    rows1[0:text_dev] = text[:, 1, :]
    right = pair(rows0[...])
    for part, target in ((1, k0), (2, v0), (0, None)):
        left = pair(attn_in[part])
        high[part], low[part] = left
        if target is not None:
            target[...] = mm3(left, right, NT)


def query_kernel(rows, high, low, q):
    q[...] = mm3(pair(rows[...]), (high[0], low[0]), NT)


def project_kernel(rows1, high, low, q1, kv1):
    cols = q1.shape[1]
    rows = pair(rows1[...])
    q1[...] = mm3(rows, (high[0], low[0]), NT)
    for part in (1, 2):
        kv1[(part - 1) * cols : part * cols] = mm3((high[part], low[part]), rows, NT)


def upstream_kernel(scal, out_grad, mlm, up0, up1):
    text_dev = out_grad.shape[0]
    row = lax.broadcasted_iota(jnp.int32, (text_dev, text_dev), 0)
    column = lax.broadcasted_iota(jnp.int32, (text_dev, text_dev), 1)
    position = lax.broadcasted_iota(jnp.int32, (text_dev, 1), 0)
    for segment, up in enumerate((up0, up1)):
        flags = mlm[segment : segment + 1].astype(F32)
        weight = jnp.sum(jnp.where(row == column, flags, 0.0), axis=1, keepdims=True)
        if segment == 1:
            weight = jnp.where(scal[SEQ] * text_dev + position < scal[LENGTH], weight, 0.0)
        up[-SMALL:] = jnp.zeros((SMALL, up.shape[1]), F32)
        up[0:text_dev] = out_grad[:, segment, :] * weight


def head_rows(values, index):
    return values[index * HD : (index + 1) * HD]


def attend_probs(scal, query, keys_own, keys_oth, masked, text_dev, probs):
    rows_dev = query.shape[0]
    if masked:
        place = lax.broadcasted_iota(jnp.int32, (1, 2 * rows_dev), 1)
        shard = jnp.where(place < rows_dev, scal[SEQ], 1 - scal[SEQ])
        inside = jnp.where(place < rows_dev, place, place - rows_dev)
        valid = (inside >= text_dev) | (shard * text_dev + inside < scal[LENGTH])
    keys = jnp.concatenate([keys_own, keys_oth], axis=1)
    for index in range(query.shape[1] // HD):
        scores = mm3(pair(head(query, index)), pair(head_rows(keys, index))) * SCALE
        if masked:
            scores = jnp.where(valid, scores, NEG)
        expo = jnp.exp(scores - jnp.max(scores, axis=-1, keepdims=True))
        probs[index] = expo * (1.0 / jnp.sum(expo, axis=-1, keepdims=True))


def attend_values(probs, values_own, values_oth, context):
    values = jnp.concatenate([values_own, values_oth], axis=1)
    for index in range(probs.shape[0]):
        term = mm3(pair(probs[index]), pair(head_rows(values, index)), NT)
        context[:, index * HD : (index + 1) * HD] = term


def attend_first_kernel(q, k_own, k_oth, probs):
    attend_probs(None, q[...], k_own[...], k_oth[...], False, 0, probs)


def attend_next_kernel(scal, probs, v_own, v_oth, wh, wl, context, give, tail):
    attend_values(probs, v_own[...], v_oth[...], context)
    give[...] = half_of(context, 1 - scal[CORE])
    tail[...] = mm3(pair(context[-SMALL:]), (wh[...], wl[...]))


def attend_last_kernel(
    text_dev, scal, q, q_tail, kv_own, kv_oth, own_tail, oth_tail,
    context, probs, give, q_full, k_own, k_oth, v_own, v_oth, rows,
):
    first = q.shape[0] - SMALL
    q_full[0:first] = q[0:first]
    q_full[first:] = q_tail[...]
    lanes = rows.shape[0]
    place = lax.broadcasted_iota(jnp.int32, (1, lanes), 1)
    rows[...] = jnp.zeros(rows.shape, F32)
    cols = q.shape[1]
    for keys, values, body, tail in (
        (k_own, v_own, kv_own, own_tail),
        (k_oth, v_oth, kv_oth, oth_tail),
    ):
        rows[-SMALL:] = tail[...]
        last = jnp.where(place < lanes - SMALL, body[:, -lanes:], rows[...].T)
        for full, some in ((keys, slice(0, cols)), (values, slice(cols, 2 * cols))):
            full[:, 0:-lanes] = body[some, 0:-lanes]
            full[:, -lanes:] = last[some]
    attend_probs(scal, q_full[...], k_own[...], k_oth[...], True, text_dev, probs)
    attend_values(probs, v_own[...], v_oth[...], context)
    give[...] = half_of(context, 1 - scal[CORE])


def attend_out_kernel(scal, context, got, wh, wl, sh, sl, partial):
    own = mm3(pair(half_of(context, scal[CORE])), (wh[...], wl[...]))
    partial[...] = own + mm3(pair(got[...]), (sh[...], sl[...]))


def feed_rows(hidden, weights, act_own, act_sib, slope_own, slope_sib):
    left = pair(hidden)
    total = None
    for (ih, il, oh, ol), act, slope in (
        (weights[:4], act_own, slope_own),
        (weights[4:], act_sib, slope_sib),
    ):
        value, grad = gelu_both(mm3(left, load((ih, il))))
        act[...] = value
        slope[...] = grad
        term = mm3(pair(value), load((oh, ol)))
        total = term if total is None else total + term
    return total


def feed_tail_kernel(rows, p0, p1, p2, p3, gains, biases, *refs):
    weights, (hidden, normed, inverse, *others, partial) = refs[:8], refs[8:]
    attended = sum_refs((p0, p1, p2, p3))
    value, unit, scale = norm_forward(rows[-SMALL:] + attended, gains[0:1], biases[0:1])
    hidden[...] = value
    normed[...] = unit
    inverse[...] = scale
    partial[...] = feed_rows(value, weights, *others)


def link_tail_kernel(
    text_dev, hidden, own, oth, gains, biases, rows, high, low, first,
    rows_full, q_tail, kv_tail, normed, inverse, first_next,
):
    first_next[...] = first[...]
    mixed = own[...] + oth[...]
    result, unit, scale = norm_forward(hidden[...] + mixed, gains[1:2], biases[1:2])
    normed[...] = unit
    inverse[...] = scale
    head_rows = rows.shape[0] - SMALL
    place = lax.broadcasted_iota(jnp.int32, (SMALL, 1), 0)
    tail = jnp.where(place < text_dev - head_rows, rows[-SMALL:], result)
    rows_full[0:head_rows] = rows[0:head_rows]
    rows_full[head_rows:] = tail
    left = pair(tail)
    cols = q_tail.shape[1]
    q_tail[...] = mm3(left, (high[0], low[0]), NT)
    kv_tail[:, 0:cols] = mm3(left, (high[1], low[1]), NT)
    kv_tail[:, cols:] = mm3(left, (high[2], low[2]), NT)


def feed_kernel(scal, rows, own, oth, gains, biases, *refs):
    weights, (hidden, normed, inverse, *others, partial) = refs[:8], refs[8:]
    inputs = half_of(rows, scal[CORE]) + (own[...] + oth[...])
    value, unit, scale = norm_forward(inputs, gains[0:1], biases[0:1])
    hidden[...] = value
    normed[...] = unit
    inverse[...] = scale
    partial[...] = feed_rows(value, weights, *others)


def feed_rows_back(grad_two, weights, slope_own, slope_sib, back_own, back_sib):
    left = pair(grad_two)
    total = None
    for (ih, il, oh, ol), slope, back in (
        (weights[:4], slope_own, back_own),
        (weights[4:], slope_sib, back_sib),
    ):
        grad = mm3(left, load((oh, ol))) * slope[...]
        back[...] = grad
        term = mm3(pair(grad), load((ih, il)))
        total = term if total is None else total + term
    return total


def feed_back_kernel(scal, hidden, own, oth, gains, biases, upstream, slope_own, slope_sib, *refs):
    weights, (outcome, pre_two, two_first, two_second, back_own, give, give_more, *others) = (
        refs[:8],
        refs[8:],
    )
    sums, partial, back_sib = others
    mixed = own[...] + oth[...]
    result, unit, scale = norm_forward(hidden[...] + mixed, gains[1:2], biases[1:2])
    outcome[...] = result
    back = half_of(upstream, scal[CORE])
    sums[0:1] = sum_rows(back * unit)
    sums[1:2] = sum_rows(back)
    grad_two = norm_backward(back, unit, scale, gains[1:2])
    pre_two[...] = grad_two
    partial[...] = feed_rows_back(grad_two, weights, slope_own, slope_sib, back_own, back_sib)
    first = give.shape[1]
    two_first[...] = grad_two[:, 0:first]
    two_second[...] = grad_two[:, first:]
    give[...] = back_sib[:, 0:first]
    give_more[:, 0:first] = back_sib[:, first:]
    give_more[:, first:] = result


def context_back_kernel(
    pre_two, own, oth, normed, inverse, gains, wh, wl, sh, sl, pre_one, sums, back_own, give
):
    hidden_back = pre_two[...] + (own[...] + oth[...])
    unit = normed[...]
    sums[0:1] = sum_rows(hidden_back * unit)
    sums[1:2] = sum_rows(hidden_back)
    grad_one = norm_backward(hidden_back, unit, inverse[...], gains[0:1])
    pre_one[...] = grad_one
    left = pair(grad_one)
    back_own[...] = mm3(left, (wh[...], wl[...]), NT)
    give[...] = mm3(left, (sh[...], sl[...]), NT)


def heads_back(context_back, context, prob_of, query, keys, values, query_back, kv_back):
    product = context_back * context
    cols = query.shape[1]
    for index in range(cols // HD):
        key = pair(head_rows(keys, index))
        value = pair(head_rows(values, index))
        back = pair(head(context_back, index))
        delta = jnp.sum(head(product, index), axis=-1, keepdims=True)
        prob = prob_of(index)
        score_back = prob * (mm3(back, value) - delta) * SCALE
        score_back = pair(score_back)
        query_back[:, index * HD : (index + 1) * HD] = mm3(score_back, key, NT)
        kv_back[index * HD : (index + 1) * HD] = mm3(pair(head(query, index)), score_back, TN)
        kv_back[cols + index * HD : cols + (index + 1) * HD] = mm3(back, pair(prob), TN)


def attend_back_kernel(
    scal, back_own, back_got, context, probs, q, k_own, k_oth, v_own, v_oth,
    q_back, own_back, give_back, own_tail, give_tail, kv_back,
):
    context_back = in_order(scal[CORE], back_own[...], back_got[...])
    heads_back(
        context_back,
        context[...],
        lambda index: probs[index],
        q[...],
        jnp.concatenate([k_own[...], k_oth[...]], axis=1),
        jnp.concatenate([v_own[...], v_oth[...]], axis=1),
        q_back,
        kv_back,
    )
    rows_dev = q.shape[0]
    own_back[...] = kv_back[:, 0:rows_dev]
    give_back[...] = kv_back[:, rows_dev:]
    own_tail[...] = kv_back[:, rows_dev - 128 : rows_dev].T[-SMALL:]
    give_tail[...] = kv_back[:, 2 * rows_dev - 128 : 2 * rows_dev].T[-SMALL:]


def project_back(query_back, kv_back, high, low):
    cols = query_back.shape[1]
    total = mm3(pair(query_back), (high[0], low[0]))
    total = total + mm3(pair(kv_back[:, 0:cols]), (high[1], low[1]))
    return total + mm3(pair(kv_back[:, cols:]), (high[2], low[2]))


def rows_tail_kernel(
    scal, q_back, own_tail, got_tail, high, low, pre_one, give_back, partial, give_next
):
    total = project_back(q_back[-SMALL:], own_tail[...] + got_tail[...], high, low)
    partial[...] = total + jnp.where(scal[MP] == 1, pre_one[-SMALL:], 0.0)
    give_next[...] = give_back[...]


def feed_back_tail_kernel(
    mem_dev, p0, p1, p2, p3, normed, inverse, gains, slope_own, slope_sib, hidden, act, *refs
):
    weights, (pre_two, back_own, partial, sums, bundle, back_sib, back) = refs[:8], refs[8:]
    rows_back = sum_refs((p0, p1, p2, p3))
    first = SMALL - mem_dev
    back[0:first] = jnp.zeros((first, back.shape[1]), F32)
    back[first:] = rows_back[first - mem_dev : first] + rows_back[first:]
    upstream = back[...]
    unit = normed[...]
    sums[0:1] = sum_rows(upstream * unit)
    sums[1:2] = sum_rows(upstream)
    grad_two = norm_backward(upstream, unit, inverse[...], gains[1:2])
    pre_two[...] = grad_two
    partial[...] = feed_rows_back(grad_two, weights, slope_own, slope_sib, back_own, back_sib)
    bundle[0:8] = hidden[8:]
    bundle[8:16] = back_own[8:]
    bundle[16:24] = pre_two[8:]
    bundle[24:32] = act[8:]


def attend_back_tail_kernel(
    scal, pre_two, own, oth, normed, inverse, gains, context, probs, q, k_own, k_oth, v_own, v_oth, wh, wl,
    q_back, own_back, give_back, sums_one0, sums_one1, sums_two0, sums_two1, sums_two_tail,
    pre_one, sums, q_back_all, own_back_all, give_back_all, q_tail, kv_back,
):
    hidden_back = pre_two[...] + (own[...] + oth[...])
    unit = normed[...]
    one = sums_one0[...] + sums_one1[...]
    two = sums_two0[...] + sums_two1[...]
    once = jnp.where(scal[CORE] == 0, 1.0, 0.0)
    two = two + once * sums_two_tail[...]
    sums[0:1] = one[0:1] + once * sum_rows(hidden_back * unit)
    sums[1:2] = two[0:1]
    sums[2:3] = one[1:2] + once * sum_rows(hidden_back)
    sums[3:4] = two[1:2]
    sums[4:] = jnp.zeros((4, sums.shape[1]), F32)
    grad_one = norm_backward(hidden_back, unit, inverse[...], gains[0:1])
    pre_one[...] = grad_one
    context_back = mm3(pair(grad_one), (wh[...], wl[...]), NT)
    heads_back(
        context_back,
        context[-SMALL:],
        lambda index: probs[index, -SMALL:],
        q[-SMALL:],
        jnp.concatenate([k_own[...], k_oth[...]], axis=1),
        jnp.concatenate([v_own[...], v_oth[...]], axis=1),
        q_tail,
        kv_back,
    )
    first = q.shape[0] - SMALL
    q_back_all[0:first] = q_back[0:first]
    q_back_all[first:] = q_back[first:] + q_tail[...]
    rows_dev = q.shape[0]
    own_back_all[...] = own_back[...] + kv_back[:, 0:rows_dev]
    keys = kv_back.shape[0]
    give_back_all[0:keys] = give_back[...] + kv_back[:, rows_dev:]
    for part in range(sums.shape[1] // rows_dev):
        place = slice(part * rows_dev, (part + 1) * rows_dev)
        give_back_all[keys + 8 * part : keys + 8 * part + 8] = sums[:, place]


def turn_back_kernel(own_back, got_back, *refs):
    rows, width = own_back.shape
    if len(refs) > 1:
        own_sums, kv_back, sums = refs
        for part in range(sums.shape[1] // width):
            place = slice(part * width, (part + 1) * width)
            sums[:, place] = own_sums[:, place] + got_back[rows + 8 * part : rows + 8 * part + 8]
    else:
        (kv_back,) = refs
    kv_back[...] = (own_back[...] + got_back[0:rows]).T


def rows_kernel(scal, q_back, kv_back, high, low, *refs):
    *sums, keep, give = refs
    half = keep.shape[0]
    total = project_back(q_back[...], kv_back[...], high, low)
    first, second = total[0:half], total[half:]
    own = scal[CORE] == 0
    keep[...] = jnp.where(own, first, second)
    give[0:half] = jnp.where(own, second, first)
    if sums:
        give[half:] = sums[0][...]


def join_kernel(keep, got, out):
    out[...] = keep[...] + got[0 : keep.shape[0]]


def end_rows_kernel(scal, one0, own0, oth0, tail, one1, own1, oth1, out0, out1):
    first = one0[...] + (own0[...] + oth0[...])
    out0[...] = first
    out0[-SMALL:] = first[-SMALL:] + jnp.where(scal[CORE] == 1, tail[...], 0.0)
    out1[...] = one1[...] + (own1[...] + oth1[...])


def end_text(core, own0, oth0, own1, oth1, memory, text, last):
    text_dev = text.shape[0]
    text[:, 0, :] = in_order(core, own0, oth0)[0:text_dev]
    text[:, 1, :] = in_order(core, own1, oth1)[0:text_dev]
    for index in range(last.shape[0]):
        last[index] = memory[index : index + 1]


def end_text_kernel(scal, own0, got0, own1, got1, text, last):
    core = scal[CORE]
    first = got0.shape[1] - own0.shape[1]
    memory = jnp.where(core == 1, own1[-SMALL:], got1[-SMALL:, first:])
    memory = memory[SMALL - last.shape[0] :]
    end_text(core, own0[...], got0[:, first:], own1[...], got1[:, first:], memory, text, last)


def end_grad_kernel(scal, own0, got0, own1, got1, text, last):
    core = scal[CORE]
    mem_dev = last.shape[0]
    memory = jnp.where(core == 1, own0[-SMALL:], got0[-SMALL:])[SMALL - 2 * mem_dev :]
    memory = memory[0:mem_dev] + memory[mem_dev:]
    end_text(core, own0[...], got0[...], own1[...], got1[...], memory, text, last)


def block_at(scal, slot):
    return jnp.bitwise_xor(scal[BATCH], slot)


def stacked(*refs):
    return jnp.concatenate([ref[...] for ref in refs], axis=0)


def put_chunks(product, scal, batch_count, chunk, outs):
    for part in range(len(outs) // 2):
        keep, give = outs[2 * part], outs[2 * part + 1]
        width = keep.shape[2]
        columns = slice(part * width, (part + 1) * width)
        for slot in range(batch_count):
            block = 2 * block_at(scal, slot)
            mine = pl.multiple_of((block + scal[SEQ]) * chunk, chunk)
            others = pl.multiple_of((block + 1 - scal[SEQ]) * chunk, chunk)
            keep[slot] = product[pl.ds(mine, chunk), columns]
            give[slot * chunk : (slot + 1) * chunk] = product[pl.ds(others, chunk), columns]


def feed_in_kernel(columns, batch_count, chunk, scal, *refs):
    lefts, rights, *more, keep, give, product = refs[0:4], refs[4:8], *refs[8:]
    given = slice(0, columns.stop - columns.start)
    rights = [ref.at[:, columns if place % 2 == 0 else given] for place, ref in enumerate(rights)]
    product[...] = mm3(pair(stacked(*lefts)), pair(stacked(*rights)), TN)
    if batch_count != 4:
        keep[...] = product[...]
        return
    put_chunks(product, scal, batch_count, chunk, (keep, give))
    if more:
        put_folded(give, batch_count * chunk, more[0][...])


def feed_out_kernel(batch_count, chunk, scal, *refs):
    lefts, rights, outs, product = refs[0:6], refs[6:10], refs[10:-1], refs[-1]
    lefts = [
        lefts[0][...],
        jnp.concatenate([lefts[1][...], lefts[2][...]], axis=1),
        lefts[3][...],
        jnp.concatenate([lefts[4][...], lefts[5][...]], axis=1),
    ]
    lefts = jnp.concatenate(lefts, axis=0)
    product[...] = mm3(pair(lefts), pair(stacked(*rights)), TN)
    if batch_count != 4:
        outs[0][...] = product[...]
        return
    for slot in range(batch_count):
        block = 2 * block_at(scal, slot)
        mine = pl.multiple_of((block + scal[SEQ]) * chunk, chunk)
        others = pl.multiple_of((block + 1 - scal[SEQ]) * chunk, chunk)
        outs[slot % 2][slot // 2, 0:chunk] = product[pl.ds(mine, chunk), :]
        outs[slot % 2][slot // 2, chunk:] = product[pl.ds(others, chunk), :]


def attend_weights_kernel(
    batch_count, chunk, scal, rows0, rows1, q0, q1, kv0, kv1,
    one0, got0, tail, one1, got1, c0, c1, *refs,
):
    *outs, product = refs
    core = scal[CORE]
    rows = pair(stacked(rows0, rows1))
    cols = q0.shape[1]
    product[:, 0:cols] = mm3(rows, pair(stacked(q0, q1)), TN)
    product[:, cols : 3 * cols] = mm3(rows, pair(stacked(kv0, kv1)), TN)
    first = in_order(core, one0[...], got0[...])
    second = in_order(core, one1[...], got1[...])
    head_rows = first.shape[0] - SMALL
    ones = jnp.concatenate(
        [first[0:head_rows], first[head_rows:] + tail[...], second], axis=0
    )
    product[:, 3 * cols :] = mm3(pair(ones), pair(stacked(c0, c1)), TN)
    if batch_count != 4:
        outs[0][...] = product[...]
        return
    put_chunks(product, scal, batch_count, chunk, outs)


def turn_seq_kernel(*refs):
    *terms, keep_next, give_next = refs
    chunk = terms[0].shape[1]
    first = 0
    for keep, got in zip(terms[0::2], terms[1::2]):
        place = slice(first, first + keep.shape[2])
        first += keep.shape[2]
        for slot in range(keep.shape[0]):
            target = give_next if slot % 2 else keep_next
            total = keep[slot] + got[slot * chunk : (slot + 1) * chunk]
            target[slot // 2, :, place] = total


def turn_batch_kernel(keep, got, keep_next, give_next):
    keep_next[...] = keep[0] + got[0]
    give_next[...] = keep[1] + got[1]


def turn_place_kernel(keep, got, keep_next, give_next):
    total = keep[...] + got[...]
    chunk = keep_next.shape[0]
    keep_next[...] = total[0:chunk]
    give_next[...] = total[chunk:]


def pick(values, blocks, chunk, index):
    picked = values[:, 0:chunk]
    for block in range(1, blocks):
        picked = jnp.where(index == block, values[:, block * chunk : (block + 1) * chunk], picked)
    return picked


def put_bundle(piece, sources, batch_count, chunk, mem_dev, index):
    first = 8 - mem_dev
    piece[...] = jnp.zeros(piece.shape, F32)
    for source in range(2):
        for kind in range(2):
            slot = 2 * source + kind
            left = sources[source][16 * kind : 16 * kind + 8]
            right = sources[source][16 * kind + 8 : 16 * kind + 16]
            left = pick(left, 2 * batch_count, chunk, index)
            piece[slot * mem_dev : (slot + 1) * mem_dev] = right[first:]
            row = 4 * mem_dev + slot
            for place in range(mem_dev):
                piece[row : row + 1, 128 * place : 128 * place + chunk] = left[
                    first + place : first + place + 1
                ]


def put_folded(target, first, values):
    rows, width = values.shape
    part = target.shape[1]
    for place in range(width // part):
        target[first : first + rows] = values[:, place * part : (place + 1) * part]
        first += rows


def get_folded(source, first, rows, width):
    places = range(width // source.shape[1])
    return jnp.concatenate(
        [source[first + place * rows : first + (place + 1) * rows] for place in places], axis=1
    )


def turn_in_kernel(batch_count, chunk, mem_dev, scal, *refs):
    *terms, bundle, keep_next, give_next, own, nearest, other, last = refs
    first = 0
    for keep, got in zip(terms[0::2], terms[1::2]):
        place = slice(first, first + keep.shape[2])
        first += keep.shape[2]
        for slot in range(keep.shape[0]):
            total = keep[slot] + got[slot * chunk : (slot + 1) * chunk]
            if slot % 2:
                give_next[slot // 2 * chunk : (slot // 2 + 1) * chunk, place] = total
            else:
                keep_next[slot // 2, :, place] = total
    sources = (bundle[...], get_folded(terms[-1], batch_count * chunk, *bundle.shape))
    pieces = (own, nearest, other, last)
    for slot in range(batch_count):
        index = 2 * block_at(scal, slot) + scal[SEQ]
        put_bundle(pieces[slot], sources, batch_count, chunk, mem_dev, index)
    rows = 4 * mem_dev
    give_next[2 * chunk : 2 * chunk + 24] = nearest[...]
    give_next[2 * chunk + 24 : 2 * chunk + 28] = last[rows : rows + 4]
    give_next[2 * chunk + 28 :] = jnp.zeros((4, first), F32)


def next_in_kernel(chunk, mem_dev, keep, got, other, keep_next, give_next, bundle):
    keep_next[...] = keep[0] + got[0:chunk]
    give_next[0:chunk] = keep[1] + got[chunk : 2 * chunk]
    rows = 4 * mem_dev
    row = 2 * chunk
    bundle[...] = got[row : row + 24]
    give_next[chunk : chunk + 24] = other[...]
    give_next[chunk + 24 : chunk + 24 + rows] = got[row : row + rows]
    give_next[chunk + 24 + rows :] = got[row + 24 : row + 28]


def turn_first_kernel(keep, got, sums, got_give, keep_next, give_next, norms):
    chunk = keep.shape[1]
    for slot in range(keep.shape[0]):
        total = keep[slot] + got[slot * chunk : (slot + 1) * chunk]
        if slot % 2:
            give_next[slot // 2 * chunk : (slot // 2 + 1) * chunk] = total
        else:
            keep_next[slot // 2] = total
    norms[...] = sums[...] + got_give[-8:]
    put_folded(give_next, 2 * chunk, norms[...])


def next_first_kernel(keep, got, norms, keep_next, give_next, norms_next):
    chunk = keep_next.shape[0]
    keep_next[...] = keep[0] + got[0:chunk]
    give_next[0:chunk] = keep[1] + got[chunk : 2 * chunk]
    norms_next[...] = norms[...] + get_folded(got, 2 * chunk, *norms.shape)
    put_folded(give_next, chunk, norms_next[...])


def end_norms_kernel(scal, got, norms, gains, biases):
    chunk = gains.shape[1]
    total = norms[...] + get_folded(got, chunk, *norms.shape)
    first = (scal[BATCH] * 2 + scal[SEQ]) * chunk
    picked = pltpu.roll(total, total.shape[1] - first, 1)[:, 0:chunk]
    gains[...] = picked[0:2]
    biases[...] = picked[2:4]


def bundle_product(kind, mem_dev, bundles, left, right):
    chunk = left.shape[1]
    left[...] = jnp.zeros(left.shape, F32)
    right[...] = jnp.zeros(right.shape, F32)
    for number, bundle in enumerate(bundles):
        for source in range(2):
            slot = 2 * source + kind
            base = 8 * (2 * number + source)
            right[base : base + mem_dev] = bundle[slot * mem_dev : (slot + 1) * mem_dev]
            row = 4 * mem_dev + slot
            for place in range(mem_dev):
                left[base + place : base + place + 1] = bundle[
                    row : row + 1, 128 * place : 128 * place + chunk
                ]
    return mm3(pair(left[...]), pair(right[...]), TN)


def end_out_kernel(mem_dev, keep, got, bundle0, bundle1, others, out, left, right):
    bundles = (bundle0, bundle1, others.at[out.shape[0] : out.shape[0] + 24], others.at[out.shape[0] + 24 :])
    extra = bundle_product(1, mem_dev, bundles, left, right)
    out[...] = keep[...] + got[...] + extra


def end_in_kernel(mem_dev, keep, got, bundle0, bundle1, out, left, right):
    chunk = out.shape[0]
    bundles = (bundle0, bundle1, got.at[chunk : chunk + 24], got.at[chunk + 24 :])
    out[...] = keep[...] + got[0:chunk] + bundle_product(0, mem_dev, bundles, left, right)


def end_attend_kernel(*refs):
    *terms, grad_in, grad_out = refs
    chunk = grad_in.shape[1]
    parts = [keep[...] + got[0:chunk] for keep, got in zip(terms[0::2], terms[1::2])]
    total = jnp.concatenate(parts, axis=1)
    cols = grad_in.shape[2]
    for part in range(3):
        grad_in[part] = total[:, part * cols : (part + 1) * cols]
    grad_out[...] = total[:, 3 * cols :].T


def shape(*dims, dtype=F32):
    return jax.ShapeDtypeStruct(dims, dtype)


class Order:
    def __init__(self, scal):
        self.scal = scal
        self.last = None
        self.extra = []
        self.name = None
        self.cost = 0.0

    def wait(self, *values):
        self.extra += values

    def call(self, kernel, outs, *args, scal=False, scratch=()):
        after = [] if self.last is None else [self.last]
        after += self.extra
        self.extra = []
        count = len(args) + scal
        skip = len(after)

        def body(*refs):
            kernel(*refs[:count], *refs[count + skip :])

        ins = [SMEM_SPEC] * scal + [VMEM_SPEC] * len(args)
        ins += [pl.BlockSpec(memory_space=pl.ANY)] * skip
        result = pl.pallas_call(
            body,
            out_shape=outs,
            in_specs=ins,
            out_specs=jax.tree.map(lambda _: VMEM_SPEC, outs),
            scratch_shapes=list(scratch),
            compiler_params=pltpu.CompilerParams(vmem_limit_bytes=KERNEL_VMEM),
            cost_estimate=pl.CostEstimate(
                flops=int(self.cost * 10**9), bytes_accessed=0, transcendentals=0
            ),
            name=self.name,
        )(*([self.scal] if scal else []), *args, *after)
        self.last = min(jax.tree.leaves(result), key=lambda value: value.size)
        return result


def swap_seq(values):
    return lax.ppermute(values, "seq", SEQ_SWAP)


def to_core(values):
    return lax.ppermute(values, "mp", CORE_SWAP)


def to_chip(values):
    return lax.ppermute(values, "mp", CHIP_SWAP)


def spread_mp(values):
    return values, to_core(values), to_chip(values), lax.ppermute(values, "mp", CROSS_SWAP)


def swap_batch(values, bit):
    count = lax.axis_size("batch")
    return lax.ppermute(values, "batch", [(place, place ^ bit) for place in range(count)])


def local(
    text_rows,
    memory_in,
    text_length,
    mlm_mask,
    out_grad,
    attn_in,
    attn_out,
    ffn_in,
    ffn_out,
    norm_gains,
    norm_biases,
):
    seg_count, text_dev, width = text_rows.shape[1:]
    mem_dev = memory_in.shape[1]
    cols = attn_in.shape[2]
    units = ffn_in.shape[1]
    heads = cols // HD
    batch_count = lax.axis_size("batch")
    seq_count = lax.axis_size("seq")
    rows_dev = text_dev + 2 * mem_dev
    half = rows_dev // 2
    most = units // 2
    chunk = width // (batch_count * seq_count)
    text_rows = text_rows.reshape(seg_count, text_dev, width).transpose(1, 0, 2)
    out_grad = out_grad.reshape(seg_count, text_dev, width).transpose(1, 0, 2)
    memory_in = memory_in.transpose(1, 0, 2)
    mlm_mask = mlm_mask.reshape(seg_count, text_dev)
    attn_in = attn_in.transpose(0, 2, 1)
    scal = jnp.stack(
        [
            lax.axis_index("mp") % 2,
            lax.axis_index("seq"),
            text_length[0],
            lax.axis_index("batch"),
            lax.axis_index("mp"),
        ]
    ).astype(jnp.int32)

    whole = shape(rows_dev, width)
    part = shape(half, width)
    tail_shape = shape(SMALL, width)
    row_sums = shape(2, width)
    order = Order(scal)
    call = order.call

    v = types.SimpleNamespace()
    in_pair = [shape(3, cols, width, dtype=BF16)] * 2
    out_pair = [shape(cols, width, dtype=BF16)] * 2
    feed_pairs = [shape(width, units, dtype=BF16)] * 2 + [shape(units, width, dtype=BF16)] * 2
    turned_pairs = [shape(units, width, dtype=BF16)] * 2 + [shape(width, units, dtype=BF16)] * 2
    attended = [shape(rows_dev, cols), shape(heads, rows_dev, seq_count * rows_dev)]
    attended += [shape(half, cols)]
    text_shape = [shape(text_dev, seg_count, width), shape(mem_dev, 1, width)]
    factors = [pltpu.VMEM((64, chunk), F32), pltpu.VMEM((64, units), F32)]
    folded = 8 * width // (2 * cols)
    halving = batch_count == 4

    def start():
        v.rows0, v.rows1_text, in_h, in_l, v.k0, v.v0 = call(
            start_kernel,
            [whole, whole] + in_pair + [shape(cols, rows_dev)] * 2,
            text_rows,
            memory_in,
            attn_in,
            scal=True,
        )
        v.in_w = (in_h, in_l)
        v.k0_oth, v.v0_oth = swap_seq(v.k0), swap_seq(v.v0)

    def query0():
        v.q0 = call(query_kernel, shape(rows_dev, cols), v.rows0, *v.in_w)

    def project():
        v.q1_text, v.kv1_text = call(
            project_kernel,
            [shape(rows_dev, cols), shape(2 * cols, rows_dev)],
            v.rows1_text,
            *v.in_w,
        )
        v.kv1_oth = swap_seq(v.kv1_text)

    def split_out():
        v.out_w = call(split_kernel, out_pair, attn_out)

    def split_feed():
        v.feed_own = call(split_kernel, feed_pairs, ffn_in, ffn_out)

    def split_feed_sib():
        v.feed_sib = call(
            split_kernel, feed_pairs, to_core(ffn_in), to_core(ffn_out)
        )

    def split_out_sib():
        v.out_sib = call(split_kernel, out_pair, to_core(attn_out))

    def turn_weights():
        v.feed_turned = call(
            turn_weights_kernel, turned_pairs * 2, *v.feed_own, *v.feed_sib
        )

    def make_upstream():
        v.upstream = call(
            upstream_kernel, [whole] * 2, out_grad, mlm_mask, scal=True
        )

    def probs0():
        v.probs0 = call(
            attend_first_kernel,
            shape(heads, rows_dev, seq_count * rows_dev),
            v.q0,
            v.k0,
            v.k0_oth,
        )

    def attend0():
        v.c0, give, tail = call(
            attend_next_kernel,
            [shape(rows_dev, cols), shape(half, cols), tail_shape],
            v.probs0,
            v.v0,
            v.v0_oth,
            *v.out_w,
            scal=True,
        )
        v.tails_one = spread_mp(tail)
        v.got_c0 = to_core(give)

    def feed_tail():
        v.hidden_tail, v.unit_one, v.scale_one, v.act_tail, _, *v.slopes_tail, v.tail_two = call(
            feed_tail_kernel,
            [tail_shape, tail_shape, shape(SMALL, 1)] + [shape(SMALL, units)] * 4 + [tail_shape],
            v.rows0,
            *v.tails_one,
            norm_gains,
            norm_biases,
            *v.feed_own,
            *v.feed_sib,
        )
        v.tail_two_oth = to_chip(v.tail_two)

    def attend_out0():
        v.own_first = call(
            attend_out_kernel,
            part,
            v.c0,
            v.got_c0,
            *v.out_w,
            *v.out_sib,
            scal=True,
        )

    def link_tail():
        v.rows1, v.q_tail, v.kv_tail, v.unit_two, v.scale_two, v.own_one0 = call(
            functools.partial(link_tail_kernel, text_dev),
            [whole, shape(SMALL, cols), shape(SMALL, 2 * cols), tail_shape, shape(SMALL, 1), part],
            v.hidden_tail,
            v.tail_two,
            v.tail_two_oth,
            norm_gains,
            norm_biases,
            v.rows1_text,
            *v.in_w,
            v.own_first,
        )
        v.kv_tail_oth = swap_seq(v.kv_tail)
        v.oth_one0 = to_chip(v.own_one0)

    def attend1():
        v.c1, v.probs1, give, v.q1, *full = call(
            functools.partial(attend_last_kernel, text_dev),
            attended + [shape(rows_dev, cols)] + [shape(cols, rows_dev)] * 4,
            v.q1_text,
            v.q_tail,
            v.kv1_text,
            v.kv1_oth,
            v.kv_tail,
            v.kv_tail_oth,
            scal=True,
            scratch=[pltpu.VMEM((128, 2 * cols), F32)],
        )
        v.keys1, v.values1 = full[0:2], full[2:4]
        v.got_c1 = to_core(give)

    def attend_out1():
        v.own_one1 = call(
            attend_out_kernel,
            part,
            v.c1,
            v.got_c1,
            *v.out_w,
            *v.out_sib,
            scal=True,
        )
        v.oth_one1 = to_chip(v.own_one1)

    def feed(rows, own, oth):
        return call(
            feed_kernel,
            [part, part, shape(half, 1)] + [shape(half, units)] * 4 + [part],
            rows,
            own,
            oth,
            norm_gains,
            norm_biases,
            *v.feed_own,
            *v.feed_sib,
            scal=True,
        )

    def feed0():
        v.hidden0, v.normed0, v.inverse0, v.act0, give, *v.slopes0, v.own_two0 = feed(
            v.rows0, v.own_one0, v.oth_one0
        )
        v.oth_two0 = to_chip(v.own_two0)
        v.got_hidden0, v.got_act0 = to_core(v.hidden0), to_core(give)

    def feed1():
        v.hidden1, v.normed1, v.inverse1, v.act1, give, *v.slopes1, v.own_two1 = feed(
            v.rows1, v.own_one1, v.oth_one1
        )
        v.oth_two1 = to_chip(v.own_two1)
        v.got_hidden1, v.got_act1 = to_core(v.hidden1), to_core(give)

    def feed_back(hidden, own, oth, upstream, slopes):
        return call(
            feed_back_kernel,
            [part, part, shape(half, most), shape(half, width - most), shape(half, units)]
            + [shape(half, most), shape(half, units - most + width), row_sums, part],
            hidden,
            own,
            oth,
            norm_gains,
            norm_biases,
            upstream,
            *slopes,
            *v.feed_turned,
            scal=True,
            scratch=[pltpu.VMEM((half, units), F32)],
        )

    def feed_back0():
        v.text0, v.two0, *gives, v.sums_two0, v.own_three0 = feed_back(
            v.hidden0, v.own_two0, v.oth_two0, v.upstream[0], v.slopes0
        )
        v.oth_three0 = to_chip(v.own_three0)
        *two, v.back0, give, give_more = gives
        v.got_two0 = [to_core(some) for some in two]
        v.got_back0, v.got_more0 = to_core(give), to_core(give_more)

    def feed_back1():
        v.text1, v.two1, *gives, v.sums_two1, v.own_three1 = feed_back(
            v.hidden1, v.own_two1, v.oth_two1, v.upstream[1], v.slopes1
        )
        v.oth_three1 = to_chip(v.own_three1)
        *two, v.back1, give, give_more = gives
        v.got_two1 = [to_core(some) for some in two]
        v.got_back1, v.got_more1 = to_core(give), to_core(give_more)

    def weights(kernel, outs, arrays, columns):
        if not halving:
            outs = [shape(width, columns), shape(8, columns)]
        return call(
            functools.partial(kernel, batch_count, chunk),
            outs,
            *arrays,
            scal=True,
            scratch=[pltpu.VMEM((width, columns), F32)],
        )

    def feed_in(first, last, got0, got1, *more):
        rows = batch_count * chunk + len(more) * 32 * width // (last - first)
        keep, give = weights(
            functools.partial(feed_in_kernel, slice(first, last)),
            [shape(batch_count, chunk, last - first), shape(rows, last - first)],
            (v.hidden0, v.got_hidden0, v.hidden1, v.got_hidden1)
            + (v.back0, got0, v.back1, got1, *more),
            last - first,
        )
        return keep, swap_seq(give) if halving else None

    def feed_in0():
        v.in0, v.got_in0 = feed_in(0, most, v.got_back0, v.got_back1)

    def feed_in1():
        v.in1, v.got_in1 = feed_in(most, units, v.got_more0, v.got_more1, v.bundle)

    def feed_out():
        v.out_keep, give = weights(
            feed_out_kernel,
            [shape(2, 2 * chunk, units)] * 2,
            (v.two0, *v.got_two0, v.two1, *v.got_two1)
            + (v.act0, v.got_act0, v.act1, v.got_act1),
            units,
        )
        v.got_out = swap_batch(give, 1) if halving else None

    def context_back(pre_two, own, oth, normed, inverse):
        return call(
            context_back_kernel,
            [part, row_sums] + [shape(half, cols)] * 2,
            pre_two,
            own,
            oth,
            normed,
            inverse,
            norm_gains,
            *v.out_w,
            *v.out_sib,
        )

    def context_back0():
        v.one0, v.sums_one0, v.context_back0, give = context_back(
            v.two0, v.own_three0, v.oth_three0, v.normed0, v.inverse0
        )
        v.got_context0, v.got_one0 = to_core(give), to_core(v.one0)

    def context_back1():
        v.one1, v.sums_one1, v.context_back1, give = context_back(
            v.two1, v.own_three1, v.oth_three1, v.normed1, v.inverse1
        )
        v.got_context1, v.got_one1 = to_core(give), to_core(v.one1)

    def attend_back(own, got, context, probs, query, keys, values):
        return call(
            attend_back_kernel,
            [shape(rows_dev, cols)]
            + [shape(2 * cols, rows_dev)] * 2
            + [shape(SMALL, 2 * cols)] * 2,
            own,
            got,
            context,
            probs,
            query,
            *keys,
            *values,
            scal=True,
            scratch=[pltpu.VMEM((2 * cols, seq_count * rows_dev), F32)],
        )

    def attend_back0():
        v.qb0_text, v.kvo0_text, v.kvg0_text, _, _ = attend_back(
            v.context_back0,
            v.got_context0,
            v.c0,
            v.probs0,
            v.q0,
            (v.k0, v.k0_oth),
            (v.v0, v.v0_oth),
        )

    def attend_back1():
        v.qb1, v.kvo1, v.kvg1_first, v.own_tail, give = attend_back(
            v.context_back1,
            v.got_context1,
            v.c1,
            v.probs1,
            v.q1,
            v.keys1,
            v.values1,
        )
        v.got_tail = swap_seq(give)

    def rows_tail():
        tail, give = call(
            rows_tail_kernel,
            [tail_shape, shape(2 * cols, rows_dev)],
            v.qb1,
            v.own_tail,
            v.got_tail,
            *v.in_w,
            v.one1,
            v.kvg1_first,
            scal=True,
        )
        v.tails_four = spread_mp(tail)
        v.got1 = swap_seq(give)

    def feed_back_tail():
        v.two_tail, _, v.tail_three, v.sums_two_tail, v.bundle = call(
            functools.partial(feed_back_tail_kernel, mem_dev),
            [tail_shape, shape(SMALL, units), tail_shape, row_sums, shape(32, width)],
            *v.tails_four,
            v.unit_two,
            v.scale_two,
            norm_gains,
            *v.slopes_tail,
            v.hidden_tail,
            v.act_tail,
            *v.feed_turned,
            scratch=[pltpu.VMEM((SMALL, units), F32), pltpu.VMEM((SMALL, width), F32)],
        )
        v.tail_three_oth = to_chip(v.tail_three)

    def attend_back_tail():
        v.one_tail, v.sums_first, v.qb0, v.kvo0, give = call(
            attend_back_tail_kernel,
            [tail_shape, shape(8, width), shape(rows_dev, cols), shape(2 * cols, rows_dev)]
            + [shape(2 * cols + 8 * (width // rows_dev), rows_dev)],
            v.two_tail,
            v.tail_three,
            v.tail_three_oth,
            v.unit_one,
            v.scale_one,
            norm_gains,
            v.c0,
            v.probs0,
            v.q0,
            v.k0,
            v.k0_oth,
            v.v0,
            v.v0_oth,
            *v.out_w,
            v.qb0_text,
            v.kvo0_text,
            v.kvg0_text,
            v.sums_one0,
            v.sums_one1,
            v.sums_two0,
            v.sums_two1,
            v.sums_two_tail,
            scal=True,
            scratch=[
                pltpu.VMEM((SMALL, cols), F32),
                pltpu.VMEM((2 * cols, seq_count * rows_dev), F32),
            ],
        )
        v.got0 = swap_seq(give)

    def turn_back1():
        v.kvb1 = call(
            turn_back_kernel, shape(rows_dev, 2 * cols), v.kvo1, v.got1
        )

    def turn_back0():
        v.kvb0, v.sums = call(
            turn_back_kernel,
            [shape(rows_dev, 2 * cols), shape(8, width)],
            v.kvo0,
            v.got0,
            v.sums_first,
        )

    def attend_weights():
        outs = [shape(batch_count, chunk, 2 * cols), shape(batch_count * chunk, 2 * cols)] * 2
        v.attend_terms = call(
            functools.partial(attend_weights_kernel, batch_count, chunk),
            outs if halving else [shape(width, 4 * cols)],
            v.rows0,
            v.rows1,
            v.qb0,
            v.qb1,
            v.kvb0,
            v.kvb1,
            v.one0,
            v.got_one0,
            v.one_tail,
            v.one1,
            v.got_one1,
            v.c0,
            v.c1,
            scal=True,
            scratch=[pltpu.VMEM((width, 4 * cols), F32)],
        )
        if halving:
            v.got_attend0 = swap_seq(v.attend_terms[1])
            v.got_attend1 = swap_seq(v.attend_terms[3])

    def rows1():
        v.rows_keep1, give = call(
            rows_kernel, [part, part], v.qb1, v.kvb1, *v.in_w, scal=True
        )
        v.got_give1 = to_core(give)

    def rows0():
        v.rows_keep0, give = call(
            rows_kernel,
            [part, shape(half + 8, width)],
            v.qb0,
            v.kvb0,
            *v.in_w,
            v.sums,
            scal=True,
        )
        v.got_give0 = to_core(give)

    def join1():
        v.own_four1 = call(join_kernel, part, v.rows_keep1, v.got_give1)
        v.oth_four1 = to_chip(v.own_four1)

    def join0():
        v.own_four0 = call(join_kernel, part, v.rows_keep0, v.got_give0)
        v.oth_four0 = to_chip(v.own_four0)

    def end_rows():
        v.rows_back = call(
            end_rows_kernel,
            [part, part],
            v.one0,
            v.own_four0,
            v.oth_four0,
            v.one_tail,
            v.one1,
            v.own_four1,
            v.oth_four1,
            scal=True,
        )
        v.got_rows = [to_core(some) for some in v.rows_back]

    def end_text():
        v.text_out, v.memory_out = call(
            end_text_kernel,
            text_shape,
            v.text0,
            v.got_more0,
            v.text1,
            v.got_more1,
            scal=True,
        )

    def end_grad():
        v.text_grad, v.memory_grad = call(
            end_grad_kernel,
            text_shape,
            v.rows_back[0],
            v.got_rows[0],
            v.rows_back[1],
            v.got_rows[1],
            scal=True,
        )

    def turn_out():
        v.out_keep_two, give = call(
            turn_batch_kernel, [shape(2 * chunk, units)] * 2, v.out_keep, v.got_out
        )
        v.got_out_two = swap_batch(give, 2)

    def next_out():
        v.out_keep_three, give = call(
            turn_place_kernel,
            [shape(chunk, units)] * 2,
            v.out_keep_two,
            v.got_out_two,
        )
        v.got_out_three = swap_seq(give)

    def turn_in():
        v.in_keep, give, v.bundle0, _, v.bundle_other, _ = call(
            functools.partial(turn_in_kernel, batch_count, chunk, mem_dev),
            [shape(2, chunk, units), shape(2 * chunk + 32, units)] + [shape(24, width)] * 4,
            v.in0,
            v.got_in0,
            v.in1,
            v.got_in1,
            v.bundle,
            scal=True,
        )
        v.got_in_one = swap_batch(give, 1)

    def next_in():
        v.in_keep_two, give, v.bundle1 = call(
            functools.partial(next_in_kernel, chunk, mem_dev),
            [shape(chunk, units), shape(chunk + 48, units), shape(24, width)],
            v.in_keep,
            v.got_in_one,
            v.bundle_other,
        )
        v.got_in_two = swap_batch(give, 2)

    def turn_attend0():
        v.attend_keep0, give, v.norms_one = call(
            turn_first_kernel,
            [shape(2, chunk, 2 * cols), shape(2 * chunk + folded, 2 * cols), shape(8, width)],
            v.attend_terms[0],
            v.got_attend0,
            v.sums,
            v.got_give0,
        )
        v.got_turn0 = swap_batch(give, 1)

    def turn_attend1():
        v.attend_keep1, give = call(
            turn_seq_kernel,
            [shape(2, chunk, 2 * cols)] * 2,
            v.attend_terms[2],
            v.got_attend1,
        )
        v.got_turn1 = swap_batch(give, 1)

    def next_attend0():
        v.attend_last0, give, v.norms_two = call(
            next_first_kernel,
            [shape(chunk, 2 * cols), shape(chunk + folded, 2 * cols), shape(8, width)],
            v.attend_keep0,
            v.got_turn0,
            v.norms_one,
        )
        v.got_last0 = swap_batch(give, 2)

    def next_attend1():
        v.attend_last1, give = call(
            turn_batch_kernel,
            [shape(chunk, 2 * cols)] * 2,
            v.attend_keep1,
            v.got_turn1,
        )
        v.got_last1 = swap_batch(give, 2)

    def end_in():
        v.ffn_in_grad = call(
            functools.partial(end_in_kernel, mem_dev),
            shape(chunk, units),
            v.in_keep_two,
            v.got_in_two,
            v.bundle0,
            v.bundle1,
            scratch=factors,
        )

    def end_out():
        v.ffn_out_grad = call(
            functools.partial(end_out_kernel, mem_dev),
            shape(chunk, units),
            v.out_keep_three,
            v.got_out_three,
            v.bundle0,
            v.bundle1,
            v.got_in_two,
            scratch=factors,
        )

    def end_norms():
        v.gains_grad, v.biases_grad = call(
            end_norms_kernel,
            [shape(2, chunk)] * 2,
            v.got_last0,
            v.norms_two,
            scal=True,
        )

    def end_attend():
        v.attn_in_grad, v.attn_out_grad = call(
            end_attend_kernel,
            [shape(3, chunk, cols), shape(cols, chunk)],
            v.attend_last0,
            v.got_last0,
            v.attend_last1,
            v.got_last1,
        )

    steps = (
        (start, 0.8, tuple),
        (query0, 0.2, tuple),
        (split_out, 6.0, tuple),
        (split_feed, 0.3, tuple),
        (probs0, 0.8, tuple),
        (split_feed_sib, 0.0, tuple),
        (split_out_sib, 0.0, tuple),
        (attend0, 0.5, tuple),
        (project, 0.05, tuple),
        (feed_tail, 2.5, tuple),
        (attend_out0, 0.3, tuple),
        (link_tail, 0.5, tuple),
        (attend1, 1.3, tuple),
        (attend_out1, 0.4, tuple),
        (feed0, 1.3, tuple),
        (turn_weights, 1.0, tuple),
        (make_upstream, 0.4, tuple),
        (feed1, 1.3, tuple),
        (feed_back0, 1.3, lambda: (v.got_hidden0, v.got_act0,)),
        (feed_back1, 1.3, lambda: (v.got_back0, v.got_act1,)),
        (feed_in0, 0.1, tuple),
        (context_back0, 0.36, tuple),
        (feed_out, 0.1, tuple),
        (attend_back0, 1.5, tuple),
        (context_back1, 0.36, tuple),
        (attend_back1, 1.5, lambda: (v.got_in0,)),
        (rows_tail, 0.4, lambda: (v.got_more0, v.got_more1,)),
        (feed_back_tail, 1.5, lambda: (v.got_one0,)),
        (feed_in1, 0.7, tuple),
        (attend_back_tail, 3.2, lambda: (v.got1, v.got_one0,)),
        (turn_out, 1.0, tuple),
        (turn_back1, 0.15, tuple),
        (rows1, 0.1, tuple),
        (join1, 0.08, tuple),
        (turn_back0, 0.3, tuple),
        (attend_weights, 0.2, tuple),
        (turn_in, 0.08, tuple),
        (next_out, 0.08, tuple),
        (end_text, 1.0, tuple),
        (rows0, 0.1, tuple),
        (join0, 0.08, tuple),
        (turn_attend0, 2.0, tuple),
        (next_in, 0.08, tuple),
        (turn_attend1, 2.0, tuple),
        (next_attend0, 0.08, tuple),
        (end_rows, 0.2, tuple),
        (next_attend1, 0.08, tuple),
        (end_in, 8.0, tuple),
        (end_out, 0.08, tuple),
        (end_grad, 0.8, tuple),
        (end_norms, 0.08, tuple),
        (end_attend, 0.08, tuple),
    )
    halving_only = (turn_out, turn_in, next_out, turn_attend0, next_in, turn_attend1, next_attend0, next_attend1, end_in, end_out, end_norms, end_attend)
    for step, cost, waits in steps:
        if halving or step not in halving_only:
            order.name, order.cost = step.__name__.removeprefix("make_"), cost
            if halving:
                order.wait(*jax.tree.leaves(waits()))
            step()

    if not halving:

        def scatter(values):
            return lax.psum_scatter(values, ("batch", "seq"), scatter_dimension=0, tiled=True)

        def outer(left, right):
            return jnp.einsum("rd,rf->df", left, right, precision=lax.Precision.HIGHEST)

        bundle = v.bundle
        v.ffn_out_grad = scatter(v.out_keep + outer(bundle[16:24], bundle[24:32]))
        in_terms = jnp.concatenate([v.in0, v.in1], axis=1)
        v.ffn_in_grad = scatter(in_terms + outer(bundle[0:8], bundle[8:16]))
        total = scatter(v.attend_terms[0])
        v.attn_in_grad = jnp.stack([total[:, t * cols : (t + 1) * cols] for t in range(3)])
        v.attn_out_grad = total[:, 3 * cols :].T
        norms = lax.psum(v.sums + v.got_give0[half:], "batch")
        place = (lax.axis_index("batch") * seq_count + lax.axis_index("seq")) * chunk
        norms = lax.dynamic_slice_in_dim(norms, place, chunk, 1)
        v.gains_grad, v.biases_grad = norms[0:2], norms[2:4]
    return (
        v.text_out.transpose(1, 0, 2)[None],
        v.memory_out.transpose(1, 0, 2),
        v.text_grad.transpose(1, 0, 2)[None],
        v.memory_grad.transpose(1, 0, 2),
        v.attn_in_grad,
        v.attn_out_grad,
        v.ffn_in_grad,
        v.ffn_out_grad.T,
        v.gains_grad,
        v.biases_grad,
    )


def solution(mesh):
    placed = (
        P("batch", None, "seq", None),
        P("batch", "seq", None),
        P("batch"),
        P("batch", None, "seq"),
        P("batch", None, "seq", None),
        P(None, None, "mp"),
        P("mp", None),
        P(None, "mp"),
        P("mp", None),
        P(),
        P(),
    )
    return jax.shard_map(
        local,
        mesh=mesh,
        in_specs=placed,
        out_specs=(
            P("batch", None, "seq", None),
            P("batch", "seq", None),
            P("batch", None, "seq", None),
            P("batch", "seq", None),
            P(None, ("batch", "seq"), "mp"),
            P("mp", ("batch", "seq")),
            P(("batch", "seq"), "mp"),
            P("mp", ("batch", "seq")),
            P(None, ("batch", "seq")),
            P(None, ("batch", "seq")),
        ),
        check_vma=False,
    )
```

```python
import functools
import math
import types

import jax
import jax.numpy as jnp
from jax import lax
from jax.experimental import pallas as pl
from jax.experimental.pallas import tpu as pltpu
from jax.sharding import PartitionSpec as P

HD = 64
EPS = 1e-12
NEG = -1e30
SMALL = 16
SCALE = 1.0 / math.sqrt(HD)
F32 = jnp.float32
BF16 = jnp.bfloat16
NN = ((1,), (0,))
NT = ((1,), (1,))
TN = ((0,), (0,))
CORE_SWAP = [(0, 1), (1, 0), (2, 3), (3, 2)]
CHIP_SWAP = [(0, 2), (2, 0), (1, 3), (3, 1)]
CROSS_SWAP = [(0, 3), (3, 0), (1, 2), (2, 1)]
SEQ_SWAP = [(0, 1), (1, 0)]
VMEM_SPEC = pl.BlockSpec(memory_space=pltpu.VMEM)
SMEM_SPEC = pl.BlockSpec(memory_space=pltpu.SMEM)
KERNEL_VMEM = 16 << 20
CORE, SEQ, LENGTH, BATCH, MP = range(5)


def pair(values):
    high = values.astype(BF16)
    return high, (values - high.astype(F32)).astype(BF16)


def dot(a, b, dims):
    return lax.dot_general(a, b, (dims, ((), ())), preferred_element_type=F32)


def mm3(a, b, dims=NN):
    rows = a[0].shape[0]
    if dims != TN and rows <= 128:
        both = dot(jnp.concatenate(a, axis=0), b[0], dims)
        return both[:rows] + (both[rows:] + dot(a[0], b[1], dims))
    return dot(a[0], b[0], dims) + (dot(a[0], b[1], dims) + dot(a[1], b[0], dims))


def load(refs):
    return refs[0][...], refs[1][...]


def mean_of(values):
    return jnp.sum(values, axis=-1, keepdims=True) * (1.0 / values.shape[-1])


def sum_rows(values):
    return jnp.sum(values, axis=0, keepdims=True)


def norm_forward(inputs, gain_row, bias_row):
    centre = inputs - mean_of(inputs)
    inverse = lax.rsqrt(mean_of(centre * centre) + EPS)
    normed = centre * inverse
    return normed * gain_row + bias_row, normed, inverse


def norm_backward(upstream, normed, inverse, gain_row):
    scaled = upstream * gain_row
    return inverse * (scaled - mean_of(scaled) - normed * mean_of(scaled * normed))


def gelu_both(inputs):
    cdf = 0.5 * (1.0 + lax.erf(inputs * (1.0 / math.sqrt(2.0))))
    density = jnp.exp(-0.5 * inputs * inputs) * (1.0 / math.sqrt(2.0 * math.pi))
    return inputs * cdf, cdf + inputs * density


def in_order(core, own, other):
    return jnp.concatenate(
        [jnp.where(core == 0, own, other), jnp.where(core == 0, other, own)], axis=0
    )


def sum_refs(refs):
    total = refs[0][...]
    for ref in refs[1:]:
        total = total + ref[...]
    return total


def head(values, index):
    return values[:, index * HD : (index + 1) * HD]


def half_of(ref, core):
    half = ref.shape[0] // 2
    return ref[pl.ds(pl.multiple_of(core * half, half), half), :]


def split_kernel(*refs):
    count = len(refs) // 3
    for index in range(count):
        high, low = pair(refs[index][...])
        refs[count + 2 * index][...] = high
        refs[count + 2 * index + 1][...] = low


def turn_weights_kernel(*refs):
    count = len(refs) // 2
    for source, target in zip(refs[:count], refs[count:]):
        target[...] = source[...].T


def start_kernel(scal, text, memory, attn_in, rows0, rows1, high, low, k0, v0):
    text_dev = text.shape[0]
    mem_dev = memory.shape[0]
    rows0[0:text_dev] = text[:, 0, :]
    for index in range(2 * mem_dev):
        rows0[text_dev + index : text_dev + index + 1] = memory[index % mem_dev]
    rows1[-SMALL:] = jnp.zeros((SMALL, rows1.shape[1]), F32)
    rows1[0:text_dev] = text[:, 1, :]
    right = pair(rows0[...])
    for part, target in ((1, k0), (2, v0), (0, None)):
        left = pair(attn_in[part])
        high[part], low[part] = left
        if target is not None:
            target[...] = mm3(left, right, NT)


def query_kernel(rows, high, low, q):
    q[...] = mm3(pair(rows[...]), (high[0], low[0]), NT)


def project_kernel(rows1, high, low, q1, kv1):
    cols = q1.shape[1]
    rows = pair(rows1[...])
    q1[...] = mm3(rows, (high[0], low[0]), NT)
    for part in (1, 2):
        kv1[(part - 1) * cols : part * cols] = mm3((high[part], low[part]), rows, NT)


def upstream_kernel(scal, out_grad, mlm, up0, up1):
    text_dev = out_grad.shape[0]
    row = lax.broadcasted_iota(jnp.int32, (text_dev, text_dev), 0)
    column = lax.broadcasted_iota(jnp.int32, (text_dev, text_dev), 1)
    position = lax.broadcasted_iota(jnp.int32, (text_dev, 1), 0)
    for segment, up in enumerate((up0, up1)):
        flags = mlm[segment : segment + 1].astype(F32)
        weight = jnp.sum(jnp.where(row == column, flags, 0.0), axis=1, keepdims=True)
        if segment == 1:
            weight = jnp.where(scal[SEQ] * text_dev + position < scal[LENGTH], weight, 0.0)
        up[-SMALL:] = jnp.zeros((SMALL, up.shape[1]), F32)
        up[0:text_dev] = out_grad[:, segment, :] * weight


def head_rows(values, index):
    return values[index * HD : (index + 1) * HD]


def attend_probs(scal, query, keys_own, keys_oth, masked, text_dev, probs):
    rows_dev = query.shape[0]
    if masked:
        place = lax.broadcasted_iota(jnp.int32, (1, 2 * rows_dev), 1)
        shard = jnp.where(place < rows_dev, scal[SEQ], 1 - scal[SEQ])
        inside = jnp.where(place < rows_dev, place, place - rows_dev)
        valid = (inside >= text_dev) | (shard * text_dev + inside < scal[LENGTH])
    keys = jnp.concatenate([keys_own, keys_oth], axis=1)
    for index in range(query.shape[1] // HD):
        scores = mm3(pair(head(query, index)), pair(head_rows(keys, index))) * SCALE
        if masked:
            scores = jnp.where(valid, scores, NEG)
        expo = jnp.exp(scores - jnp.max(scores, axis=-1, keepdims=True))
        probs[index] = expo * (1.0 / jnp.sum(expo, axis=-1, keepdims=True))


def attend_values(probs, values_own, values_oth, context):
    values = jnp.concatenate([values_own, values_oth], axis=1)
    for index in range(probs.shape[0]):
        term = mm3(pair(probs[index]), pair(head_rows(values, index)), NT)
        context[:, index * HD : (index + 1) * HD] = term


def attend_first_kernel(q, k_own, k_oth, probs):
    attend_probs(None, q[...], k_own[...], k_oth[...], False, 0, probs)


def attend_next_kernel(scal, probs, v_own, v_oth, wh, wl, context, give, tail):
    attend_values(probs, v_own[...], v_oth[...], context)
    give[...] = half_of(context, 1 - scal[CORE])
    tail[...] = mm3(pair(context[-SMALL:]), (wh[...], wl[...]))


def attend_last_kernel(
    text_dev, scal, q, q_tail, kv_own, kv_oth, own_tail, oth_tail,
    context, probs, give, q_full, k_own, k_oth, v_own, v_oth, rows,
):
    first = q.shape[0] - SMALL
    q_full[0:first] = q[0:first]
    q_full[first:] = q_tail[...]
    lanes = rows.shape[0]
    place = lax.broadcasted_iota(jnp.int32, (1, lanes), 1)
    rows[...] = jnp.zeros(rows.shape, F32)
    cols = q.shape[1]
    for keys, values, body, tail in (
        (k_own, v_own, kv_own, own_tail),
        (k_oth, v_oth, kv_oth, oth_tail),
    ):
        rows[-SMALL:] = tail[...]
        last = jnp.where(place < lanes - SMALL, body[:, -lanes:], rows[...].T)
        for full, some in ((keys, slice(0, cols)), (values, slice(cols, 2 * cols))):
            full[:, 0:-lanes] = body[some, 0:-lanes]
            full[:, -lanes:] = last[some]
    attend_probs(scal, q_full[...], k_own[...], k_oth[...], True, text_dev, probs)
    attend_values(probs, v_own[...], v_oth[...], context)
    give[...] = half_of(context, 1 - scal[CORE])


def attend_out_kernel(scal, context, got, wh, wl, sh, sl, partial):
    own = mm3(pair(half_of(context, scal[CORE])), (wh[...], wl[...]))
    partial[...] = own + mm3(pair(got[...]), (sh[...], sl[...]))


def feed_rows(hidden, weights, act_own, act_sib, slope_own, slope_sib):
    left = pair(hidden)
    total = None
    for (ih, il, oh, ol), act, slope in (
        (weights[:4], act_own, slope_own),
        (weights[4:], act_sib, slope_sib),
    ):
        value, grad = gelu_both(mm3(left, load((ih, il))))
        act[...] = value
        slope[...] = grad
        term = mm3(pair(value), load((oh, ol)))
        total = term if total is None else total + term
    return total


def feed_tail_kernel(rows, p0, p1, p2, p3, gains, biases, *refs):
    weights, (hidden, normed, inverse, *others, partial) = refs[:8], refs[8:]
    attended = sum_refs((p0, p1, p2, p3))
    value, unit, scale = norm_forward(rows[-SMALL:] + attended, gains[0:1], biases[0:1])
    hidden[...] = value
    normed[...] = unit
    inverse[...] = scale
    partial[...] = feed_rows(value, weights, *others)


def link_tail_kernel(
    text_dev, hidden, own, oth, gains, biases, rows, high, low, first,
    rows_full, q_tail, kv_tail, normed, inverse, first_next,
):
    first_next[...] = first[...]
    mixed = own[...] + oth[...]
    result, unit, scale = norm_forward(hidden[...] + mixed, gains[1:2], biases[1:2])
    normed[...] = unit
    inverse[...] = scale
    head_rows = rows.shape[0] - SMALL
    place = lax.broadcasted_iota(jnp.int32, (SMALL, 1), 0)
    tail = jnp.where(place < text_dev - head_rows, rows[-SMALL:], result)
    rows_full[0:head_rows] = rows[0:head_rows]
    rows_full[head_rows:] = tail
    left = pair(tail)
    cols = q_tail.shape[1]
    q_tail[...] = mm3(left, (high[0], low[0]), NT)
    kv_tail[:, 0:cols] = mm3(left, (high[1], low[1]), NT)
    kv_tail[:, cols:] = mm3(left, (high[2], low[2]), NT)


def feed_kernel(scal, rows, own, oth, gains, biases, *refs):
    weights, (hidden, normed, inverse, *others, partial) = refs[:8], refs[8:]
    inputs = half_of(rows, scal[CORE]) + (own[...] + oth[...])
    value, unit, scale = norm_forward(inputs, gains[0:1], biases[0:1])
    hidden[...] = value
    normed[...] = unit
    inverse[...] = scale
    partial[...] = feed_rows(value, weights, *others)


def feed_rows_back(grad_two, weights, slope_own, slope_sib, back_own, back_sib):
    left = pair(grad_two)
    total = None
    for (ih, il, oh, ol), slope, back in (
        (weights[:4], slope_own, back_own),
        (weights[4:], slope_sib, back_sib),
    ):
        grad = mm3(left, load((oh, ol))) * slope[...]
        back[...] = grad
        term = mm3(pair(grad), load((ih, il)))
        total = term if total is None else total + term
    return total


def feed_back_kernel(scal, hidden, own, oth, gains, biases, upstream, slope_own, slope_sib, *refs):
    weights, (outcome, pre_two, two_first, two_second, back_own, give, give_more, *others) = (
        refs[:8],
        refs[8:],
    )
    sums, partial, back_sib = others
    mixed = own[...] + oth[...]
    result, unit, scale = norm_forward(hidden[...] + mixed, gains[1:2], biases[1:2])
    outcome[...] = result
    back = half_of(upstream, scal[CORE])
    sums[0:1] = sum_rows(back * unit)
    sums[1:2] = sum_rows(back)
    grad_two = norm_backward(back, unit, scale, gains[1:2])
    pre_two[...] = grad_two
    partial[...] = feed_rows_back(grad_two, weights, slope_own, slope_sib, back_own, back_sib)
    first = give.shape[1]
    two_first[...] = grad_two[:, 0:first]
    two_second[...] = grad_two[:, first:]
    give[...] = back_sib[:, 0:first]
    give_more[:, 0:first] = back_sib[:, first:]
    give_more[:, first:] = result


def context_back_kernel(
    pre_two, own, oth, normed, inverse, gains, wh, wl, sh, sl, pre_one, sums, back_own, give
):
    hidden_back = pre_two[...] + (own[...] + oth[...])
    unit = normed[...]
    sums[0:1] = sum_rows(hidden_back * unit)
    sums[1:2] = sum_rows(hidden_back)
    grad_one = norm_backward(hidden_back, unit, inverse[...], gains[0:1])
    pre_one[...] = grad_one
    left = pair(grad_one)
    back_own[...] = mm3(left, (wh[...], wl[...]), NT)
    give[...] = mm3(left, (sh[...], sl[...]), NT)


def heads_back(context_back, context, prob_of, query, keys, values, query_back, kv_back):
    product = context_back * context
    cols = query.shape[1]
    for index in range(cols // HD):
        key = pair(head_rows(keys, index))
        value = pair(head_rows(values, index))
        back = pair(head(context_back, index))
        delta = jnp.sum(head(product, index), axis=-1, keepdims=True)
        prob = prob_of(index)
        score_back = prob * (mm3(back, value) - delta) * SCALE
        score_back = pair(score_back)
        query_back[:, index * HD : (index + 1) * HD] = mm3(score_back, key, NT)
        kv_back[index * HD : (index + 1) * HD] = mm3(pair(head(query, index)), score_back, TN)
        kv_back[cols + index * HD : cols + (index + 1) * HD] = mm3(back, pair(prob), TN)


def attend_back_kernel(
    scal, back_own, back_got, context, probs, q, k_own, k_oth, v_own, v_oth,
    q_back, own_back, give_back, own_tail, give_tail, kv_back,
):
    context_back = in_order(scal[CORE], back_own[...], back_got[...])
    heads_back(
        context_back,
        context[...],
        lambda index: probs[index],
        q[...],
        jnp.concatenate([k_own[...], k_oth[...]], axis=1),
        jnp.concatenate([v_own[...], v_oth[...]], axis=1),
        q_back,
        kv_back,
    )
    rows_dev = q.shape[0]
    own_back[...] = kv_back[:, 0:rows_dev]
    give_back[...] = kv_back[:, rows_dev:]
    own_tail[...] = kv_back[:, rows_dev - 128 : rows_dev].T[-SMALL:]
    give_tail[...] = kv_back[:, 2 * rows_dev - 128 : 2 * rows_dev].T[-SMALL:]


def project_back(query_back, kv_back, high, low):
    cols = query_back.shape[1]
    total = mm3(pair(query_back), (high[0], low[0]))
    total = total + mm3(pair(kv_back[:, 0:cols]), (high[1], low[1]))
    return total + mm3(pair(kv_back[:, cols:]), (high[2], low[2]))


def rows_tail_kernel(
    scal, q_back, own_tail, got_tail, high, low, pre_one, give_back, partial, give_next
):
    total = project_back(q_back[-SMALL:], own_tail[...] + got_tail[...], high, low)
    partial[...] = total + jnp.where(scal[MP] == 1, pre_one[-SMALL:], 0.0)
    give_next[...] = give_back[...]


def feed_back_tail_kernel(
    mem_dev, p0, p1, p2, p3, normed, inverse, gains, slope_own, slope_sib, hidden, act, *refs
):
    weights, (pre_two, back_own, partial, sums, bundle, back_sib, back) = refs[:8], refs[8:]
    rows_back = sum_refs((p0, p1, p2, p3))
    first = SMALL - mem_dev
    back[0:first] = jnp.zeros((first, back.shape[1]), F32)
    back[first:] = rows_back[first - mem_dev : first] + rows_back[first:]
    upstream = back[...]
    unit = normed[...]
    sums[0:1] = sum_rows(upstream * unit)
    sums[1:2] = sum_rows(upstream)
    grad_two = norm_backward(upstream, unit, inverse[...], gains[1:2])
    pre_two[...] = grad_two
    partial[...] = feed_rows_back(grad_two, weights, slope_own, slope_sib, back_own, back_sib)
    bundle[0:8] = hidden[8:]
    bundle[8:16] = back_own[8:]
    bundle[16:24] = pre_two[8:]
    bundle[24:32] = act[8:]


def attend_back_tail_kernel(
    scal, pre_two, own, oth, normed, inverse, gains, context, probs, q, k_own, k_oth, v_own, v_oth, wh, wl,
    q_back, own_back, give_back, sums_one0, sums_one1, sums_two0, sums_two1, sums_two_tail,
    pre_one, sums, q_back_all, own_back_all, give_back_all, q_tail, kv_back,
):
    hidden_back = pre_two[...] + (own[...] + oth[...])
    unit = normed[...]
    one = sums_one0[...] + sums_one1[...]
    two = sums_two0[...] + sums_two1[...]
    once = jnp.where(scal[CORE] == 0, 1.0, 0.0)
    two = two + once * sums_two_tail[...]
    sums[0:1] = one[0:1] + once * sum_rows(hidden_back * unit)
    sums[1:2] = two[0:1]
    sums[2:3] = one[1:2] + once * sum_rows(hidden_back)
    sums[3:4] = two[1:2]
    sums[4:] = jnp.zeros((4, sums.shape[1]), F32)
    grad_one = norm_backward(hidden_back, unit, inverse[...], gains[0:1])
    pre_one[...] = grad_one
    context_back = mm3(pair(grad_one), (wh[...], wl[...]), NT)
    heads_back(
        context_back,
        context[-SMALL:],
        lambda index: probs[index, -SMALL:],
        q[-SMALL:],
        jnp.concatenate([k_own[...], k_oth[...]], axis=1),
        jnp.concatenate([v_own[...], v_oth[...]], axis=1),
        q_tail,
        kv_back,
    )
    first = q.shape[0] - SMALL
    q_back_all[0:first] = q_back[0:first]
    q_back_all[first:] = q_back[first:] + q_tail[...]
    rows_dev = q.shape[0]
    own_back_all[...] = own_back[...] + kv_back[:, 0:rows_dev]
    keys = kv_back.shape[0]
    give_back_all[0:keys] = give_back[...] + kv_back[:, rows_dev:]
    for part in range(sums.shape[1] // rows_dev):
        place = slice(part * rows_dev, (part + 1) * rows_dev)
        give_back_all[keys + 8 * part : keys + 8 * part + 8] = sums[:, place]


def turn_back_kernel(own_back, got_back, *refs):
    rows, width = own_back.shape
    if len(refs) > 1:
        own_sums, kv_back, sums = refs
        for part in range(sums.shape[1] // width):
            place = slice(part * width, (part + 1) * width)
            sums[:, place] = own_sums[:, place] + got_back[rows + 8 * part : rows + 8 * part + 8]
    else:
        (kv_back,) = refs
    kv_back[...] = (own_back[...] + got_back[0:rows]).T


def rows_kernel(scal, q_back, kv_back, high, low, *refs):
    *sums, keep, give = refs
    half = keep.shape[0]
    total = project_back(q_back[...], kv_back[...], high, low)
    first, second = total[0:half], total[half:]
    own = scal[CORE] == 0
    keep[...] = jnp.where(own, first, second)
    give[0:half] = jnp.where(own, second, first)
    if sums:
        give[half:] = sums[0][...]


def join_kernel(keep, got, out):
    out[...] = keep[...] + got[0 : keep.shape[0]]


def end_rows_kernel(scal, one0, own0, oth0, tail, one1, own1, oth1, out0, out1):
    first = one0[...] + (own0[...] + oth0[...])
    out0[...] = first
    out0[-SMALL:] = first[-SMALL:] + jnp.where(scal[CORE] == 1, tail[...], 0.0)
    out1[...] = one1[...] + (own1[...] + oth1[...])


def end_text(core, own0, oth0, own1, oth1, memory, text, last):
    text_dev = text.shape[0]
    text[:, 0, :] = in_order(core, own0, oth0)[0:text_dev]
    text[:, 1, :] = in_order(core, own1, oth1)[0:text_dev]
    for index in range(last.shape[0]):
        last[index] = memory[index : index + 1]


def end_text_kernel(scal, own0, got0, own1, got1, text, last):
    core = scal[CORE]
    first = got0.shape[1] - own0.shape[1]
    memory = jnp.where(core == 1, own1[-SMALL:], got1[-SMALL:, first:])
    memory = memory[SMALL - last.shape[0] :]
    end_text(core, own0[...], got0[:, first:], own1[...], got1[:, first:], memory, text, last)


def end_grad_kernel(scal, own0, got0, own1, got1, text, last):
    core = scal[CORE]
    mem_dev = last.shape[0]
    memory = jnp.where(core == 1, own0[-SMALL:], got0[-SMALL:])[SMALL - 2 * mem_dev :]
    memory = memory[0:mem_dev] + memory[mem_dev:]
    end_text(core, own0[...], got0[...], own1[...], got1[...], memory, text, last)


def block_at(scal, slot):
    return jnp.bitwise_xor(scal[BATCH], slot)


def stacked(*refs):
    return jnp.concatenate([ref[...] for ref in refs], axis=0)


def put_chunks(product, scal, batch_count, chunk, outs):
    for part in range(len(outs) // 2):
        keep, give = outs[2 * part], outs[2 * part + 1]
        width = keep.shape[2]
        columns = slice(part * width, (part + 1) * width)
        for slot in range(batch_count):
            block = 2 * block_at(scal, slot)
            mine = pl.multiple_of((block + scal[SEQ]) * chunk, chunk)
            others = pl.multiple_of((block + 1 - scal[SEQ]) * chunk, chunk)
            keep[slot] = product[pl.ds(mine, chunk), columns]
            give[slot * chunk : (slot + 1) * chunk] = product[pl.ds(others, chunk), columns]


def feed_in_kernel(columns, batch_count, chunk, scal, *refs):
    lefts, rights, *more, keep, give, product = refs[0:4], refs[4:8], *refs[8:]
    given = slice(0, columns.stop - columns.start)
    rights = [ref.at[:, columns if place % 2 == 0 else given] for place, ref in enumerate(rights)]
    product[...] = mm3(pair(stacked(*lefts)), pair(stacked(*rights)), TN)
    if batch_count != 4:
        keep[...] = product[...]
        return
    put_chunks(product, scal, batch_count, chunk, (keep, give))
    if more:
        put_folded(give, batch_count * chunk, more[0][...])


def feed_out_kernel(batch_count, chunk, scal, *refs):
    lefts, rights, outs, product = refs[0:6], refs[6:10], refs[10:-1], refs[-1]
    lefts = [
        lefts[0][...],
        jnp.concatenate([lefts[1][...], lefts[2][...]], axis=1),
        lefts[3][...],
        jnp.concatenate([lefts[4][...], lefts[5][...]], axis=1),
    ]
    lefts = jnp.concatenate(lefts, axis=0)
    product[...] = mm3(pair(lefts), pair(stacked(*rights)), TN)
    if batch_count != 4:
        outs[0][...] = product[...]
        return
    for slot in range(batch_count):
        block = 2 * block_at(scal, slot)
        mine = pl.multiple_of((block + scal[SEQ]) * chunk, chunk)
        others = pl.multiple_of((block + 1 - scal[SEQ]) * chunk, chunk)
        outs[slot % 2][slot // 2, 0:chunk] = product[pl.ds(mine, chunk), :]
        outs[slot % 2][slot // 2, chunk:] = product[pl.ds(others, chunk), :]


def attend_weights_kernel(
    batch_count, chunk, scal, rows0, rows1, q0, q1, kv0, kv1,
    one0, got0, tail, one1, got1, c0, c1, *refs,
):
    *outs, product = refs
    core = scal[CORE]
    rows = pair(stacked(rows0, rows1))
    cols = q0.shape[1]
    product[:, 0:cols] = mm3(rows, pair(stacked(q0, q1)), TN)
    product[:, cols : 3 * cols] = mm3(rows, pair(stacked(kv0, kv1)), TN)
    first = in_order(core, one0[...], got0[...])
    second = in_order(core, one1[...], got1[...])
    head_rows = first.shape[0] - SMALL
    ones = jnp.concatenate(
        [first[0:head_rows], first[head_rows:] + tail[...], second], axis=0
    )
    product[:, 3 * cols :] = mm3(pair(ones), pair(stacked(c0, c1)), TN)
    if batch_count != 4:
        outs[0][...] = product[...]
        return
    put_chunks(product, scal, batch_count, chunk, outs)


def turn_seq_kernel(*refs):
    *terms, keep_next, give_next = refs
    chunk = terms[0].shape[1]
    first = 0
    for keep, got in zip(terms[0::2], terms[1::2]):
        place = slice(first, first + keep.shape[2])
        first += keep.shape[2]
        for slot in range(keep.shape[0]):
            target = give_next if slot % 2 else keep_next
            total = keep[slot] + got[slot * chunk : (slot + 1) * chunk]
            target[slot // 2, :, place] = total


def turn_batch_kernel(keep, got, keep_next, give_next):
    keep_next[...] = keep[0] + got[0]
    give_next[...] = keep[1] + got[1]


def turn_place_kernel(keep, got, keep_next, give_next):
    total = keep[...] + got[...]
    chunk = keep_next.shape[0]
    keep_next[...] = total[0:chunk]
    give_next[...] = total[chunk:]


def pick(values, blocks, chunk, index):
    width = blocks * chunk
    return pltpu.roll(values, width - index * chunk, 1)[:, 0:chunk]


def put_bundle(piece, sources, batch_count, chunk, mem_dev, index):
    first = 8 - mem_dev
    piece[...] = jnp.zeros(piece.shape, F32)
    for source in range(2):
        for kind in range(2):
            slot = 2 * source + kind
            left = sources[source][16 * kind : 16 * kind + 8]
            right = sources[source][16 * kind + 8 : 16 * kind + 16]
            left = pick(left, 2 * batch_count, chunk, index)
            piece[slot * mem_dev : (slot + 1) * mem_dev] = right[first:]
            row = 4 * mem_dev + slot
            for place in range(mem_dev):
                piece[row : row + 1, 128 * place : 128 * place + chunk] = left[
                    first + place : first + place + 1
                ]


def put_folded(target, first, values):
    rows, width = values.shape
    part = target.shape[1]
    for place in range(width // part):
        target[first : first + rows] = values[:, place * part : (place + 1) * part]
        first += rows


def get_folded(source, first, rows, width):
    places = range(width // source.shape[1])
    return jnp.concatenate(
        [source[first + place * rows : first + (place + 1) * rows] for place in places], axis=1
    )


def turn_in_kernel(batch_count, chunk, mem_dev, scal, *refs):
    *terms, bundle, keep_next, give_next, own, nearest, other, last = refs
    first = 0
    for keep, got in zip(terms[0::2], terms[1::2]):
        place = slice(first, first + keep.shape[2])
        first += keep.shape[2]
        for slot in range(keep.shape[0]):
            total = keep[slot] + got[slot * chunk : (slot + 1) * chunk]
            if slot % 2:
                give_next[slot // 2 * chunk : (slot // 2 + 1) * chunk, place] = total
            else:
                keep_next[slot // 2, :, place] = total
    sources = (bundle[...], get_folded(terms[-1], batch_count * chunk, *bundle.shape))
    pieces = (own, nearest, other, last)
    for slot in range(batch_count):
        index = 2 * block_at(scal, slot) + scal[SEQ]
        put_bundle(pieces[slot], sources, batch_count, chunk, mem_dev, index)
    rows = 4 * mem_dev
    give_next[2 * chunk : 2 * chunk + 24] = nearest[...]
    give_next[2 * chunk + 24 : 2 * chunk + 28] = last[rows : rows + 4]
    give_next[2 * chunk + 28 :] = jnp.zeros((4, first), F32)


def next_in_kernel(chunk, mem_dev, keep, got, other, keep_next, give_next, bundle):
    keep_next[...] = keep[0] + got[0:chunk]
    give_next[0:chunk] = keep[1] + got[chunk : 2 * chunk]
    rows = 4 * mem_dev
    row = 2 * chunk
    bundle[...] = got[row : row + 24]
    give_next[chunk : chunk + 24] = other[...]
    give_next[chunk + 24 : chunk + 24 + rows] = got[row : row + rows]
    give_next[chunk + 24 + rows :] = got[row + 24 : row + 28]


def turn_first_kernel(keep, got, sums, got_give, keep_next, give_next, norms):
    chunk = keep.shape[1]
    for slot in range(keep.shape[0]):
        total = keep[slot] + got[slot * chunk : (slot + 1) * chunk]
        if slot % 2:
            give_next[slot // 2 * chunk : (slot // 2 + 1) * chunk] = total
        else:
            keep_next[slot // 2] = total
    norms[...] = sums[...] + got_give[-8:]
    put_folded(give_next, 2 * chunk, norms[...])


def next_first_kernel(keep, got, norms, keep_next, give_next, norms_next):
    chunk = keep_next.shape[0]
    keep_next[...] = keep[0] + got[0:chunk]
    give_next[0:chunk] = keep[1] + got[chunk : 2 * chunk]
    norms_next[...] = norms[...] + get_folded(got, 2 * chunk, *norms.shape)
    put_folded(give_next, chunk, norms_next[...])


def end_norms_kernel(scal, got, norms, gains, biases):
    chunk = gains.shape[1]
    total = norms[...] + get_folded(got, chunk, *norms.shape)
    first = (scal[BATCH] * 2 + scal[SEQ]) * chunk
    picked = pltpu.roll(total, total.shape[1] - first, 1)[:, 0:chunk]
    gains[...] = picked[0:2]
    biases[...] = picked[2:4]


def bundle_product(kind, mem_dev, bundles, left, right):
    chunk = left.shape[1]
    left[...] = jnp.zeros(left.shape, F32)
    right[...] = jnp.zeros(right.shape, F32)
    for number, bundle in enumerate(bundles):
        for source in range(2):
            slot = 2 * source + kind
            base = 8 * (2 * number + source)
            right[base : base + mem_dev] = bundle[slot * mem_dev : (slot + 1) * mem_dev]
            row = 4 * mem_dev + slot
            for place in range(mem_dev):
                left[base + place : base + place + 1] = bundle[
                    row : row + 1, 128 * place : 128 * place + chunk
                ]
    return mm3(pair(left[...]), pair(right[...]), TN)


def end_out_kernel(mem_dev, keep, got, bundle0, bundle1, others, out, left, right):
    bundles = (bundle0, bundle1, others.at[out.shape[0] : out.shape[0] + 24], others.at[out.shape[0] + 24 :])
    extra = bundle_product(1, mem_dev, bundles, left, right)
    out[...] = keep[...] + got[...] + extra


def end_in_kernel(mem_dev, keep, got, bundle0, bundle1, out, left, right):
    chunk = out.shape[0]
    bundles = (bundle0, bundle1, got.at[chunk : chunk + 24], got.at[chunk + 24 :])
    out[...] = keep[...] + got[0:chunk] + bundle_product(0, mem_dev, bundles, left, right)


def end_attend_kernel(*refs):
    *terms, grad_in, grad_out = refs
    chunk = grad_in.shape[1]
    parts = [keep[...] + got[0:chunk] for keep, got in zip(terms[0::2], terms[1::2])]
    total = jnp.concatenate(parts, axis=1)
    cols = grad_in.shape[2]
    for part in range(3):
        grad_in[part] = total[:, part * cols : (part + 1) * cols]
    grad_out[...] = total[:, 3 * cols :].T


def shape(*dims, dtype=F32):
    return jax.ShapeDtypeStruct(dims, dtype)


class Order:
    def __init__(self, scal):
        self.scal = scal
        self.last = None
        self.extra = []
        self.name = None
        self.cost = 0.0

    def wait(self, *values):
        self.extra += values

    def call(self, kernel, outs, *args, scal=False, scratch=()):
        after = [] if self.last is None else [self.last]
        after += self.extra
        self.extra = []
        count = len(args) + scal
        skip = len(after)

        def body(*refs):
            kernel(*refs[:count], *refs[count + skip :])

        ins = [SMEM_SPEC] * scal + [VMEM_SPEC] * len(args)
        ins += [pl.BlockSpec(memory_space=pl.ANY)] * skip
        result = pl.pallas_call(
            body,
            out_shape=outs,
            in_specs=ins,
            out_specs=jax.tree.map(lambda _: VMEM_SPEC, outs),
            scratch_shapes=list(scratch),
            compiler_params=pltpu.CompilerParams(vmem_limit_bytes=KERNEL_VMEM),
            cost_estimate=pl.CostEstimate(
                flops=int(self.cost * 10**9), bytes_accessed=0, transcendentals=0
            ),
            name=self.name,
        )(*([self.scal] if scal else []), *args, *after)
        self.last = min(jax.tree.leaves(result), key=lambda value: value.size)
        return result


def swap_seq(values):
    return lax.ppermute(values, "seq", SEQ_SWAP)


def to_core(values):
    return lax.ppermute(values, "mp", CORE_SWAP)


def to_chip(values):
    return lax.ppermute(values, "mp", CHIP_SWAP)


def spread_mp(values):
    return values, to_core(values), to_chip(values), lax.ppermute(values, "mp", CROSS_SWAP)


def swap_batch(values, bit):
    count = lax.axis_size("batch")
    return lax.ppermute(values, "batch", [(place, place ^ bit) for place in range(count)])


def local(
    text_rows,
    memory_in,
    text_length,
    mlm_mask,
    out_grad,
    attn_in,
    attn_out,
    ffn_in,
    ffn_out,
    norm_gains,
    norm_biases,
):
    seg_count, text_dev, width = text_rows.shape[1:]
    mem_dev = memory_in.shape[1]
    cols = attn_in.shape[2]
    units = ffn_in.shape[1]
    heads = cols // HD
    batch_count = lax.axis_size("batch")
    seq_count = lax.axis_size("seq")
    rows_dev = text_dev + 2 * mem_dev
    half = rows_dev // 2
    most = units // 2
    chunk = width // (batch_count * seq_count)
    text_rows = text_rows.reshape(seg_count, text_dev, width).transpose(1, 0, 2)
    out_grad = out_grad.reshape(seg_count, text_dev, width).transpose(1, 0, 2)
    memory_in = memory_in.transpose(1, 0, 2)
    mlm_mask = mlm_mask.reshape(seg_count, text_dev)
    attn_in = attn_in.transpose(0, 2, 1)
    scal = jnp.stack(
        [
            lax.axis_index("mp") % 2,
            lax.axis_index("seq"),
            text_length[0],
            lax.axis_index("batch"),
            lax.axis_index("mp"),
        ]
    ).astype(jnp.int32)

    whole = shape(rows_dev, width)
    part = shape(half, width)
    tail_shape = shape(SMALL, width)
    row_sums = shape(2, width)
    order = Order(scal)
    call = order.call

    v = types.SimpleNamespace()
    in_pair = [shape(3, cols, width, dtype=BF16)] * 2
    out_pair = [shape(cols, width, dtype=BF16)] * 2
    feed_pairs = [shape(width, units, dtype=BF16)] * 2 + [shape(units, width, dtype=BF16)] * 2
    turned_pairs = [shape(units, width, dtype=BF16)] * 2 + [shape(width, units, dtype=BF16)] * 2
    attended = [shape(rows_dev, cols), shape(heads, rows_dev, seq_count * rows_dev)]
    attended += [shape(half, cols)]
    text_shape = [shape(text_dev, seg_count, width), shape(mem_dev, 1, width)]
    factors = [pltpu.VMEM((64, chunk), F32), pltpu.VMEM((64, units), F32)]
    folded = 8 * width // (2 * cols)
    halving = batch_count == 4

    def start():
        v.rows0, v.rows1_text, in_h, in_l, v.k0, v.v0 = call(
            start_kernel,
            [whole, whole] + in_pair + [shape(cols, rows_dev)] * 2,
            text_rows,
            memory_in,
            attn_in,
            scal=True,
        )
        v.in_w = (in_h, in_l)
        v.k0_oth, v.v0_oth = swap_seq(v.k0), swap_seq(v.v0)

    def query0():
        v.q0 = call(query_kernel, shape(rows_dev, cols), v.rows0, *v.in_w)

    def project():
        v.q1_text, v.kv1_text = call(
            project_kernel,
            [shape(rows_dev, cols), shape(2 * cols, rows_dev)],
            v.rows1_text,
            *v.in_w,
        )
        v.kv1_oth = swap_seq(v.kv1_text)

    def split_out():
        v.out_w = call(split_kernel, out_pair, attn_out)

    def split_feed():
        v.feed_own = call(split_kernel, feed_pairs, ffn_in, ffn_out)

    def split_feed_sib():
        v.feed_sib = call(
            split_kernel, feed_pairs, to_core(ffn_in), to_core(ffn_out)
        )

    def split_out_sib():
        v.out_sib = call(split_kernel, out_pair, to_core(attn_out))

    def turn_weights():
        v.feed_turned = call(
            turn_weights_kernel, turned_pairs * 2, *v.feed_own, *v.feed_sib
        )

    def make_upstream():
        v.upstream = call(
            upstream_kernel, [whole] * 2, out_grad, mlm_mask, scal=True
        )

    def probs0():
        v.probs0 = call(
            attend_first_kernel,
            shape(heads, rows_dev, seq_count * rows_dev),
            v.q0,
            v.k0,
            v.k0_oth,
        )

    def attend0():
        v.c0, give, tail = call(
            attend_next_kernel,
            [shape(rows_dev, cols), shape(half, cols), tail_shape],
            v.probs0,
            v.v0,
            v.v0_oth,
            *v.out_w,
            scal=True,
        )
        v.tails_one = spread_mp(tail)
        v.got_c0 = to_core(give)

    def feed_tail():
        v.hidden_tail, v.unit_one, v.scale_one, v.act_tail, _, *v.slopes_tail, v.tail_two = call(
            feed_tail_kernel,
            [tail_shape, tail_shape, shape(SMALL, 1)] + [shape(SMALL, units)] * 4 + [tail_shape],
            v.rows0,
            *v.tails_one,
            norm_gains,
            norm_biases,
            *v.feed_own,
            *v.feed_sib,
        )
        v.tail_two_oth = to_chip(v.tail_two)

    def attend_out0():
        v.own_first = call(
            attend_out_kernel,
            part,
            v.c0,
            v.got_c0,
            *v.out_w,
            *v.out_sib,
            scal=True,
        )

    def link_tail():
        v.rows1, v.q_tail, v.kv_tail, v.unit_two, v.scale_two, v.own_one0 = call(
            functools.partial(link_tail_kernel, text_dev),
            [whole, shape(SMALL, cols), shape(SMALL, 2 * cols), tail_shape, shape(SMALL, 1), part],
            v.hidden_tail,
            v.tail_two,
            v.tail_two_oth,
            norm_gains,
            norm_biases,
            v.rows1_text,
            *v.in_w,
            v.own_first,
        )
        v.kv_tail_oth = swap_seq(v.kv_tail)
        v.oth_one0 = to_chip(v.own_one0)

    def attend1():
        v.c1, v.probs1, give, v.q1, *full = call(
            functools.partial(attend_last_kernel, text_dev),
            attended + [shape(rows_dev, cols)] + [shape(cols, rows_dev)] * 4,
            v.q1_text,
            v.q_tail,
            v.kv1_text,
            v.kv1_oth,
            v.kv_tail,
            v.kv_tail_oth,
            scal=True,
            scratch=[pltpu.VMEM((128, 2 * cols), F32)],
        )
        v.keys1, v.values1 = full[0:2], full[2:4]
        v.got_c1 = to_core(give)

    def attend_out1():
        v.own_one1 = call(
            attend_out_kernel,
            part,
            v.c1,
            v.got_c1,
            *v.out_w,
            *v.out_sib,
            scal=True,
        )
        v.oth_one1 = to_chip(v.own_one1)

    def feed(rows, own, oth):
        return call(
            feed_kernel,
            [part, part, shape(half, 1)] + [shape(half, units)] * 4 + [part],
            rows,
            own,
            oth,
            norm_gains,
            norm_biases,
            *v.feed_own,
            *v.feed_sib,
            scal=True,
        )

    def feed0():
        v.hidden0, v.normed0, v.inverse0, v.act0, give, *v.slopes0, v.own_two0 = feed(
            v.rows0, v.own_one0, v.oth_one0
        )
        v.oth_two0 = to_chip(v.own_two0)
        v.got_hidden0, v.got_act0 = to_core(v.hidden0), to_core(give)

    def feed1():
        v.hidden1, v.normed1, v.inverse1, v.act1, give, *v.slopes1, v.own_two1 = feed(
            v.rows1, v.own_one1, v.oth_one1
        )
        v.oth_two1 = to_chip(v.own_two1)
        v.got_hidden1, v.got_act1 = to_core(v.hidden1), to_core(give)

    def feed_back(hidden, own, oth, upstream, slopes):
        return call(
            feed_back_kernel,
            [part, part, shape(half, most), shape(half, width - most), shape(half, units)]
            + [shape(half, most), shape(half, units - most + width), row_sums, part],
            hidden,
            own,
            oth,
            norm_gains,
            norm_biases,
            upstream,
            *slopes,
            *v.feed_turned,
            scal=True,
            scratch=[pltpu.VMEM((half, units), F32)],
        )

    def feed_back0():
        v.text0, v.two0, *gives, v.sums_two0, v.own_three0 = feed_back(
            v.hidden0, v.own_two0, v.oth_two0, v.upstream[0], v.slopes0
        )
        v.oth_three0 = to_chip(v.own_three0)
        *two, v.back0, give, give_more = gives
        v.got_two0 = [to_core(some) for some in two]
        v.got_back0, v.got_more0 = to_core(give), to_core(give_more)

    def feed_back1():
        v.text1, v.two1, *gives, v.sums_two1, v.own_three1 = feed_back(
            v.hidden1, v.own_two1, v.oth_two1, v.upstream[1], v.slopes1
        )
        v.oth_three1 = to_chip(v.own_three1)
        *two, v.back1, give, give_more = gives
        v.got_two1 = [to_core(some) for some in two]
        v.got_back1, v.got_more1 = to_core(give), to_core(give_more)

    def weights(kernel, outs, arrays, columns):
        if not halving:
            outs = [shape(width, columns), shape(8, columns)]
        return call(
            functools.partial(kernel, batch_count, chunk),
            outs,
            *arrays,
            scal=True,
            scratch=[pltpu.VMEM((width, columns), F32)],
        )

    def feed_in(first, last, got0, got1, *more):
        rows = batch_count * chunk + len(more) * 32 * width // (last - first)
        keep, give = weights(
            functools.partial(feed_in_kernel, slice(first, last)),
            [shape(batch_count, chunk, last - first), shape(rows, last - first)],
            (v.hidden0, v.got_hidden0, v.hidden1, v.got_hidden1)
            + (v.back0, got0, v.back1, got1, *more),
            last - first,
        )
        return keep, swap_seq(give) if halving else None

    def feed_in0():
        v.in0, v.got_in0 = feed_in(0, most, v.got_back0, v.got_back1)

    def feed_in1():
        v.in1, v.got_in1 = feed_in(most, units, v.got_more0, v.got_more1, v.bundle)

    def feed_out():
        v.out_keep, give = weights(
            feed_out_kernel,
            [shape(2, 2 * chunk, units)] * 2,
            (v.two0, *v.got_two0, v.two1, *v.got_two1)
            + (v.act0, v.got_act0, v.act1, v.got_act1),
            units,
        )
        v.got_out = swap_batch(give, 1) if halving else None

    def context_back(pre_two, own, oth, normed, inverse):
        return call(
            context_back_kernel,
            [part, row_sums] + [shape(half, cols)] * 2,
            pre_two,
            own,
            oth,
            normed,
            inverse,
            norm_gains,
            *v.out_w,
            *v.out_sib,
        )

    def context_back0():
        v.one0, v.sums_one0, v.context_back0, give = context_back(
            v.two0, v.own_three0, v.oth_three0, v.normed0, v.inverse0
        )
        v.got_context0, v.got_one0 = to_core(give), to_core(v.one0)

    def context_back1():
        v.one1, v.sums_one1, v.context_back1, give = context_back(
            v.two1, v.own_three1, v.oth_three1, v.normed1, v.inverse1
        )
        v.got_context1, v.got_one1 = to_core(give), to_core(v.one1)

    def attend_back(own, got, context, probs, query, keys, values):
        return call(
            attend_back_kernel,
            [shape(rows_dev, cols)]
            + [shape(2 * cols, rows_dev)] * 2
            + [shape(SMALL, 2 * cols)] * 2,
            own,
            got,
            context,
            probs,
            query,
            *keys,
            *values,
            scal=True,
            scratch=[pltpu.VMEM((2 * cols, seq_count * rows_dev), F32)],
        )

    def attend_back0():
        v.qb0_text, v.kvo0_text, v.kvg0_text, _, _ = attend_back(
            v.context_back0,
            v.got_context0,
            v.c0,
            v.probs0,
            v.q0,
            (v.k0, v.k0_oth),
            (v.v0, v.v0_oth),
        )

    def attend_back1():
        v.qb1, v.kvo1, v.kvg1_first, v.own_tail, give = attend_back(
            v.context_back1,
            v.got_context1,
            v.c1,
            v.probs1,
            v.q1,
            v.keys1,
            v.values1,
        )
        v.got_tail = swap_seq(give)

    def rows_tail():
        tail, give = call(
            rows_tail_kernel,
            [tail_shape, shape(2 * cols, rows_dev)],
            v.qb1,
            v.own_tail,
            v.got_tail,
            *v.in_w,
            v.one1,
            v.kvg1_first,
            scal=True,
        )
        v.tails_four = spread_mp(tail)
        v.got1 = swap_seq(give)

    def feed_back_tail():
        v.two_tail, _, v.tail_three, v.sums_two_tail, v.bundle = call(
            functools.partial(feed_back_tail_kernel, mem_dev),
            [tail_shape, shape(SMALL, units), tail_shape, row_sums, shape(32, width)],
            *v.tails_four,
            v.unit_two,
            v.scale_two,
            norm_gains,
            *v.slopes_tail,
            v.hidden_tail,
            v.act_tail,
            *v.feed_turned,
            scratch=[pltpu.VMEM((SMALL, units), F32), pltpu.VMEM((SMALL, width), F32)],
        )
        v.tail_three_oth = to_chip(v.tail_three)

    def attend_back_tail():
        v.one_tail, v.sums_first, v.qb0, v.kvo0, give = call(
            attend_back_tail_kernel,
            [tail_shape, shape(8, width), shape(rows_dev, cols), shape(2 * cols, rows_dev)]
            + [shape(2 * cols + 8 * (width // rows_dev), rows_dev)],
            v.two_tail,
            v.tail_three,
            v.tail_three_oth,
            v.unit_one,
            v.scale_one,
            norm_gains,
            v.c0,
            v.probs0,
            v.q0,
            v.k0,
            v.k0_oth,
            v.v0,
            v.v0_oth,
            *v.out_w,
            v.qb0_text,
            v.kvo0_text,
            v.kvg0_text,
            v.sums_one0,
            v.sums_one1,
            v.sums_two0,
            v.sums_two1,
            v.sums_two_tail,
            scal=True,
            scratch=[
                pltpu.VMEM((SMALL, cols), F32),
                pltpu.VMEM((2 * cols, seq_count * rows_dev), F32),
            ],
        )
        v.got0 = swap_seq(give)

    def turn_back1():
        v.kvb1 = call(
            turn_back_kernel, shape(rows_dev, 2 * cols), v.kvo1, v.got1
        )

    def turn_back0():
        v.kvb0, v.sums = call(
            turn_back_kernel,
            [shape(rows_dev, 2 * cols), shape(8, width)],
            v.kvo0,
            v.got0,
            v.sums_first,
        )

    def attend_weights():
        outs = [shape(batch_count, chunk, 2 * cols), shape(batch_count * chunk, 2 * cols)] * 2
        v.attend_terms = call(
            functools.partial(attend_weights_kernel, batch_count, chunk),
            outs if halving else [shape(width, 4 * cols)],
            v.rows0,
            v.rows1,
            v.qb0,
            v.qb1,
            v.kvb0,
            v.kvb1,
            v.one0,
            v.got_one0,
            v.one_tail,
            v.one1,
            v.got_one1,
            v.c0,
            v.c1,
            scal=True,
            scratch=[pltpu.VMEM((width, 4 * cols), F32)],
        )
        if halving:
            v.got_attend0 = swap_seq(v.attend_terms[1])
            v.got_attend1 = swap_seq(v.attend_terms[3])

    def rows1():
        v.rows_keep1, give = call(
            rows_kernel, [part, part], v.qb1, v.kvb1, *v.in_w, scal=True
        )
        v.got_give1 = to_core(give)

    def rows0():
        v.rows_keep0, give = call(
            rows_kernel,
            [part, shape(half + 8, width)],
            v.qb0,
            v.kvb0,
            *v.in_w,
            v.sums,
            scal=True,
        )
        v.got_give0 = to_core(give)

    def join1():
        v.own_four1 = call(join_kernel, part, v.rows_keep1, v.got_give1)
        v.oth_four1 = to_chip(v.own_four1)

    def join0():
        v.own_four0 = call(join_kernel, part, v.rows_keep0, v.got_give0)
        v.oth_four0 = to_chip(v.own_four0)

    def end_rows():
        v.rows_back = call(
            end_rows_kernel,
            [part, part],
            v.one0,
            v.own_four0,
            v.oth_four0,
            v.one_tail,
            v.one1,
            v.own_four1,
            v.oth_four1,
            scal=True,
        )
        v.got_rows = [to_core(some) for some in v.rows_back]

    def end_text():
        v.text_out, v.memory_out = call(
            end_text_kernel,
            text_shape,
            v.text0,
            v.got_more0,
            v.text1,
            v.got_more1,
            scal=True,
        )

    def end_grad():
        v.text_grad, v.memory_grad = call(
            end_grad_kernel,
            text_shape,
            v.rows_back[0],
            v.got_rows[0],
            v.rows_back[1],
            v.got_rows[1],
            scal=True,
        )

    def turn_out():
        v.out_keep_two, give = call(
            turn_batch_kernel, [shape(2 * chunk, units)] * 2, v.out_keep, v.got_out
        )
        v.got_out_two = swap_batch(give, 2)

    def next_out():
        v.out_keep_three, give = call(
            turn_place_kernel,
            [shape(chunk, units)] * 2,
            v.out_keep_two,
            v.got_out_two,
        )
        v.got_out_three = swap_seq(give)

    def turn_in():
        v.in_keep, give, v.bundle0, _, v.bundle_other, _ = call(
            functools.partial(turn_in_kernel, batch_count, chunk, mem_dev),
            [shape(2, chunk, units), shape(2 * chunk + 32, units)] + [shape(24, width)] * 4,
            v.in0,
            v.got_in0,
            v.in1,
            v.got_in1,
            v.bundle,
            scal=True,
        )
        v.got_in_one = swap_batch(give, 1)

    def next_in():
        v.in_keep_two, give, v.bundle1 = call(
            functools.partial(next_in_kernel, chunk, mem_dev),
            [shape(chunk, units), shape(chunk + 48, units), shape(24, width)],
            v.in_keep,
            v.got_in_one,
            v.bundle_other,
        )
        v.got_in_two = swap_batch(give, 2)

    def turn_attend0():
        v.attend_keep0, give, v.norms_one = call(
            turn_first_kernel,
            [shape(2, chunk, 2 * cols), shape(2 * chunk + folded, 2 * cols), shape(8, width)],
            v.attend_terms[0],
            v.got_attend0,
            v.sums,
            v.got_give0,
        )
        v.got_turn0 = swap_batch(give, 1)

    def turn_attend1():
        v.attend_keep1, give = call(
            turn_seq_kernel,
            [shape(2, chunk, 2 * cols)] * 2,
            v.attend_terms[2],
            v.got_attend1,
        )
        v.got_turn1 = swap_batch(give, 1)

    def next_attend0():
        v.attend_last0, give, v.norms_two = call(
            next_first_kernel,
            [shape(chunk, 2 * cols), shape(chunk + folded, 2 * cols), shape(8, width)],
            v.attend_keep0,
            v.got_turn0,
            v.norms_one,
        )
        v.got_last0 = swap_batch(give, 2)

    def next_attend1():
        v.attend_last1, give = call(
            turn_batch_kernel,
            [shape(chunk, 2 * cols)] * 2,
            v.attend_keep1,
            v.got_turn1,
        )
        v.got_last1 = swap_batch(give, 2)

    def end_in():
        v.ffn_in_grad = call(
            functools.partial(end_in_kernel, mem_dev),
            shape(chunk, units),
            v.in_keep_two,
            v.got_in_two,
            v.bundle0,
            v.bundle1,
            scratch=factors,
        )

    def end_out():
        v.ffn_out_grad = call(
            functools.partial(end_out_kernel, mem_dev),
            shape(chunk, units),
            v.out_keep_three,
            v.got_out_three,
            v.bundle0,
            v.bundle1,
            v.got_in_two,
            scratch=factors,
        )

    def end_norms():
        v.gains_grad, v.biases_grad = call(
            end_norms_kernel,
            [shape(2, chunk)] * 2,
            v.got_last0,
            v.norms_two,
            scal=True,
        )

    def end_attend():
        v.attn_in_grad, v.attn_out_grad = call(
            end_attend_kernel,
            [shape(3, chunk, cols), shape(cols, chunk)],
            v.attend_last0,
            v.got_last0,
            v.attend_last1,
            v.got_last1,
        )

    steps = (
        (start, 0.8, tuple),
        (query0, 0.2, tuple),
        (split_out, 6.0, tuple),
        (split_feed, 0.3, tuple),
        (probs0, 0.8, tuple),
        (split_feed_sib, 0.0, tuple),
        (split_out_sib, 0.0, tuple),
        (attend0, 0.5, tuple),
        (project, 0.05, tuple),
        (feed_tail, 2.5, tuple),
        (attend_out0, 0.3, tuple),
        (link_tail, 0.5, tuple),
        (attend1, 1.3, tuple),
        (attend_out1, 0.4, tuple),
        (feed0, 1.3, tuple),
        (turn_weights, 1.0, tuple),
        (make_upstream, 0.4, tuple),
        (feed1, 1.3, tuple),
        (feed_back0, 1.3, lambda: (v.got_hidden0, v.got_act0,)),
        (feed_back1, 1.3, lambda: (v.got_back0, v.got_act1,)),
        (feed_in0, 0.1, tuple),
        (context_back0, 0.36, tuple),
        (feed_out, 0.1, tuple),
        (attend_back0, 1.5, tuple),
        (context_back1, 0.36, tuple),
        (attend_back1, 1.5, lambda: (v.got_in0,)),
        (rows_tail, 0.4, lambda: (v.got_more0, v.got_more1,)),
        (feed_back_tail, 1.5, lambda: (v.got_one0,)),
        (feed_in1, 0.7, tuple),
        (attend_back_tail, 3.2, lambda: (v.got1, v.got_one0,)),
        (turn_out, 1.0, tuple),
        (turn_back1, 0.15, tuple),
        (rows1, 0.1, tuple),
        (join1, 0.08, tuple),
        (turn_back0, 0.3, tuple),
        (attend_weights, 0.2, tuple),
        (turn_in, 0.08, tuple),
        (next_out, 0.08, tuple),
        (end_text, 1.0, tuple),
        (rows0, 0.1, tuple),
        (join0, 0.08, tuple),
        (turn_attend0, 2.0, tuple),
        (next_in, 0.08, tuple),
        (turn_attend1, 2.0, tuple),
        (next_attend0, 0.08, tuple),
        (end_rows, 0.2, tuple),
        (next_attend1, 0.08, tuple),
        (end_in, 8.0, tuple),
        (end_out, 0.08, tuple),
        (end_grad, 0.8, tuple),
        (end_norms, 0.08, tuple),
        (end_attend, 0.08, tuple),
    )
    halving_only = (turn_out, turn_in, next_out, turn_attend0, next_in, turn_attend1, next_attend0, next_attend1, end_in, end_out, end_norms, end_attend)
    for step, cost, waits in steps:
        if halving or step not in halving_only:
            order.name, order.cost = step.__name__.removeprefix("make_"), cost
            if halving:
                order.wait(*jax.tree.leaves(waits()))
            step()

    if not halving:

        def scatter(values):
            return lax.psum_scatter(values, ("batch", "seq"), scatter_dimension=0, tiled=True)

        def outer(left, right):
            return jnp.einsum("rd,rf->df", left, right, precision=lax.Precision.HIGHEST)

        bundle = v.bundle
        v.ffn_out_grad = scatter(v.out_keep + outer(bundle[16:24], bundle[24:32]))
        in_terms = jnp.concatenate([v.in0, v.in1], axis=1)
        v.ffn_in_grad = scatter(in_terms + outer(bundle[0:8], bundle[8:16]))
        total = scatter(v.attend_terms[0])
        v.attn_in_grad = jnp.stack([total[:, t * cols : (t + 1) * cols] for t in range(3)])
        v.attn_out_grad = total[:, 3 * cols :].T
        norms = lax.psum(v.sums + v.got_give0[half:], "batch")
        place = (lax.axis_index("batch") * seq_count + lax.axis_index("seq")) * chunk
        norms = lax.dynamic_slice_in_dim(norms, place, chunk, 1)
        v.gains_grad, v.biases_grad = norms[0:2], norms[2:4]
    return (
        v.text_out.transpose(1, 0, 2)[None],
        v.memory_out.transpose(1, 0, 2),
        v.text_grad.transpose(1, 0, 2)[None],
        v.memory_grad.transpose(1, 0, 2),
        v.attn_in_grad,
        v.attn_out_grad,
        v.ffn_in_grad,
        v.ffn_out_grad.T,
        v.gains_grad,
        v.biases_grad,
    )


def solution(mesh):
    placed = (
        P("batch", None, "seq", None),
        P("batch", "seq", None),
        P("batch"),
        P("batch", None, "seq"),
        P("batch", None, "seq", None),
        P(None, None, "mp"),
        P("mp", None),
        P(None, "mp"),
        P("mp", None),
        P(),
        P(),
    )
    return jax.shard_map(
        local,
        mesh=mesh,
        in_specs=placed,
        out_specs=(
            P("batch", None, "seq", None),
            P("batch", "seq", None),
            P("batch", None, "seq", None),
            P("batch", "seq", None),
            P(None, ("batch", "seq"), "mp"),
            P("mp", ("batch", "seq")),
            P(("batch", "seq"), "mp"),
            P("mp", ("batch", "seq")),
            P(None, ("batch", "seq")),
            P(None, ("batch", "seq")),
        ),
        check_vma=False,
    )
```
